32 devices in a mesh: dp: 4 (over y, x), tensor: 8 (over z, core).
Axes of the slice: x: 2, y: 2, z: 4, core: 2. Of those that a mesh axis runs over, the one named last changes fastest.
Arguments:
- tokens: bfloat16 [65536, 1024], P(('dp', 'tensor')), may hold values from -6 to 6
- routes: int32 [32, 256], P(('dp', 'tensor')), may hold values from 0 to 2047, as said below
- router_weight: bfloat16 [1024], replicated, may hold values from -0.1875 to 0.1875
- attn_gain: float32 [1024], replicated, may hold values from 0.5 to 1.5
- qkv_weight: bfloat16 [3, 16, 64, 1024], P(None, 'tensor'), may hold values from -0.1875 to 0.1875
- out_weight: bfloat16 [16, 64, 1024], P('tensor'), may hold values from -1 to 1
- mlp_gain: float32 [1024], replicated, may hold values from 0.5 to 1.5
- up_weight: bfloat16 [1024, 4096], P(None, 'tensor'), may hold values from -0.1875 to 0.1875
- down_weight: bfloat16 [4096, 1024], P('tensor'), may hold values from -0.09375 to 0.09375
- cotangent: bfloat16 [65536, 1024], P(('dp', 'tensor')), may hold values from -6 to 6
Outputs:
- output: bfloat16 [65536, 1024], P(('dp', 'tensor'))
- tokens_grad: bfloat16 [65536, 1024], P(('dp', 'tensor'))
- router_grad: float32 [1024], replicated
- attn_gain_grad: float32 [1024], replicated
- qkv_grad: float32 [3, 16, 64, 1024], P(None, 'tensor')
- out_grad: float32 [16, 64, 1024], P('tensor')
- mlp_gain_grad: float32 [1024], replicated
- up_grad: float32 [1024, 4096], P(None, 'tensor')
- down_grad: float32 [4096, 1024], P('tensor')
The draws below stay inside these ranges and needn't reach their ends.
Inputs may be any that keep to these rules, and one draw needn't show every extreme that they name: `routes`: each row lists 256 different token positions of one sequence in increasing order; the first and the last position of every sequence are always listed.
All inputs are finite; a program needn't handle non-finite values.
Results may differ from the reference program's by a relative error of at most 0.019.
Values may be sent and summed in bfloat16 or wider, within the bound.
No kernel may reach another device: no remote copies, remote signals or barrier semaphores. Data moves between devices by JAX's collectives and lax.ppermute only.
A program may use at most 256 MiB of HBM per device.

```python
import jax
import jax.numpy as jnp
from jax import lax

D = 1024
H = 16
HD = 64
FF = 4096
SEQUENCE_TOKENS = 2048
K = 256
NSEQ = 32
TOKENS = 65536


def draw_routes(key, part):
    random_noise = jax.random.randint(jax.random.fold_in(key, 11), (NSEQ, SEQUENCE_TOKENS), 0, 4096)
    grouped_positions = jax.random.randint(jax.random.fold_in(key, 12), (NSEQ, 1), 0, 2)
    token_place = jnp.arange(SEQUENCE_TOKENS, dtype=jnp.int32)[None, :]
    early_reward = grouped_positions * (SEQUENCE_TOKENS - token_place) * 8
    final_reward = jnp.where((token_place == 0) | (token_place == SEQUENCE_TOKENS - 1), 1 << 17, 0)
    rank_order = (random_noise + early_reward + final_reward) * SEQUENCE_TOKENS + (SEQUENCE_TOKENS - 1 - token_place)
    ranked_values, picked = lax.top_k(rank_order, K)
    return jnp.sort(picked, axis=1).astype(jnp.int32)


def shard_levels(rng, dims, shards, smallest, high):
    factor_of, own = 1.0, jax.random.fold_in(rng, 6)
    for dim, shards_of in shards:
        draws = jnp.exp(jax.random.uniform(jax.random.fold_in(own, dim), (shards_of,), jnp.float32, smallest / len(shards), high / len(shards)))
        factor_of = factor_of * jnp.repeat(draws, dims[dim] // shards_of).reshape([-1 if axis == dim else 1 for axis in range(len(dims))])
    return factor_of


def scatter_about(stream_key, dims, deviation, limit, split=(), kind=jnp.bfloat16):
    drawn = deviation * jax.random.normal(stream_key, dims, jnp.float32)
    if split:
        drawn = drawn * shard_levels(stream_key, dims, split, -0.22, 0.18)
    return jnp.clip(drawn, -limit, limit).astype(kind)


def setup_inputs(seed: int = 0) -> dict:
    splits = jax.random.split(jax.random.key(seed), 11)
    return {
        "tokens": scatter_about(splits[0], (TOKENS, D), 1.0, 6.0, ((0, 32),)),
        "routes": draw_routes(jax.random.fold_in(splits[10], 71), 0),
        "router_weight": scatter_about(splits[2], (D,), D ** -0.5, 0.1875),
        "attn_gain": jnp.clip(1.0 + 0.1 * jax.random.normal(splits[3], (D,), jnp.float32), 0.5, 1.5),
        "qkv_weight": scatter_about(splits[4], (3, H, HD, D), D ** -0.5, 0.1875, ((1, 8),)),
        "out_weight": scatter_about(splits[5], (H, HD, D), (H * HD // 32) ** -0.5, 1.0, ((0, 8),)),
        "mlp_gain": jnp.clip(1.0 + 0.1 * jax.random.normal(splits[6], (D,), jnp.float32), 0.5, 1.5),
        "up_weight": scatter_about(splits[7], (D, FF), D ** -0.5, 0.1875, ((1, 8),)),
        "down_weight": scatter_about(splits[8], (FF, D), FF ** -0.5, 0.09375, ((0, 8),)),
        "cotangent": scatter_about(splits[9], (TOKENS, D), 1.0, 6.0, ((0, 32),)),
    }


epsilon = 1e-05
highest = lax.Precision.HIGHEST

@jax.custom_vjp
def low(v):
    return lax.optimization_barrier(v.astype(jnp.bfloat16)).astype(jnp.float32)

@jax.custom_vjp
def low_back(v):
    return v

def low_keep(v):
    return (low(v), None)

def low_pass(kept, grad):
    return (grad,)

def back_keep(v):
    return (v, None)

def back_low(kept, grad):
    return (low(grad),)
low.defvjp(low_keep, low_pass)
low_back.defvjp(back_keep, back_low)

def rms_scaled(values, gain):
    return values * lax.rsqrt(lax.optimization_barrier(jnp.mean(values * values, axis=-1, keepdims=True)) + epsilon) * gain

def branch(block, params):
    router_w, attn_gain, qkv_w, out_w, mlp_gain, up_w, down_w = params
    score = jnp.einsum('skd,d->sk', block, router_w, precision=highest)
    normed = low(rms_scaled(block, attn_gain))
    projected = low_back(low(jnp.einsum('skd,ched->chske', normed, qkv_w, precision=highest)))
    query_heads = projected[0]
    key_heads = projected[1]
    value_heads = projected[2]
    logits = low_back(jnp.einsum('hsqe,hske->hsqk', query_heads, key_heads, precision=highest) * HD ** (-0.5))
    positions = jnp.arange(K)
    allowed = positions[:, None] >= positions[None, :]
    logits = jnp.where(allowed, logits, -1e+30)
    shifted = logits - lax.optimization_barrier(jnp.max(logits, axis=-1, keepdims=True))
    exponent = jnp.exp(shifted)
    softmaxed = low(exponent / lax.optimization_barrier(jnp.sum(exponent, axis=-1, keepdims=True)))
    attended = low_back(low(jnp.einsum('hsqk,hske->hsqe', softmaxed, value_heads, precision=highest)))
    attn_sum = low_back(jnp.einsum('hsqe,hed->sqd', attended, out_w, precision=highest))
    mixed = block + attn_sum
    normed_mid = low(rms_scaled(mixed, mlp_gain))
    pre_act = low_back(jnp.einsum('skd,df->skf', normed_mid, up_w, precision=highest))
    hidden = low(jax.nn.gelu(pre_act, approximate=True))
    mlp_sum = low_back(jnp.einsum('skf,fd->skd', hidden, down_w, precision=highest))
    return score[:, :, None] * (attn_sum + mlp_sum)

def forward(rows_x, params):
    pairs = rows_x.reshape(NSEQ // 2, 2, K, D)

    def one_pair(block):
        return branch(block, params)
    return lax.map(jax.checkpoint(one_pair), pairs).reshape(NSEQ, K, D)

def reference(tokens, routes, router_weight, attn_gain, qkv_weight, out_weight, mlp_gain, up_weight, down_weight, cotangent):
    picker = (jnp.arange(NSEQ)[:, None], routes)
    token_seqs = tokens.reshape(NSEQ, SEQUENCE_TOKENS, D)
    grad_seqs = cotangent.reshape(NSEQ, SEQUENCE_TOKENS, D)
    rows_x = token_seqs[picker].astype(jnp.float32)
    grad_rows = grad_seqs[picker].astype(jnp.float32)
    params = (router_weight.astype(jnp.float32), attn_gain, qkv_weight.astype(jnp.float32), out_weight.astype(jnp.float32), mlp_gain, up_weight.astype(jnp.float32), down_weight.astype(jnp.float32))
    delta, backward = jax.vjp(forward, rows_x, params)
    rows_back, grads = backward(grad_rows)
    output = token_seqs.at[picker].set((rows_x + delta).astype(jnp.bfloat16)).reshape(NSEQ * SEQUENCE_TOKENS, D)
    tokens_grad = grad_seqs.at[picker].set((grad_rows + rows_back).astype(jnp.bfloat16)).reshape(NSEQ * SEQUENCE_TOKENS, D)
    return (output, tokens_grad, grads[0], grads[1], grads[2], grads[3], grads[4], grads[5], grads[6])
```

```python
import jax
import jax.numpy as jnp
from jax import lax
from jax.sharding import PartitionSpec as P

epsilon = 1e-05
f32 = jnp.float32
low = jnp.bfloat16


def inverse_rms(values):
    return lax.rsqrt(jnp.mean(values * values, axis=1, keepdims=True) + epsilon)


def norm_back(values, inverse, gain, upstream):
    unit_rows = values * inverse
    scaled = upstream * gain
    return inverse * (scaled - unit_rows * jnp.mean(scaled * unit_rows, axis=1, keepdims=True))


def dot(a, b, contract):
    return lax.dot_general(a, b, (contract, ((), ())), preferred_element_type=f32)


def make_local(dp_size, tensor_size):
    dp_bits = [1 << k for k in range(dp_size.bit_length() - 1)]
    far_bits = [1 << k for k in range(2, tensor_size.bit_length() - 1)]

    def swap(x, axis, bit):
        size = dp_size if axis == "dp" else tensor_size
        return lax.ppermute(x, axis, [(i, i ^ bit) for i in range(size)])

    def gather_rows(x):
        near = swap(x, "tensor", 2)
        core = swap(x, "tensor", 1)
        both = swap(near, "tensor", 1)
        return jnp.concatenate([x, near, core, both], axis=0)

    def scatter_rows(keep, send):
        rows = keep.shape[0] // 2
        near = keep[rows:] + swap(send[rows:], "tensor", 1).astype(f32)
        own = keep[:rows] + swap(send[:rows], "tensor", 1).astype(f32)
        return own + swap(near.astype(low), "tensor", 2).astype(f32)

    def product_scatter(left, weight, contract):
        half = left.shape[0] // 2
        send = dot(left[half:], weight, contract).astype(low)
        keep = dot(left[:half], weight, contract)
        return scatter_rows(keep, send)

    def spread(own, axis, order):
        me = lax.axis_index("dp")
        size = own.shape[axis] // dp_size
        mine = [
            lax.dynamic_slice_in_dim(own, (me ^ r) * size, size, axis) for r in range(dp_size)
        ]
        shards = [mine[0]]
        for bit in far_bits:
            shards = shards + [swap(s, "tensor", bit) for s in shards]
        found = [mine]
        for shard in shards[1:]:
            pieces = {0: shard}
            for bit in order:
                pieces.update({r ^ bit: swap(p, "dp", bit) for r, p in pieces.items()})
            found.append([pieces[r] for r in range(dp_size)])
        return found

    def collect(grad, order):
        me = lax.axis_index("dp")
        held = {r: grad[:, r] for r in range(dp_size)}
        for bit in order:
            sent = [r for r in held if r & bit]
            came = swap(jnp.stack([held[r] for r in sent]), "dp", bit)
            held = {
                r ^ bit: (held[r ^ bit].astype(f32) + came[k].astype(f32)).astype(low)
                for k, r in enumerate(sent)
            }
        total = held[0]
        for bit in reversed(far_bits):
            half = total.shape[0] // 2
            came = swap(total[half:], "tensor", bit)
            total = (total[:half].astype(f32) + came.astype(f32)).astype(low)
        pieces = {0: total[0]}
        for bit in reversed(order):
            pieces.update({r ^ bit: swap(p, "dp", bit) for r, p in pieces.items()})
        stacked = jnp.stack([pieces[r] for r in range(dp_size)])
        return jnp.concatenate(
            [lax.dynamic_slice_in_dim(stacked, me ^ a, 1, 0) for a in range(dp_size)], axis=0
        ).astype(f32)

    def local(
        tokens,
        routes,
        router_weight,
        attn_gain,
        qkv_weight,
        out_weight,
        mlp_gain,
        up_weight,
        down_weight,
        cotangent,
    ):
        seq_count, routed = routes.shape
        width = tokens.shape[1]
        length = tokens.shape[0] // seq_count
        own_rows = seq_count * routed
        heads, head_size = qkv_weight.shape[1:3]
        hidden_own = up_weight.shape[1]

        places = (routes + jnp.arange(seq_count, dtype=jnp.int32)[:, None] * length).reshape(own_rows)
        token_ids = jnp.arange(tokens.shape[0], dtype=jnp.int32)
        chosen = (places[:, None] == token_ids[None, :]).astype(low)
        rows = dot(chosen, tokens, ((1,), (0,)))
        grad_rows = dot(chosen, cotangent, ((1,), (0,)))

        first, second = dp_bits, dp_bits[::-1]
        qkv_all = jnp.concatenate(
            [p for s in spread(qkv_weight.reshape(3, heads, head_size, width), 2, first) for p in [jnp.concatenate(s, axis=2)]],
            axis=1,
        )
        out_all = jnp.concatenate([jnp.concatenate(s, axis=1) for s in spread(out_weight, 1, second)], axis=0)
        up_all = jnp.concatenate([p for s in spread(up_weight, 1, first) for p in s], axis=1)
        down_all = jnp.concatenate([p for s in spread(down_weight, 0, second) for p in s], axis=0)
        all_heads = qkv_all.shape[1]
        shard_count = all_heads // heads
        qkv_flat = qkv_all.reshape(3 * all_heads * head_size, width)
        out_flat = out_all.reshape(all_heads * head_size, width)

        score = jnp.sum(rows * router_weight.astype(f32), axis=1, keepdims=True)
        inverse_in = inverse_rms(rows)
        normed_in = gather_rows((rows * inverse_in * attn_gain).astype(low))
        branch_term = grad_rows * score
        branch = gather_rows(branch_term.astype(low))

        group_rows = normed_in.shape[0]
        group_seqs = group_rows // routed
        projected = dot(qkv_flat, normed_in, ((1,), (1,))).astype(low)
        projected = projected.reshape(3, all_heads, head_size, group_seqs, routed)
        query, key, value = projected[0], projected[1], projected[2]
        scaling = head_size**-0.5
        order = jnp.arange(routed)
        logits = jnp.einsum("heni,henj->hnij", query, key, preferred_element_type=f32) * scaling
        logits = jnp.where(order[:, None] >= order[None, :], logits, -1e30)
        highest = jnp.max(logits, axis=3, keepdims=True)
        exponent = jnp.exp(logits - highest)
        softmaxed = exponent / jnp.sum(exponent, axis=3, keepdims=True)
        probs_low = softmaxed.astype(low)
        attended = jnp.einsum("hnij,henj->heni", probs_low, value, preferred_element_type=f32)
        attended = attended.astype(low).reshape(all_heads * head_size, group_rows)
        attended_rows = attended.T
        attn_sum = product_scatter(attended_rows, out_flat, ((1,), (0,)))
        mixed = rows + attn_sum
        inverse_mid = inverse_rms(mixed)
        normed_mid = gather_rows((mixed * inverse_mid * mlp_gain).astype(low))

        pre_act = dot(normed_mid, up_all, ((1,), (0,)))
        inner = jnp.sqrt(2 / jnp.pi).astype(f32) * (pre_act + 0.044715 * pre_act**3)
        tanh = jnp.tanh(inner)
        hidden = (0.5 * pre_act * (1 + tanh)).astype(low)
        slope = 0.5 * (1 + tanh) + 0.5 * pre_act * (1 - tanh * tanh) * jnp.sqrt(2 / jnp.pi).astype(f32) * (
            1 + 3 * 0.044715 * pre_act * pre_act
        )
        hidden_grad = dot(branch, down_all, ((1,), (1,)))
        pre_grad = (hidden_grad * slope).astype(low)
        mid_grad = product_scatter(pre_grad, up_all, ((1,), (1,)))
        mlp_sum = product_scatter(hidden, down_all, ((1,), (0,)))
        down_grad = dot(hidden, branch, ((0,), (0,)))
        up_grad = dot(pre_grad, normed_mid, ((0,), (0,)))
        mlp_gain_part = jnp.sum(up_all.astype(f32).T * up_grad, axis=0) / mlp_gain

        mixed_grad = norm_back(mixed, inverse_mid, mlp_gain, mid_grad)
        attn_grad = gather_rows((branch_term + mixed_grad).astype(low))
        attended_grad = dot(out_flat, attn_grad, ((1,), (1,))).astype(low)
        out_grad = dot(attended, attn_grad, ((1,), (0,)))
        attended_grad = attended_grad.reshape(all_heads, head_size, group_seqs, routed)
        value_grad = jnp.einsum("hnij,heni->henj", probs_low, attended_grad, preferred_element_type=f32)
        prob_grad = jnp.einsum("heni,henj->hnij", attended_grad, value, preferred_element_type=f32)
        logit_grad = (
            softmaxed * (prob_grad - jnp.sum(softmaxed * prob_grad, axis=3, keepdims=True))
        ).astype(low)
        query_grad = jnp.einsum("hnij,henj->heni", logit_grad, key, preferred_element_type=f32) * scaling
        key_grad = jnp.einsum("hnij,heni->henj", logit_grad, query, preferred_element_type=f32) * scaling
        proj_grad = jnp.stack([query_grad, key_grad, value_grad]).astype(low)
        proj_grad = proj_grad.reshape(3 * all_heads * head_size, group_rows)
        qkv_grad = dot(proj_grad, normed_in, ((1,), (0,)))
        normed_grad = product_scatter(proj_grad.T, qkv_flat, ((1,), (0,)))
        attn_gain_part = jnp.sum(qkv_flat.astype(f32) * qkv_grad, axis=0) / attn_gain

        branch_sum = attn_sum + mlp_sum
        score_grad = jnp.sum(grad_rows * branch_sum, axis=1, keepdims=True)
        router_part = jnp.sum(score_grad * rows, axis=0)
        rows_back = norm_back(rows, inverse_in, attn_gain, normed_grad)
        rows_total = grad_rows + mixed_grad + rows_back + score_grad * router_weight.astype(f32)

        listed = jnp.any(chosen > 0, axis=0)[:, None]
        output = jnp.where(
            listed, dot(chosen, (rows + score * branch_sum).astype(low), ((0,), (0,))).astype(low), tokens
        )
        tokens_grad = jnp.where(
            listed, dot(chosen, rows_total.astype(low), ((0,), (0,))).astype(low), cotangent
        )

        small = jnp.stack([router_part, attn_gain_part, mlp_gain_part])
        for axis, bits in (("dp", dp_bits), ("tensor", [1, 2] + far_bits)):
            for bit in bits:
                small = small + swap(small, axis, bit)

        piece = head_size // dp_size
        cut = qkv_grad.astype(low).reshape(3, shard_count, heads, dp_size, piece, width)
        qkv_out = collect(cut.transpose(1, 3, 0, 2, 4, 5), first)
        qkv_out = qkv_out.transpose(1, 2, 0, 3, 4).reshape(qkv_weight.shape)
        cut = out_grad.astype(low).reshape(shard_count, heads, dp_size, piece, width)
        out_out = collect(cut.transpose(0, 2, 1, 3, 4), second)
        out_out = out_out.transpose(1, 0, 2, 3).reshape(out_weight.shape)
        piece = hidden_own // dp_size
        up_out = collect(up_grad.astype(low).reshape(shard_count, dp_size, piece, width), first)
        up_out = up_out.reshape(hidden_own, width).T
        down_out = collect(down_grad.astype(low).reshape(shard_count, dp_size, piece, width), second)
        down_out = down_out.reshape(hidden_own, width)
        return (
            output,
            tokens_grad,
            small[0],
            small[1],
            qkv_out,
            out_out,
            small[2],
            up_out,
            down_out,
        )

    return local


def solution(mesh):
    rows = P(("dp", "tensor"), None)
    heads = P("tensor", None, None)
    return jax.shard_map(
        make_local(mesh.shape["dp"], mesh.shape["tensor"]),
        mesh=mesh,
        in_specs=(
            rows,
            rows,
            P(),
            P(),
            P(None, "tensor", None, None),
            heads,
            P(),
            P(None, "tensor"),
            P("tensor", None),
            rows,
        ),
        out_specs=(
            rows,
            rows,
            P(),
            P(),
            P(None, "tensor", None, None),
            heads,
            P(),
            P(None, "tensor"),
            P("tensor", None),
        ),
        check_vma=False,
    )
```

```python
from functools import partial

import jax
import jax.numpy as jnp
from jax import lax
from jax.experimental import pallas as pl
from jax.experimental.pallas import tpu as pltpu
from jax.sharding import PartitionSpec as P

epsilon = 1e-05
f32 = jnp.float32
low = jnp.bfloat16
MIB = 1 << 20
gelu_scale = 0.7978845608028654
whole = pl.BlockSpec(memory_space=pltpu.VMEM)
anywhere = pl.BlockSpec(memory_space=pl.ANY)
scalar = pl.BlockSpec(memory_space=pltpu.SMEM)


def nn(a, b):
    return lax.dot_general(a, b, (((1,), (0,)), ((), ())), preferred_element_type=f32)


def nt(a, b):
    return lax.dot_general(a, b, (((1,), (1,)), ((), ())), preferred_element_type=f32)


def tn(a, b):
    return lax.dot_general(a, b, (((0,), (0,)), ((), ())), preferred_element_type=f32)


def inverse_rms(values):
    return lax.rsqrt(jnp.mean(values * values, axis=1, keepdims=True) + epsilon)


def norm_back(values, inverse, gain, upstream):
    unit_rows = values * inverse
    scaled = upstream * gain
    return inverse * (scaled - unit_rows * jnp.mean(scaled * unit_rows, axis=1, keepdims=True))


def score_of(rows, router):
    return jnp.sum(rows * router, axis=1, keepdims=True)


def struct(shape, kind):
    return jax.ShapeDtypeStruct(shape, kind)


def call(body, outs, in_specs, out_specs=None, scratch=(), grid=None, vmem=40, cost=None, **more):
    return pl.pallas_call(
        body,
        out_shape=outs,
        in_specs=in_specs,
        out_specs=[whole] * len(outs) if out_specs is None else out_specs,
        scratch_shapes=list(scratch),
        grid=() if grid is None else grid,
        compiler_params=pltpu.CompilerParams(vmem_limit_bytes=vmem * MIB),
        cost_estimate=None
        if cost is None
        else pl.CostEstimate(flops=int(cost[0]), bytes_accessed=int(cost[1]), transcendentals=0),
        **more,
    )


def picked(places_ref, block_ref, total_ref):
    count = places_ref.shape[1]
    step = pl.program_id(0)
    size = block_ref.shape[0]
    column = jnp.transpose(jnp.broadcast_to(places_ref[...], (128, count)))
    column = jnp.concatenate([column] * (size // 128), axis=1)
    ids = lax.broadcasted_iota(jnp.int32, (count, size), 1) + step * size
    part = nn(jnp.where(column == ids, 1.0, 0.0).astype(low), block_ref[...])

    @pl.when(step == 0)
    def _():
        total_ref[...] = part

    @pl.when(step > 0)
    def _():
        total_ref[...] += part


def pick_tokens(places_ref, gain_ref, tokens_ref, rows_ref, normed_ref, total_ref):
    picked(places_ref, tokens_ref, total_ref)

    @pl.when(pl.program_id(0) == pl.num_programs(0) - 1)
    def _():
        rows = total_ref[...]
        rows_ref[...] = rows.astype(low)
        normed_ref[...] = (rows * inverse_rms(rows) * gain_ref[...]).astype(low)


def pick_grads(places_ref, router_ref, rows_ref, grads_ref, grad_rows_ref, branch_ref, total_ref):
    picked(places_ref, grads_ref, total_ref)

    @pl.when(pl.program_id(0) == pl.num_programs(0) - 1)
    def _():
        grads = total_ref[...]
        score = score_of(rows_ref[...].astype(f32), router_ref[...].astype(f32))
        grad_rows_ref[...] = grads.astype(low)
        branch_ref[...] = (grads * score).astype(low)


def put_back(places_ref, rows_ref, block_ref, out_ref):
    count = places_ref.shape[1]
    size = block_ref.shape[0]
    ids = lax.broadcasted_iota(jnp.int32, (size, count), 0) + pl.program_id(0) * size
    chosen = jnp.where(ids == places_ref[...], 1.0, 0.0)
    listed = jnp.sum(chosen, axis=1, keepdims=True) > 0
    placed = nn(chosen.astype(low), rows_ref[...])
    out_ref[...] = jnp.where(listed, placed, block_ref[...].astype(f32)).astype(low)


def put_output(places_ref, router_ref, rows_ref, attn_ref, keep_ref, core_ref, near_ref, block_ref, out_ref, sum_ref, new_ref):
    @pl.when(pl.program_id(0) == 0)
    def _():
        rows = rows_ref[...].astype(f32)
        mlp = keep_ref[...] + core_ref[: keep_ref.shape[0]].astype(f32) + near_ref[...].astype(f32)
        branch_sum = attn_ref[...] + mlp
        sum_ref[...] = branch_sum
        new_ref[...] = (rows + score_of(rows, router_ref[...].astype(f32)) * branch_sum).astype(low)

    put_back(places_ref, new_ref, block_ref, out_ref)


def put_grads(
    places_ref, router_ref, gain_ref, rows_ref, grads_ref, sum_ref, mixed_ref, keep_ref, core_ref, near_ref, block_ref,
    out_ref, new_ref,
):
    @pl.when(pl.program_id(0) == 0)
    def _():
        rows = rows_ref[...].astype(f32)
        grads = grads_ref[...].astype(f32)
        normed_grad = keep_ref[...] + core_ref[: keep_ref.shape[0]].astype(f32) + near_ref[...].astype(f32)
        rows_back = norm_back(rows, inverse_rms(rows), gain_ref[...], normed_grad)
        score_grad = jnp.sum(grads * sum_ref[...], axis=1, keepdims=True)
        total = grads + mixed_ref[...] + rows_back + score_grad * router_ref[...].astype(f32)
        new_ref[...] = total.astype(low)

    put_back(places_ref, new_ref, block_ref, out_ref)


def middle(gain_ref, rows_ref, keep_ref, core_ref, near_ref, attn_ref, normed_ref):
    attn = keep_ref[...] + core_ref[: keep_ref.shape[0]].astype(f32) + near_ref[...].astype(f32)
    attn_ref[...] = attn
    mixed = rows_ref[...].astype(f32) + attn
    normed_ref[...] = (mixed * inverse_rms(mixed) * gain_ref[...]).astype(low)


def middle_back(
    gain_ref, router_ref, rows_ref, grads_ref, attn_ref, keep_ref, core_ref, near_ref, mixed_grad_ref, attn_grad_ref
):
    rows = rows_ref[...].astype(f32)
    mixed = rows + attn_ref[...]
    mid = keep_ref[...] + core_ref[: keep_ref.shape[0]].astype(f32) + near_ref[...].astype(f32)
    mixed_grad = norm_back(mixed, inverse_rms(mixed), gain_ref[...], mid)
    mixed_grad_ref[...] = mixed_grad
    branch = grads_ref[...].astype(f32) * score_of(rows, router_ref[...].astype(f32))
    attn_grad_ref[...] = (branch + mixed_grad).astype(low)


def router_product(rows_ref, grads_ref, sum_ref, out_ref):
    score_grad = jnp.sum(grads_ref[...].astype(f32) * sum_ref[...], axis=1, keepdims=True)
    out_ref[...] = jnp.sum(score_grad * rows_ref[...].astype(f32), axis=0, keepdims=True)


def fill_attn(me_ref, qkv_ref, out_ref, far_refs, dp_size, held_ref, sems):
    _, heads, head_size, _ = qkv_ref.shape
    rows = heads * head_size
    piece = 4 * rows // dp_size
    copies = []
    for h in range(heads):
        for c in range(3):
            copies.append((qkv_ref.at[c, h], held_ref.at[c, pl.ds(h * head_size, head_size)]))
        copies.append((out_ref.at[h], held_ref.at[3, pl.ds(h * head_size, head_size)]))
    for k, far_ref in enumerate(far_refs):
        shard, r = 1 + k // dp_size, k % dp_size
        start = lax.bitwise_xor(me_ref[0], r) * piece
        part = min(piece, rows)
        for p in range(piece // part):
            place = start + p * part
            inside = pl.multiple_of(lax.rem(place, rows), part)
            copies.append(
                (
                    far_ref.at[pl.ds(p * part, part)],
                    held_ref.at[lax.div(place, rows), pl.ds(shard * rows + inside, part)],
                )
            )
    started = [pltpu.make_async_copy(a, b, sems.at[i]) for i, (a, b) in enumerate(copies)]
    for c in started:
        c.start()
    return started


def attn_copies(heads, far_count, dp_size):
    return heads * 4 + far_count * max(1, 4 // dp_size)


def attn_forward(dp_size, far_count, head_size, *refs):
    me_ref, qkv_ref, out_ref = refs[:3]
    far_refs = refs[3 : 3 + far_count]
    rows_refs = refs[3 + far_count : 7 + far_count]
    proj_ref, att_ref, log_ref, keep_own, keep_near, send_ref, held_ref, sems = refs[7 + far_count :]
    started = fill_attn(me_ref, qkv_ref, out_ref, far_refs, dp_size, held_ref, sems)
    for c in started:
        c.wait()
    size, width = held_ref.shape[1:]
    count = rows_refs[0].shape[0]
    allowed = lax.broadcasted_iota(jnp.int32, (count, count), 0) <= lax.broadcasted_iota(jnp.int32, (count, count), 1)
    for s in (3, 2, 1, 0):
        proj = nt(held_ref[0:3].reshape(3 * size, width), rows_refs[s][...]).astype(low)
        proj_ref[s] = proj
        for h in range(size // head_size):
            a = h * head_size
            q, k, v = (proj[c * size + a : c * size + a + head_size] for c in range(3))
            logits = jnp.where(allowed, tn(k, q) * head_size**-0.5, -1e30)
            highest = jnp.max(logits, axis=0, keepdims=True)
            exponent = jnp.exp(logits - highest)
            total = jnp.sum(exponent, axis=0, keepdims=True)
            probs = (exponent * (1.0 / total)).astype(low)
            log_ref[s, h : h + 1] = highest + jnp.log(total)
            att_ref[s, a : a + head_size] = nn(v, probs).astype(low)
        part = tn(att_ref[s], held_ref[3])
        if s == 0:
            keep_own[...] = part
        elif s == 1:
            keep_near[...] = part
        else:
            send_ref[(s - 2) * count : (s - 1) * count] = part.astype(low)


def attn_backward(dp_size, far_count, head_size, *refs):
    me_ref, qkv_ref, out_ref = refs[:3]
    far_refs = refs[3 : 3 + far_count]
    proj_ref, att_ref, log_ref = refs[3 + far_count : 6 + far_count]
    rows_refs = refs[6 + far_count : 10 + far_count]
    grad_refs = refs[10 + far_count : 14 + far_count]
    back_ref, gain_ref, *outs, held_ref, total_ref, cut_a, cut_b, sems, out_sems = refs[14 + far_count :]
    started = fill_attn(me_ref, qkv_ref, out_ref, far_refs, dp_size, held_ref, sems)
    for c in started:
        c.wait()
    size, width = held_ref.shape[1:]
    count = rows_refs[0].shape[0]
    allowed = lax.broadcasted_iota(jnp.int32, (count, count), 0) <= lax.broadcasted_iota(jnp.int32, (count, count), 1)
    scaling = head_size**-0.5
    for s in range(4):
        attended_grad = nt(held_ref[3], grad_refs[s][...]).astype(low)
        for h in range(size // head_size):
            a = h * head_size
            q, k, v = (proj_ref[s, c * size + a : c * size + a + head_size] for c in range(3))
            da = attended_grad[a : a + head_size]
            logits = jnp.where(allowed, tn(k, q) * scaling, -1e30)
            probs = jnp.exp(logits - log_ref[s, h : h + 1])
            prob_grad = tn(v, da)
            weighted = probs * prob_grad
            logit_grad = (weighted - probs * jnp.sum(weighted, axis=0, keepdims=True)).astype(low)
            back_ref[s, a : a + head_size] = (nn(k, logit_grad) * scaling).astype(low)
            back_ref[s, size + a : size + a + head_size] = (nt(q, logit_grad) * scaling).astype(low)
            back_ref[s, 2 * size + a : 2 * size + a + head_size] = nt(da, probs.astype(low)).astype(low)
    for c in range(4):
        total = None
        for s in range(4):
            left = att_ref[s] if c == 3 else back_ref[s, c * size : (c + 1) * size]
            right = grad_refs[s][...] if c == 3 else rows_refs[s][...]
            part = nn(left, right)
            total = part if total is None else total + part
        total_ref[c] = total.astype(low)
        if c < 3:
            share = jnp.sum(total * held_ref[c].astype(f32), axis=0, keepdims=True)
            gain_ref[...] = share if c == 0 else gain_ref[...] + share
    rows = qkv_ref.shape[1] * head_size
    piece = 4 * rows // dp_size
    part = min(piece, rows)
    half = width // 2
    for shard in range(size // rows):
        for a in range(dp_size):
            r = lax.bitwise_xor(me_ref[0], a)
            for p in range(piece // part):
                place = a * piece + p * part
                inside = shard * rows + place % rows
                cut = total_ref[place // rows, inside : inside + part]
                cut_a[position(r, dp_size, False), shard, p * part : (p + 1) * part] = cut[:, :half]
                cut_b[position(r, dp_size, True), shard, p * part : (p + 1) * part] = cut[:, half:]
    send_off((cut_a, cut_b), outs, dp_size, out_sems)


def attn_rows_back(dp_size, far_count, head_size, *refs):
    me_ref, qkv_ref, out_ref = refs[:3]
    far_refs = refs[3 : 3 + far_count]
    back_ref, keep_own, keep_near, send_ref, held_ref, sems = refs[3 + far_count :]
    started = fill_attn(me_ref, qkv_ref, out_ref, far_refs, dp_size, held_ref, sems)
    for c in started:
        c.wait()
    size, width = held_ref.shape[1:]
    count = keep_own.shape[0]
    for s in (3, 2, 1, 0):
        part = tn(back_ref[s], held_ref[0:3].reshape(3 * size, width))
        if s == 0:
            keep_own[...] = part
        elif s == 1:
            keep_near[...] = part
        else:
            send_ref[(s - 2) * count : (s - 1) * count] = part.astype(low)


def position(r, dp_size, swapped):
    if swapped:
        return r
    bits = dp_size.bit_length() - 1
    place = 0
    for k in range(bits):
        place = place + lax.shift_left(lax.bitwise_and(lax.shift_right_logical(r, k), 1), bits - 1 - k)
    return place


def send_off(cuts, outs, dp_size, sems):
    half = dp_size // 2
    copies = []
    for k, cut in enumerate(cuts):
        copies.append(pltpu.make_async_copy(cut.at[pl.ds(0, half)], outs[2 * k], sems.at[2 * k]))
        copies.append(pltpu.make_async_copy(cut.at[pl.ds(half, half)], outs[2 * k + 1], sems.at[2 * k + 1]))
    for c in copies:
        c.start()
    for c in copies:
        c.wait()


def fill_mlp(me_ref, up_ref, down_ref, far_refs, dp_size, up_held, down_held, sems):
    rows = down_ref.shape[0]
    piece = rows // dp_size
    copies = []
    if up_held is not None:
        copies.append((up_ref, up_held.at[pl.ds(0, rows)]))
    if down_held is not None:
        copies.append((down_ref, down_held.at[pl.ds(0, rows)]))
    for k, far_ref in enumerate(far_refs):
        shard, r = 1 + k // dp_size, k % dp_size
        start = pl.multiple_of(shard * rows + lax.bitwise_xor(me_ref[0], r) * piece, piece)
        if up_held is not None:
            copies.append((far_ref.at[0], up_held.at[pl.ds(start, piece)]))
        if down_held is not None:
            copies.append((far_ref.at[1], down_held.at[pl.ds(start, piece)]))
    started = [pltpu.make_async_copy(a, b, sems.at[i]) for i, (a, b) in enumerate(copies)]
    for c in started:
        c.start()
    return started


def mlp_main(dp_size, far_count, *refs):
    me_ref, up_ref, down_ref = refs[:3]
    far_refs = refs[3 : 3 + far_count]
    rows_refs = refs[3 + far_count : 7 + far_count]
    grad_refs = refs[7 + far_count : 11 + far_count]
    hidden_ref, back_ref, keep_own, keep_near, send_ref, up_held, down_held, sems = refs[11 + far_count :]
    started = fill_mlp(me_ref, up_ref, down_ref, far_refs, dp_size, up_held, down_held, sems)
    for c in started:
        c.wait()
    count = rows_refs[0].shape[0]
    step = 256
    for s in (3, 2, 1, 0):
        normed = rows_refs[s][...]
        branch = grad_refs[s][...]

        for f in range(0, up_held.shape[0], step):
            pre = nt(up_held[f : f + step], normed)
            upstream = nt(down_held[f : f + step], branch)
            square = pre * pre
            tanh = jnp.tanh(pre * (gelu_scale + gelu_scale * 0.044715 * square))
            half = 0.5 + 0.5 * tanh
            hidden_ref[s, f : f + step] = (pre * half).astype(low)
            slope = half + (pre * (0.5 - 0.5 * tanh * tanh)) * (gelu_scale + 3 * gelu_scale * 0.044715 * square)
            back_ref[s, f : f + step] = (upstream * slope).astype(low)

        part = tn(back_ref[s], up_held[...])
        if s == 0:
            keep_own[...] = part
        elif s == 1:
            keep_near[...] = part
        else:
            send_ref[(s - 2) * count : (s - 1) * count] = part.astype(low)


def mlp_out(dp_size, far_count, *refs):
    me_ref, up_ref, down_ref = refs[:3]
    far_refs = refs[3 : 3 + far_count]
    hidden_ref, keep_own, keep_near, send_ref, down_held, sems = refs[3 + far_count :]
    started = fill_mlp(me_ref, up_ref, down_ref, far_refs, dp_size, None, down_held, sems)
    for c in started:
        c.wait()
    count = keep_own.shape[0]
    for s in (3, 2, 1, 0):
        part = tn(hidden_ref[s], down_held[...])
        if s == 0:
            keep_own[...] = part
        elif s == 1:
            keep_near[...] = part
        else:
            send_ref[(s - 2) * count : (s - 1) * count] = part.astype(low)


def mlp_weights(dp_size, far_count, *refs):
    me_ref, up_ref, down_ref = refs[:3]
    far_refs = refs[3 : 3 + far_count]
    hidden_ref, back_ref = refs[3 + far_count : 5 + far_count]
    rows_refs = refs[5 + far_count : 9 + far_count]
    grad_refs = refs[9 + far_count : 13 + far_count]
    gain_ref, *outs, up_held, cut_a, cut_b, sems, out_sems = refs[13 + far_count :]
    started = fill_mlp(me_ref, up_ref, down_ref, far_refs, dp_size, up_held, None, sems)
    for c in started:
        c.wait()
    rows = down_ref.shape[0]
    piece = rows // dp_size
    for f in range(0, up_held.shape[0], rows):
        for a in range(dp_size):
            r = lax.bitwise_xor(me_ref[0], a)
            b = f + a * piece
            down_total, up_total = None, None
            for s in range(4):
                part = nn(hidden_ref[s, b : b + piece], grad_refs[s][...])
                down_total = part if down_total is None else down_total + part
                part = nn(back_ref[s, b : b + piece], rows_refs[s][...])
                up_total = part if up_total is None else up_total + part
            cut_a[position(r, dp_size, False), f // rows] = down_total.astype(low)
            cut_b[position(r, dp_size, True), f // rows] = up_total.astype(low)
            share = jnp.sum(up_total * up_held[b : b + piece].astype(f32), axis=0, keepdims=True)
            gain_ref[...] = share if b == 0 else gain_ref[...] + share
    send_off((cut_a, cut_b), outs, dp_size, out_sems)


def make_local(dp_size, tensor_size):
    dp_bits = [1 << k for k in range(dp_size.bit_length() - 1)]
    far_bits = [1 << k for k in range(2, tensor_size.bit_length() - 1)]
    shards = tensor_size // 4
    far_count = (shards - 1) * dp_size

    def swap(x, axis, bit):
        size = dp_size if axis == "dp" else tensor_size
        return lax.ppermute(x, axis, [(i, i ^ bit) for i in range(size)])

    def gather_rows(x):
        near = swap(x, "tensor", 2)
        core = swap(x, "tensor", 1)
        return [x, near, core, swap(near, "tensor", 1)]

    def scatter_rows(keep_near, send):
        rows = keep_near.shape[0]
        core = swap(send, "tensor", 1)
        near = (keep_near + core[rows:].astype(f32)).astype(low)
        return core, swap(near, "tensor", 2)

    def spread(piece):
        found = [piece]
        for bit in far_bits:
            found = found + [swap(p, "tensor", bit) for p in found]
        return [p if r == 0 else swap(p, "dp", r) for p in found[1:] for r in range(dp_size)]

    def collect(keep, send, order):
        me = lax.axis_index("dp")
        for k, bit in enumerate(order):
            came = swap(send, "dp", bit)
            half = keep.shape[0] // 2
            if half:
                send = (keep[half:].astype(f32) + came[half:].astype(f32)).astype(low)
                keep = (keep[:half].astype(f32) + came[:half].astype(f32)).astype(low)
            else:
                keep, came = keep[0], came[0]
        total = keep.astype(f32) + came.astype(f32)
        for bit in reversed(far_bits):
            half = total.shape[0] // 2
            total = total[:half] + swap(total[half:].astype(low), "tensor", bit).astype(f32)
        piece = total[0].astype(low)
        stacked = jnp.stack([piece if r == 0 else swap(piece, "dp", r) for r in range(dp_size)])
        return jnp.concatenate(
            [lax.dynamic_slice_in_dim(stacked, me ^ a, 1, 0) for a in range(dp_size)], axis=0
        )

    def local(
        tokens,
        routes,
        router_weight,
        attn_gain,
        qkv_weight,
        out_weight,
        mlp_gain,
        up_weight,
        down_weight,
        cotangent,
    ):
        seq_count, routed = routes.shape
        token_count, width = tokens.shape
        length = token_count // seq_count
        own = seq_count * routed
        heads, head_size = qkv_weight.shape[1:3]
        hidden_own = up_weight.shape[1]
        shard_rows = heads * head_size
        size = shards * shard_rows
        hidden = shards * hidden_own
        me = lax.axis_index("dp").astype(jnp.int32)[None]
        router = router_weight[None, :]
        attn_gain_row = attn_gain[None, :]
        mlp_gain_row = mlp_gain[None, :]
        places = (routes + jnp.arange(seq_count, dtype=jnp.int32)[:, None] * length).reshape(1, own)

        rows_f = struct((own, width), f32)
        rows_l = struct((own, width), low)
        block = 256
        grid = (token_count // block,)
        blocks = pl.BlockSpec((block, width), lambda i: (i, 0))

        def flat(shape):
            return pl.BlockSpec(shape, lambda i: (0,) * len(shape))

        row_block = flat((own, width))
        line = flat((1, width))
        place_block = flat((1, own))
        pair_block = flat((2 * own, width))

        attn_own = jnp.concatenate(
            [qkv_weight.reshape(3 * shard_rows, width), out_weight.reshape(shard_rows, width)]
        )
        attn_piece = 4 * shard_rows // dp_size
        attn_far = spread(lax.dynamic_slice_in_dim(attn_own, me[0] * attn_piece, attn_piece, 0))
        up_turned = up_weight.T
        mlp_piece = hidden_own // dp_size
        mlp_far = spread(
            jnp.stack(
                [
                    lax.dynamic_slice_in_dim(up_turned, me[0] * mlp_piece, mlp_piece, 0),
                    lax.dynamic_slice_in_dim(down_weight, me[0] * mlp_piece, mlp_piece, 0),
                ]
            )
        )

        rows, normed_own = call(
            pick_tokens,
            [rows_l, rows_l],
            [place_block, line, blocks],
            [row_block, row_block],
            [pltpu.VMEM((own, width), f32)],
            grid,
        )(places, attn_gain_row, tokens)
        normed_in = gather_rows(normed_own)
        grad_rows, branch_own = call(
            pick_grads,
            [rows_l, rows_l],
            [place_block, line, row_block, blocks],
            [row_block, row_block],
            [pltpu.VMEM((own, width), f32)],
            grid,
        )(places, router, rows, cotangent)
        branch = gather_rows(branch_own)

        attn_sems = pltpu.SemaphoreType.DMA((attn_copies(heads, far_count, dp_size),))
        attn_held = pltpu.VMEM((4, size, width), low)
        attn_weights = [me, qkv_weight, out_weight, *attn_far]
        attn_specs = [scalar] + [anywhere] * (2 + far_count)
        partial_sums = [rows_f, rows_f, struct((2 * own, width), low)]
        head_count = size // head_size
        proj, attended, log_total, keep, keep_near, send = call(
            partial(attn_forward, dp_size, far_count, head_size),
            [struct((4, 3 * size, own), low), struct((4, size, own), low), struct((4, head_count, own), f32)] + partial_sums,
            attn_specs + [whole] * 4,
            scratch=[attn_held, attn_sems],
            cost=(2 * 4 * own * width * 4 * size, 12 * MIB),
        )(*attn_weights, *normed_in)
        core, near = scatter_rows(keep_near, send)
        attn_sum, normed_own = call(middle, [rows_f, rows_l], [whole] * 5)(mlp_gain_row, rows, keep, core, near)
        normed_mid = gather_rows(normed_own)

        mlp_sems = pltpu.SemaphoreType.DMA((2 + 2 * far_count,))
        mlp_held = pltpu.VMEM((hidden, width), low)
        mlp_weights_in = [me, up_turned, down_weight, *mlp_far]
        mlp_specs = [scalar] + [anywhere] * (2 + far_count)
        hidden_rows, pre_grad, keep, keep_near, send = call(
            partial(mlp_main, dp_size, far_count),
            [struct((4, hidden, own), low)] * 2 + partial_sums,
            mlp_specs + [whole] * 8,
            scratch=[mlp_held, mlp_held, mlp_sems],
            cost=(3 * 2 * 4 * own * width * hidden, 16 * MIB),
        )(*mlp_weights_in, *normed_mid, *branch)
        mid_core, mid_near = scatter_rows(keep_near, send)
        mid_keep = keep
        keep, keep_near, send = call(
            partial(mlp_out, dp_size, far_count),
            partial_sums,
            mlp_specs + [whole],
            scratch=[mlp_held, mlp_sems],
            cost=(2 * 4 * own * width * hidden, 8 * MIB),
        )(*mlp_weights_in, hidden_rows)
        mlp_core, mlp_near = scatter_rows(keep_near, send)
        mlp_keep = keep
        cut_shape = (dp_size, shards, mlp_piece, width)
        half_cut = struct((dp_size // 2, shards, mlp_piece, width), low)
        mlp_gain_part, down_keep, down_send, up_keep, up_send = call(
            partial(mlp_weights, dp_size, far_count),
            [struct((1, width), f32)] + [half_cut] * 4,
            mlp_specs + [whole] * 10,
            [whole] + [anywhere] * 4,
            [mlp_held, pltpu.VMEM(cut_shape, low), pltpu.VMEM(cut_shape, low), mlp_sems, pltpu.SemaphoreType.DMA((4,))],
            cost=(2 * 2 * 4 * own * width * hidden, 16 * MIB),
        )(*mlp_weights_in, hidden_rows, pre_grad, *normed_mid, *branch)

        mixed_grad, attn_grad_own = call(middle_back, [rows_f, rows_l], [whole] * 8)(
            mlp_gain_row, router, rows, grad_rows, attn_sum, mid_keep, mid_core, mid_near
        )
        attn_grad = gather_rows(attn_grad_own)
        half = width // 2
        cut_shape = (dp_size, shards, attn_piece, half)
        half_cut = struct((dp_size // 2, shards, attn_piece, half), low)
        proj_grad, attn_gain_part, *attn_cuts = call(
            partial(attn_backward, dp_size, far_count, head_size),
            [struct((4, 3 * size, own), low), struct((1, width), f32)] + [half_cut] * 4,
            attn_specs + [whole] * 11,
            [whole] * 2 + [anywhere] * 4,
            [
                attn_held,
                pltpu.VMEM((4, size, width), low),
                pltpu.VMEM(cut_shape, low),
                pltpu.VMEM(cut_shape, low),
                attn_sems,
                pltpu.SemaphoreType.DMA((4,)),
            ],
            cost=(2 * 2 * 4 * own * width * 4 * size, 16 * MIB),
        )(*attn_weights, proj, attended, log_total, *normed_in, *attn_grad)
        keep, keep_near, send = call(
            partial(attn_rows_back, dp_size, far_count, head_size),
            partial_sums,
            attn_specs + [whole],
            scratch=[attn_held, attn_sems],
            cost=(2 * 4 * own * width * 3 * size, 8 * MIB),
        )(*attn_weights, proj_grad)
        rows_core, rows_near = scatter_rows(keep_near, send)

        output, branch_sum = call(
            put_output,
            [struct(tokens.shape, low), rows_f],
            [place_block, line, row_block, row_block, row_block, pair_block, row_block, blocks],
            [blocks, row_block],
            [pltpu.VMEM((own, width), low)],
            grid,
        )(places, router, rows, attn_sum, mlp_keep, mlp_core, mlp_near, tokens)
        (router_part,) = call(router_product, [struct((1, width), f32)], [whole] * 3)(rows, grad_rows, branch_sum)
        (tokens_grad,) = call(
            put_grads,
            [struct(tokens.shape, low)],
            [place_block, line, line] + [row_block] * 5 + [pair_block, row_block, blocks],
            [blocks],
            [pltpu.VMEM((own, width), low)],
            grid,
        )(places, router, attn_gain_row, rows, grad_rows, branch_sum, mixed_grad, keep, rows_core, rows_near, cotangent)

        small = jnp.concatenate([router_part, attn_gain_part / attn_gain_row, mlp_gain_part / mlp_gain_row])
        for axis, bits in (("dp", dp_bits), ("tensor", [1, 2] + far_bits)):
            for bit in bits:
                small = small + swap(small, axis, bit)

        first, second = dp_bits, dp_bits[::-1]
        down_out = collect(down_keep, down_send, first).astype(f32).reshape(hidden_own, width)
        up_out = collect(up_keep, up_send, second).reshape(hidden_own, width).T.astype(f32)
        left = collect(*attn_cuts[:2], first).reshape(4, heads, head_size, half)
        right = collect(*attn_cuts[2:], second).reshape(4, heads, head_size, half)
        attn_out = jnp.concatenate([left, right], axis=3).astype(f32)
        return (
            output,
            tokens_grad,
            small[0],
            small[1],
            attn_out[:3],
            attn_out[3],
            small[2],
            up_out,
            down_out,
        )

    return local


def solution(mesh):
    rows = P(("dp", "tensor"), None)
    heads = P("tensor", None, None)
    return jax.shard_map(
        make_local(mesh.shape["dp"], mesh.shape["tensor"]),
        mesh=mesh,
        in_specs=(
            rows,
            rows,
            P(),
            P(),
            P(None, "tensor", None, None),
            heads,
            P(),
            P(None, "tensor"),
            P("tensor", None),
            rows,
        ),
        out_specs=(
            rows,
            rows,
            P(),
            P(),
            P(None, "tensor", None, None),
            heads,
            P(),
            P(None, "tensor"),
            P("tensor", None),
        ),
        check_vma=False,
    )
```

```python
from functools import partial

import jax
import jax.numpy as jnp
from jax import lax
from jax.experimental import pallas as pl
from jax.experimental.pallas import tpu as pltpu
from jax.sharding import PartitionSpec as P

epsilon = 1e-05
f32 = jnp.float32
low = jnp.bfloat16
MIB = 1 << 20
gelu_scale = 0.7978845608028654
whole = pl.BlockSpec(memory_space=pltpu.VMEM)
anywhere = pl.BlockSpec(memory_space=pl.ANY)
scalar = pl.BlockSpec(memory_space=pltpu.SMEM)


def nn(a, b):
    return lax.dot_general(a, b, (((1,), (0,)), ((), ())), preferred_element_type=f32)


def nt(a, b):
    return lax.dot_general(a, b, (((1,), (1,)), ((), ())), preferred_element_type=f32)


def tn(a, b):
    return lax.dot_general(a, b, (((0,), (0,)), ((), ())), preferred_element_type=f32)


def inverse_rms(values):
    return lax.rsqrt(jnp.mean(values * values, axis=1, keepdims=True) + epsilon)


def norm_back(values, inverse, gain, upstream):
    unit_rows = values * inverse
    scaled = upstream * gain
    return inverse * (scaled - unit_rows * jnp.mean(scaled * unit_rows, axis=1, keepdims=True))


def score_of(rows, router):
    return jnp.sum(rows * router, axis=1, keepdims=True)


def struct(shape, kind):
    return jax.ShapeDtypeStruct(shape, kind)


class Steps:
    def __init__(self):
        self.token = None

    def __call__(self, body, outs, in_specs, out_specs=None, scratch=(), grid=None, vmem=8, cost=(1e6, 1e6)):
        count = len(in_specs)
        first = self.token is None

        def run(*refs):
            if first:
                body(*refs[:count], *refs[count + 1 :])
            else:
                body(*refs[1 : count + 1], *refs[count + 2 :])

        kernel = pl.pallas_call(
            run,
            out_shape=[struct((8, 128), f32), *outs],
            in_specs=[*([] if first else [anywhere]), *in_specs],
            out_specs=[anywhere, *([whole] * len(outs) if out_specs is None else out_specs)],
            scratch_shapes=list(scratch),
            grid=() if grid is None else grid,
            compiler_params=pltpu.CompilerParams(vmem_limit_bytes=vmem * MIB),
            cost_estimate=pl.CostEstimate(flops=int(cost[0]), bytes_accessed=int(cost[1]), transcendentals=0),
        )

        def launch(*args):
            self.token, *results = kernel(*([] if first else [self.token]), *args)
            return results

        return launch


def picked(places_ref, block_ref, total_ref):
    count = places_ref.shape[1]
    step = pl.program_id(0)
    size = block_ref.shape[0]
    column = jnp.transpose(jnp.broadcast_to(places_ref[...], (128, count)))
    column = jnp.concatenate([column] * (size // 128), axis=1)
    ids = lax.broadcasted_iota(jnp.int32, (count, size), 1) + step * size
    part = nn(jnp.where(column == ids, 1.0, 0.0).astype(low), block_ref[...])

    @pl.when(step == 0)
    def _():
        total_ref[...] = part

    @pl.when(step > 0)
    def _():
        total_ref[...] += part


def pick_tokens(places_ref, gain_ref, tokens_ref, rows_ref, normed_ref, total_ref):
    picked(places_ref, tokens_ref, total_ref)

    @pl.when(pl.program_id(0) == pl.num_programs(0) - 1)
    def _():
        rows = total_ref[...]
        rows_ref[...] = rows.astype(low)
        normed_ref[...] = (rows * inverse_rms(rows) * gain_ref[...]).astype(low)


def pick_grads(places_ref, router_ref, rows_ref, grads_ref, grad_rows_ref, branch_ref, total_ref):
    picked(places_ref, grads_ref, total_ref)

    @pl.when(pl.program_id(0) == pl.num_programs(0) - 1)
    def _():
        grads = total_ref[...]
        score = score_of(rows_ref[...].astype(f32), router_ref[...].astype(f32))
        grad_rows_ref[...] = grads.astype(low)
        branch_ref[...] = (grads * score).astype(low)


def put_back(places_ref, rows_ref, block_ref, out_ref):
    count = places_ref.shape[1]
    size = block_ref.shape[0]
    ids = lax.broadcasted_iota(jnp.int32, (size, count), 0) + pl.program_id(0) * size
    chosen = jnp.where(ids == places_ref[...], 1.0, 0.0)
    listed = jnp.sum(chosen, axis=1, keepdims=True) > 0
    placed = nn(chosen.astype(low), rows_ref[...])
    out_ref[...] = jnp.where(listed, placed, block_ref[...].astype(f32)).astype(low)


def put_output(places_ref, router_ref, rows_ref, attn_ref, keep_ref, core_ref, near_ref, block_ref, out_ref, sum_ref, new_ref):
    @pl.when(pl.program_id(0) == 0)
    def _():
        rows = rows_ref[...].astype(f32)
        mlp = keep_ref[...] + core_ref[: keep_ref.shape[0]].astype(f32) + near_ref[...].astype(f32)
        branch_sum = attn_ref[...] + mlp
        sum_ref[...] = branch_sum
        new_ref[...] = (rows + score_of(rows, router_ref[...].astype(f32)) * branch_sum).astype(low)

    put_back(places_ref, new_ref, block_ref, out_ref)


def put_grads(
    places_ref, router_ref, gain_ref, rows_ref, grads_ref, sum_ref, mixed_ref, keep_ref, core_ref, near_ref, block_ref,
    out_ref, new_ref,
):
    @pl.when(pl.program_id(0) == 0)
    def _():
        rows = rows_ref[...].astype(f32)
        grads = grads_ref[...].astype(f32)
        normed_grad = keep_ref[...] + core_ref[: keep_ref.shape[0]].astype(f32) + near_ref[...].astype(f32)
        rows_back = norm_back(rows, inverse_rms(rows), gain_ref[...], normed_grad)
        score_grad = jnp.sum(grads * sum_ref[...], axis=1, keepdims=True)
        total = grads + mixed_ref[...] + rows_back + score_grad * router_ref[...].astype(f32)
        new_ref[...] = total.astype(low)

    put_back(places_ref, new_ref, block_ref, out_ref)


def middle(gain_ref, rows_ref, keep_ref, core_ref, near_ref, attn_ref, normed_ref):
    attn = keep_ref[...] + core_ref[: keep_ref.shape[0]].astype(f32) + near_ref[...].astype(f32)
    attn_ref[...] = attn
    mixed = rows_ref[...].astype(f32) + attn
    normed_ref[...] = (mixed * inverse_rms(mixed) * gain_ref[...]).astype(low)


def middle_back(
    gain_ref, router_ref, rows_ref, grads_ref, attn_ref, keep_ref, core_ref, near_ref, mixed_grad_ref, attn_grad_ref
):
    rows = rows_ref[...].astype(f32)
    mixed = rows + attn_ref[...]
    mid = keep_ref[...] + core_ref[: keep_ref.shape[0]].astype(f32) + near_ref[...].astype(f32)
    mixed_grad = norm_back(mixed, inverse_rms(mixed), gain_ref[...], mid)
    mixed_grad_ref[...] = mixed_grad
    branch = grads_ref[...].astype(f32) * score_of(rows, router_ref[...].astype(f32))
    attn_grad_ref[...] = (branch + mixed_grad).astype(low)


def fill_attn(me_ref, qkv_ref, out_ref, far_refs, dp_size, held_ref, sems):
    _, heads, head_size, _ = qkv_ref.shape
    rows = heads * head_size
    piece = 4 * rows // dp_size
    copies = []
    for h in range(heads):
        for c in range(3):
            copies.append((qkv_ref.at[c, h], held_ref.at[c, pl.ds(h * head_size, head_size)]))
        copies.append((out_ref.at[h], held_ref.at[3, pl.ds(h * head_size, head_size)]))
    for k, far_ref in enumerate(far_refs):
        shard, r = 1 + k // dp_size, k % dp_size
        start = lax.bitwise_xor(me_ref[0], r) * piece
        part = min(piece, rows)
        for p in range(piece // part):
            place = start + p * part
            inside = pl.multiple_of(lax.rem(place, rows), part)
            copies.append(
                (
                    far_ref.at[pl.ds(p * part, part)],
                    held_ref.at[lax.div(place, rows), pl.ds(shard * rows + inside, part)],
                )
            )
    started = [pltpu.make_async_copy(a, b, sems.at[i]) for i, (a, b) in enumerate(copies)]
    for c in started:
        c.start()
    return started


def attn_copies(heads, far_count, dp_size):
    return heads * 4 + far_count * max(1, 4 // dp_size)


def attn_forward(dp_size, far_count, head_size, *refs):
    me_ref, qkv_ref, out_ref = refs[:3]
    far_refs = refs[3 : 3 + far_count]
    rows_refs = refs[3 + far_count : 7 + far_count]
    held_ref, proj_ref, att_ref, log_ref, keep_own, keep_near, send_ref, sems = refs[7 + far_count :]
    started = fill_attn(me_ref, qkv_ref, out_ref, far_refs, dp_size, held_ref, sems)
    for c in started:
        c.wait()
    size, width = held_ref.shape[1:]
    count = rows_refs[0].shape[0]
    allowed = lax.broadcasted_iota(jnp.int32, (count, count), 0) <= lax.broadcasted_iota(jnp.int32, (count, count), 1)
    for s in (3, 2, 1, 0):
        proj = nt(held_ref[0:3].reshape(3 * size, width), rows_refs[s][...]).astype(low)
        proj_ref[s] = proj
        for h in range(size // head_size):
            a = h * head_size
            q, k, v = (proj[c * size + a : c * size + a + head_size] for c in range(3))
            logits = jnp.where(allowed, tn(k, q) * head_size**-0.5, -1e30)
            highest = jnp.max(logits, axis=0, keepdims=True)
            exponent = jnp.exp(logits - highest)
            total = jnp.sum(exponent, axis=0, keepdims=True)
            probs = (exponent * (1.0 / total)).astype(low)
            log_ref[s, h : h + 1] = highest + jnp.log(total)
            att_ref[s, a : a + head_size] = nn(v, probs).astype(low)
        part = tn(att_ref[s], held_ref[3])
        if s == 0:
            keep_own[...] = part
        elif s == 1:
            keep_near[...] = part
        else:
            send_ref[(s - 2) * count : (s - 1) * count] = part.astype(low)


def attn_backward(dp_size, shards, head_size, *refs):
    me_ref, held_ref, proj_ref, att_ref, log_ref = refs[:5]
    rows_refs, grad_refs = refs[5:9], refs[9:13]
    back_ref, gain_ref, *outs, total_ref, cut_a, cut_b, out_sems = refs[13:]
    size, width = held_ref.shape[1:]
    count = rows_refs[0].shape[0]
    allowed = lax.broadcasted_iota(jnp.int32, (count, count), 0) <= lax.broadcasted_iota(jnp.int32, (count, count), 1)
    scaling = head_size**-0.5
    for s in range(4):
        attended_grad = nt(held_ref[3], grad_refs[s][...]).astype(low)
        for h in range(size // head_size):
            a = h * head_size
            q, k, v = (proj_ref[s, c * size + a : c * size + a + head_size] for c in range(3))
            da = attended_grad[a : a + head_size]
            logits = jnp.where(allowed, tn(k, q) * scaling, -1e30)
            probs = jnp.exp(logits - log_ref[s, h : h + 1])
            prob_grad = tn(v, da)
            weighted = probs * prob_grad
            logit_grad = (weighted - probs * jnp.sum(weighted, axis=0, keepdims=True)).astype(low)
            back_ref[s, a : a + head_size] = (nn(k, logit_grad) * scaling).astype(low)
            back_ref[s, size + a : size + a + head_size] = (nt(q, logit_grad) * scaling).astype(low)
            back_ref[s, 2 * size + a : 2 * size + a + head_size] = nt(da, probs.astype(low)).astype(low)
    for c in range(4):
        total = None
        for s in range(4):
            left = att_ref[s] if c == 3 else back_ref[s, c * size : (c + 1) * size]
            right = grad_refs[s][...] if c == 3 else rows_refs[s][...]
            part = nn(left, right)
            total = part if total is None else total + part
        total_ref[c] = total.astype(low)
        if c < 3:
            share = jnp.sum(total * held_ref[c].astype(f32), axis=0, keepdims=True)
            gain_ref[...] = share if c == 0 else gain_ref[...] + share
    rows = size // shards
    piece = 4 * rows // dp_size
    part = min(piece, rows)
    half = width // 2
    for shard in range(shards):
        for a in range(dp_size):
            r = lax.bitwise_xor(me_ref[0], a)
            for p in range(piece // part):
                place = a * piece + p * part
                inside = shard * rows + place % rows
                cut = total_ref[place // rows, inside : inside + part]
                cut_a[position(r, dp_size, False) * shards + shard, p * part : (p + 1) * part] = cut[:, :half]
                cut_b[position(r, dp_size, True) * shards + shard, p * part : (p + 1) * part] = cut[:, half:]
    send_off((cut_a, cut_b), outs, out_sems)


def attn_rows_back(held_ref, back_ref, keep_own, keep_near, send_ref):
    size, width = held_ref.shape[1:]
    count = keep_own.shape[0]
    for s in (3, 2, 1, 0):
        part = tn(back_ref[s], held_ref[0:3].reshape(3 * size, width))
        if s == 0:
            keep_own[...] = part
        elif s == 1:
            keep_near[...] = part
        else:
            send_ref[(s - 2) * count : (s - 1) * count] = part.astype(low)


def position(r, dp_size, swapped):
    if swapped:
        return r
    bits = dp_size.bit_length() - 1
    place = 0
    for k in range(bits):
        place = place + lax.shift_left(lax.bitwise_and(lax.shift_right_logical(r, k), 1), bits - 1 - k)
    return place


def send_off(cuts, outs, sems):
    half = cuts[0].shape[0] // 2
    copies = []
    for k, cut in enumerate(cuts):
        copies.append(pltpu.make_async_copy(cut.at[pl.ds(0, half)], outs[0].at[k], sems.at[2 * k]))
        copies.append(pltpu.make_async_copy(cut.at[pl.ds(half, half)], outs[1 + k], sems.at[2 * k + 1]))
    for c in copies:
        c.start()
    for c in copies:
        c.wait()


def fold(packed, *refs):
    if packed:
        keep_ref, came_ref, *outs = refs
        came = [came_ref.at[0], came_ref.at[1]]
    else:
        keep_ref, *came = refs[:3]
        outs = refs[3:]
    count = keep_ref.shape[1]
    half = count // 2
    for k in range(2):
        total = keep_ref[k].astype(f32) + came[k][...].astype(f32)
        if half == 0:
            outs[0][k] = total[0].astype(low)
            continue
        outs[0][k] = total[:half].astype(low)
        if len(outs) == 2:
            outs[1][k] = total[half:].astype(low)
        else:
            outs[1 + k][...] = total[half:].astype(low)


def place_attn(me_ref, *refs):
    *piece_refs, qkv_ref, out_ref, all_ref, sems = refs
    half, rows = piece_refs[0].shape[2], all_ref.shape[1]
    piece = piece_refs[0].shape[1]
    part = min(piece, rows)
    for r, piece_ref in enumerate(piece_refs):
        start = lax.bitwise_xor(me_ref[0], r) * piece
        for p in range(piece // part):
            place = start + p * part
            inside = pl.ds(pl.multiple_of(lax.rem(place, rows), part), part)
            for k in range(2):
                all_ref[lax.div(place, rows), inside, k * half : (k + 1) * half] = piece_ref[
                    k, p * part : (p + 1) * part
                ].astype(f32)
    _, heads, head_size, _ = qkv_ref.shape
    copies = []
    for h in range(heads):
        span = pl.ds(h * head_size, head_size)
        for c in range(4):
            out = out_ref.at[h] if c == 3 else qkv_ref.at[c, h]
            copies.append(pltpu.make_async_copy(all_ref.at[c, span], out, sems.at[h * 4 + c]))
    for c in copies:
        c.start()
    for c in copies:
        c.wait()


def place_mlp(me_ref, *refs):
    *piece_refs, up_ref, down_ref, turned_ref = refs
    piece = piece_refs[0].shape[1]
    for r, piece_ref in enumerate(piece_refs):
        span = pl.ds(pl.multiple_of(lax.bitwise_xor(me_ref[0], r) * piece, piece), piece)
        down_ref[span] = piece_ref[0].astype(f32)
        turned_ref[span] = piece_ref[1].astype(f32)
    up_ref[...] = turned_ref[...].T


def cut_mlp(me_ref, up_ref, down_ref, turned_ref, piece_ref):
    turned_ref[...] = up_ref[...].astype(f32).T.astype(low)
    piece = piece_ref.shape[1]
    span = pl.ds(pl.multiple_of(me_ref[0] * piece, piece), piece)
    piece_ref[0] = turned_ref[span]
    piece_ref[1] = down_ref[span]


def near_sum(keep_ref, core_ref, out_ref):
    rows = keep_ref.shape[0]
    out_ref[...] = (keep_ref[...] + core_ref[rows:].astype(f32)).astype(low)


def small_start(attn_gain_ref, mlp_gain_ref, attn_ref, mlp_ref, rows_ref, grads_ref, sum_ref, out_ref):
    score_grad = jnp.sum(grads_ref[...].astype(f32) * sum_ref[...], axis=1, keepdims=True)
    out_ref[0:1] = jnp.sum(score_grad * rows_ref[...].astype(f32), axis=0, keepdims=True)
    out_ref[1:2] = attn_ref[...] / attn_gain_ref[...]
    out_ref[2:3] = mlp_ref[...] / mlp_gain_ref[...]


def small_sum(a_ref, b_ref, out_ref):
    out_ref[...] = a_ref[...] + b_ref[...]


def fill_mlp(me_ref, up_ref, down_ref, far_refs, dp_size, up_held, down_held, sems):
    rows = down_ref.shape[0]
    piece = rows // dp_size
    copies = []
    if up_held is not None:
        copies.append((up_ref, up_held.at[pl.ds(0, rows)]))
    if down_held is not None:
        copies.append((down_ref, down_held.at[pl.ds(0, rows)]))
    for k, far_ref in enumerate(far_refs):
        shard, r = 1 + k // dp_size, k % dp_size
        start = pl.multiple_of(shard * rows + lax.bitwise_xor(me_ref[0], r) * piece, piece)
        if up_held is not None:
            copies.append((far_ref.at[0], up_held.at[pl.ds(start, piece)]))
        if down_held is not None:
            copies.append((far_ref.at[1], down_held.at[pl.ds(start, piece)]))
    started = [pltpu.make_async_copy(a, b, sems.at[i]) for i, (a, b) in enumerate(copies)]
    for c in started:
        c.start()
    return started


def mlp_main(dp_size, far_count, *refs):
    me_ref, up_ref, down_ref = refs[:3]
    far_refs = refs[3 : 3 + far_count]
    rows_refs = refs[3 + far_count : 7 + far_count]
    grad_refs = refs[7 + far_count : 11 + far_count]
    up_held, down_held, hidden_ref, back_ref, keep_own, keep_near, send_ref, sems = refs[11 + far_count :]
    started = fill_mlp(me_ref, up_ref, down_ref, far_refs, dp_size, up_held, down_held, sems)
    for c in started:
        c.wait()
    count = rows_refs[0].shape[0]
    step = 256
    for s in (3, 2, 1, 0):
        normed = rows_refs[s][...]
        branch = grad_refs[s][...]

        for f in range(0, up_held.shape[0], step):
            pre = nt(up_held[f : f + step], normed)
            upstream = nt(down_held[f : f + step], branch)
            square = pre * pre
            tanh = jnp.tanh(pre * (gelu_scale + gelu_scale * 0.044715 * square))
            half = 0.5 + 0.5 * tanh
            hidden_ref[s, f : f + step] = (pre * half).astype(low)
            slope = half + (pre * (0.5 - 0.5 * tanh * tanh)) * (gelu_scale + 3 * gelu_scale * 0.044715 * square)
            back_ref[s, f : f + step] = (upstream * slope).astype(low)

        part = tn(back_ref[s], up_held[...])
        if s == 0:
            keep_own[...] = part
        elif s == 1:
            keep_near[...] = part
        else:
            send_ref[(s - 2) * count : (s - 1) * count] = part.astype(low)


def mlp_out(down_held, hidden_ref, keep_own, keep_near, send_ref):
    count = keep_own.shape[0]
    for s in (3, 2, 1, 0):
        part = tn(hidden_ref[s], down_held[...])
        if s == 0:
            keep_own[...] = part
        elif s == 1:
            keep_near[...] = part
        else:
            send_ref[(s - 2) * count : (s - 1) * count] = part.astype(low)


def mlp_weights(dp_size, shards, *refs):
    me_ref, up_held, hidden_ref, back_ref = refs[:4]
    rows_refs, grad_refs = refs[4:8], refs[8:12]
    gain_ref, *outs, cut_a, cut_b, out_sems = refs[12:]
    rows = up_held.shape[0] // shards
    piece = rows // dp_size
    for f in range(0, up_held.shape[0], rows):
        for a in range(dp_size):
            r = lax.bitwise_xor(me_ref[0], a)
            b = f + a * piece
            down_total, up_total = None, None
            for s in range(4):
                part = nn(hidden_ref[s, b : b + piece], grad_refs[s][...])
                down_total = part if down_total is None else down_total + part
                part = nn(back_ref[s, b : b + piece], rows_refs[s][...])
                up_total = part if up_total is None else up_total + part
            cut_a[position(r, dp_size, False) * shards + f // rows] = down_total.astype(low)
            cut_b[position(r, dp_size, True) * shards + f // rows] = up_total.astype(low)
            share = jnp.sum(up_total * up_held[b : b + piece].astype(f32), axis=0, keepdims=True)
            gain_ref[...] = share if b == 0 else gain_ref[...] + share
    send_off((cut_a, cut_b), outs, out_sems)


def make_local(dp_size, tensor_size):
    dp_bits = [1 << k for k in range(dp_size.bit_length() - 1)]
    far_bits = [1 << k for k in range(2, tensor_size.bit_length() - 1)]
    shards = tensor_size // 4
    far_count = (shards - 1) * dp_size

    def swap(x, axis, bit):
        size = dp_size if axis == "dp" else tensor_size
        return lax.ppermute(x, axis, [(i, i ^ bit) for i in range(size)])

    def far_spread(piece):
        found = [piece]
        for bit in far_bits:
            found = found + [swap(p, "tensor", bit) for p in found]
        return found[1:]

    def dp_spread(pieces):
        return [p if r == 0 else swap(p, "dp", r) for p in pieces for r in range(dp_size)]

    def local(
        tokens,
        routes,
        router_weight,
        attn_gain,
        qkv_weight,
        out_weight,
        mlp_gain,
        up_weight,
        down_weight,
        cotangent,
    ):
        seq_count, routed = routes.shape
        token_count, width = tokens.shape
        length = token_count // seq_count
        own = seq_count * routed
        heads, head_size = qkv_weight.shape[1:3]
        hidden_own = up_weight.shape[1]
        shard_rows = heads * head_size
        size = shards * shard_rows
        hidden = shards * hidden_own
        me = lax.axis_index("dp").astype(jnp.int32)[None]
        router = router_weight[None, :]
        attn_gain_row = attn_gain[None, :]
        mlp_gain_row = mlp_gain[None, :]
        places = (routes + jnp.arange(seq_count, dtype=jnp.int32)[:, None] * length).reshape(1, own)

        rows_f = struct((own, width), f32)
        rows_l = struct((own, width), low)
        line_f = struct((1, width), f32)
        block = 256
        grid = (token_count // block,)
        blocks = pl.BlockSpec((block, width), lambda i: (i, 0))
        steps = Steps()

        def flat(shape):
            return pl.BlockSpec(shape, lambda i: (0,) * len(shape))

        row_block = flat((own, width))
        line = flat((1, width))
        place_block = flat((1, own))
        pair_block = flat((2 * own, width))

        def gather_start(x):
            return x, swap(x, "tensor", 2), swap(x, "tensor", 1)

        def gather_end(x, near, core):
            return [x, near, core, swap(near, "tensor", 1)]

        def near_back(keep_near, core):
            (near,) = steps(near_sum, [rows_l], [whole] * 2)(keep_near, core)
            return swap(near, "tensor", 2)

        class Fold:
            def __init__(self, keep, sends, places):
                self.places = places
                self.keep = keep
                self.sent = [swap(x, "dp", bits[0]) for x, bits in zip(sends, (dp_bits, dp_bits[::-1]))]
                self.at = 1

            def step(self):
                _, count, piece, columns = self.keep.shape
                packed = len(self.sent) == 1
                half = count // 2
                kept = struct((2, half, piece, columns) if half else (2, piece, columns), low)
                at_dp = self.at < len(dp_bits)
                if half and at_dp:
                    outs = [kept] + [struct((half, piece, columns), low)] * 2
                else:
                    outs = [kept] * (2 if half else 1)
                results = steps(partial(fold, packed), outs, [whole] * (1 + len(self.sent)))(self.keep, *self.sent)
                self.keep = results[0]
                if not half:
                    self.pieces = [self.keep if r == 0 else swap(self.keep, "dp", r) for r in range(dp_size)]
                elif at_dp:
                    orders = (dp_bits, dp_bits[::-1])
                    self.sent = [swap(x, "dp", bits[self.at]) for x, bits in zip(results[1:], orders)]
                else:
                    self.sent = [swap(results[1], "tensor", far_bits[::-1][self.at - len(dp_bits)])]
                self.at += 1

            @property
            def left(self):
                return len(dp_bits) + len(far_bits) + 1 - self.at

        attn_own = jnp.concatenate(
            [qkv_weight.reshape(3 * shard_rows, width), out_weight.reshape(shard_rows, width)]
        )
        attn_piece = 4 * shard_rows // dp_size
        piece_own = lax.dynamic_slice_in_dim(attn_own, me[0] * attn_piece, attn_piece, 0)
        attn_far = far_spread(piece_own)
        steps.token = piece_own
        rows, normed_own = steps(
            pick_tokens,
            [rows_l, rows_l],
            [place_block, line, blocks],
            [row_block, row_block],
            [pltpu.VMEM((own, width), f32)],
            grid,
            vmem=56,
        )(places, attn_gain_row, tokens)
        normed_in = gather_start(normed_own)
        mlp_piece = hidden_own // dp_size
        up_turned, mlp_own = steps(
            cut_mlp, [struct((hidden_own, width), low), struct((2, mlp_piece, width), low)], [scalar, whole, whole]
        )(me, up_weight, down_weight)
        grad_rows, branch_own = steps(
            pick_grads,
            [rows_l, rows_l],
            [place_block, line, row_block, blocks],
            [row_block, row_block],
            [pltpu.VMEM((own, width), f32)],
            grid,
        )(places, router, rows, cotangent)
        attn_far = dp_spread(attn_far)
        normed_in = gather_end(*normed_in)
        mlp_far = far_spread(mlp_own)
        branch = gather_start(branch_own)

        attn_sems = pltpu.SemaphoreType.DMA((attn_copies(heads, far_count, dp_size),))
        partial_sums = [rows_f, rows_f, struct((2 * own, width), low)]
        head_count = size // head_size
        attn_held, proj, attended, log_total, attn_keep, keep_near, send = steps(
            partial(attn_forward, dp_size, far_count, head_size),
            [
                struct((4, size, width), low),
                struct((4, 3 * size, own), low),
                struct((4, size, own), low),
                struct((4, head_count, own), f32),
                *partial_sums,
            ],
            [scalar] + [anywhere] * (2 + far_count) + [whole] * 4,
            scratch=[attn_sems],
            cost=(2 * 4 * own * width * 4 * size, 12 * MIB),
        )(me, qkv_weight, out_weight, *attn_far, *normed_in)
        attn_core = swap(send, "tensor", 1)
        mlp_far = dp_spread(mlp_far)
        attn_near = near_back(keep_near, attn_core)
        branch = gather_end(*branch)
        attn_sum, normed_own = steps(middle, [rows_f, rows_l], [whole] * 5)(
            mlp_gain_row, rows, attn_keep, attn_core, attn_near
        )
        normed_mid = gather_end(*gather_start(normed_own))

        mlp_sems = pltpu.SemaphoreType.DMA((2 + 2 * far_count,))
        held = struct((hidden, width), low)
        up_held, down_held, hidden_rows, pre_grad, mid_keep, keep_near, send = steps(
            partial(mlp_main, dp_size, far_count),
            [held, held] + [struct((4, hidden, own), low)] * 2 + partial_sums,
            [scalar] + [anywhere] * (2 + far_count) + [whole] * 8,
            scratch=[mlp_sems],
            vmem=12,
            cost=(3 * 2 * 4 * own * width * hidden, 16 * MIB),
        )(me, up_turned, down_weight, *mlp_far, *normed_mid, *branch)
        mid_core = swap(send, "tensor", 1)
        mlp_keep, mlp_keep_near, send = steps(
            mlp_out, partial_sums, [whole] * 2, cost=(2 * 4 * own * width * hidden, 8 * MIB)
        )(down_held, hidden_rows)
        mid_near = near_back(keep_near, mid_core)
        mlp_core = swap(send, "tensor", 1)
        cuts = dp_size * shards
        cut_shape = (cuts, mlp_piece, width)
        half_cut = struct((cuts // 2, mlp_piece, width), low)
        mlp_gain_part, down_up_keep, down_send, up_send = steps(
            partial(mlp_weights, dp_size, shards),
            [line_f, struct((2, cuts // 2, mlp_piece, width), low), half_cut, half_cut],
            [scalar] + [whole] * 11,
            [whole] + [anywhere] * 3,
            [pltpu.VMEM(cut_shape, low), pltpu.VMEM(cut_shape, low), pltpu.SemaphoreType.DMA((4,))],
            vmem=16,
            cost=(2 * 2 * 4 * own * width * hidden, 16 * MIB),
        )(me, up_held, hidden_rows, pre_grad, *normed_mid, *branch)
        mlp_fold = Fold(down_up_keep, (down_send, up_send), place_mlp)
        mlp_near = near_back(mlp_keep_near, mlp_core)

        mixed_grad, attn_grad_own = steps(middle_back, [rows_f, rows_l], [whole] * 8)(
            mlp_gain_row, router, rows, grad_rows, attn_sum, mid_keep, mid_core, mid_near
        )
        attn_grad = gather_start(attn_grad_own)
        output, branch_sum = steps(
            put_output,
            [struct(tokens.shape, low), rows_f],
            [place_block, line, row_block, row_block, row_block, pair_block, row_block, blocks],
            [blocks, row_block],
            [pltpu.VMEM((own, width), low)],
            grid,
        )(places, router, rows, attn_sum, mlp_keep, mlp_core, mlp_near, tokens)
        mlp_fold.step()
        attn_grad = gather_end(*attn_grad)
        half = width // 2
        cut_shape = (cuts, attn_piece, half)
        half_cut = struct((cuts // 2, attn_piece, half), low)
        proj_grad, attn_gain_part, attn_cut_keep, *attn_cuts = steps(
            partial(attn_backward, dp_size, shards, head_size),
            [struct((4, 3 * size, own), low), line_f, struct((2, cuts // 2, attn_piece, half), low), half_cut, half_cut],
            [scalar] + [whole] * 12,
            [whole] * 2 + [anywhere] * 3,
            [
                pltpu.VMEM((4, size, width), low),
                pltpu.VMEM(cut_shape, low),
                pltpu.VMEM(cut_shape, low),
                pltpu.SemaphoreType.DMA((4,)),
            ],
            vmem=16,
            cost=(2 * 2 * 4 * own * width * 4 * size, 16 * MIB),
        )(me, attn_held, proj, attended, log_total, *normed_in, *attn_grad)
        attn_fold = Fold(attn_cut_keep, attn_cuts, place_attn)
        rows_keep, keep_near, send = steps(
            attn_rows_back, partial_sums, [whole] * 2, cost=(2 * 4 * own * width * 3 * size, 8 * MIB)
        )(attn_held, proj_grad)
        rows_core = swap(send, "tensor", 1)
        mlp_fold.step()
        rows_near = near_back(keep_near, rows_core)
        small_bits = [("dp", bit) for bit in dp_bits] + [("tensor", bit) for bit in [1, 2] + far_bits]

        def small_step(small, k):
            return steps(small_sum, [struct((3, width), f32)], [whole] * 2)(small, swap(small, *small_bits[k]))[0]

        (small,) = steps(small_start, [struct((3, width), f32)], [whole] * 7)(
            attn_gain_row, mlp_gain_row, attn_gain_part, mlp_gain_part, rows, grad_rows, branch_sum
        )
        attn_fold.step()
        small = small_step(small, 0)
        while mlp_fold.left:
            mlp_fold.step()
        small = small_step(small, 1)
        attn_fold.step()
        (tokens_grad,) = steps(
            put_grads,
            [struct(tokens.shape, low)],
            [place_block, line, line] + [row_block] * 5 + [pair_block, row_block, blocks],
            [blocks],
            [pltpu.VMEM((own, width), low)],
            grid,
        )(
            places, router, attn_gain_row, rows, grad_rows, branch_sum, mixed_grad, rows_keep, rows_core, rows_near,
            cotangent,
        )
        while attn_fold.left:
            attn_fold.step()
        for k in range(2, len(small_bits)):
            small = small_step(small, k)
        up_out, down_out = steps(
            place_mlp,
            [struct(up_weight.shape, f32), struct(down_weight.shape, f32)],
            [scalar] + [whole] * dp_size,
            scratch=[pltpu.VMEM((hidden_own, width), f32)],
        )(me, *mlp_fold.pieces)
        qkv_out, out_out = steps(
            place_attn,
            [struct(qkv_weight.shape, f32), struct(out_weight.shape, f32)],
            [scalar] + [whole] * dp_size,
            [anywhere] * 2,
            [pltpu.VMEM((4, shard_rows, width), f32), pltpu.SemaphoreType.DMA((4 * heads,))],
        )(me, *attn_fold.pieces)
        return (output, tokens_grad, small[0], small[1], qkv_out, out_out, small[2], up_out, down_out)

    return local


def solution(mesh):
    rows = P(("dp", "tensor"), None)
    heads = P("tensor", None, None)
    return jax.shard_map(
        make_local(mesh.shape["dp"], mesh.shape["tensor"]),
        mesh=mesh,
        in_specs=(
            rows,
            rows,
            P(),
            P(),
            P(None, "tensor", None, None),
            heads,
            P(),
            P(None, "tensor"),
            P("tensor", None),
            rows,
        ),
        out_specs=(
            rows,
            rows,
            P(),
            P(),
            P(None, "tensor", None, None),
            heads,
            P(),
            P(None, "tensor"),
            P("tensor", None),
        ),
        check_vma=False,
    )
```

```python
from functools import partial

import jax
import jax.numpy as jnp
from jax import lax
from jax.experimental import pallas as pl
from jax.experimental.pallas import tpu as pltpu
from jax.sharding import PartitionSpec as P

epsilon = 1e-05
f32 = jnp.float32
low = jnp.bfloat16
MIB = 1 << 20
unit = 1.0e9
gelu_scale = 0.7978845608028654
whole = pl.BlockSpec(memory_space=pltpu.VMEM)
anywhere = pl.BlockSpec(memory_space=pl.ANY)
scalar = pl.BlockSpec(memory_space=pltpu.SMEM)


def nn(a, b):
    return lax.dot_general(a, b, (((1,), (0,)), ((), ())), preferred_element_type=f32)


def nt(a, b):
    return lax.dot_general(a, b, (((1,), (1,)), ((), ())), preferred_element_type=f32)


def tn(a, b):
    return lax.dot_general(a, b, (((0,), (0,)), ((), ())), preferred_element_type=f32)


def inverse_rms(values):
    return lax.rsqrt(jnp.mean(values * values, axis=1, keepdims=True) + epsilon)


def norm_back(values, inverse, gain, upstream):
    unit_rows = values * inverse
    scaled = upstream * gain
    return inverse * (scaled - unit_rows * jnp.mean(scaled * unit_rows, axis=1, keepdims=True))


def score_of(rows, router):
    return jnp.sum(rows * router, axis=1, keepdims=True)


def struct(shape, kind):
    return jax.ShapeDtypeStruct(shape, kind)


class Steps:
    def __init__(self):
        self.token = None

    def __call__(self, body, outs, in_specs, out_specs=None, scratch=(), grid=None, vmem=8, cost=0.0):
        count = len(in_specs)
        first = self.token is None

        def run(*refs):
            if first:
                body(*refs[:count], *refs[count + 1 :])
            else:
                body(*refs[1 : count + 1], *refs[count + 2 :])

        kernel = pl.pallas_call(
            run,
            out_shape=[struct((8, 128), f32), *outs],
            in_specs=[*([] if first else [anywhere]), *in_specs],
            out_specs=[anywhere, *([whole] * len(outs) if out_specs is None else out_specs)],
            scratch_shapes=list(scratch),
            grid=() if grid is None else grid,
            compiler_params=pltpu.CompilerParams(vmem_limit_bytes=vmem * MIB),
            cost_estimate=pl.CostEstimate(flops=1 + int(cost * unit), bytes_accessed=1, transcendentals=0),
        )

        def launch(*args):
            self.token, *results = kernel(*([] if first else [self.token]), *args)
            return results

        return launch


    def hold(self, *arrays):
        count = len(arrays)
        kernel = pl.pallas_call(
            lambda *refs: None,
            out_shape=[struct((8, 128), f32)] + [struct(x.shape, x.dtype) for x in arrays],
            in_specs=[anywhere] * (1 + count),
            out_specs=[anywhere] * (1 + count),
            input_output_aliases={1 + k: 1 + k for k in range(count)},
            compiler_params=pltpu.CompilerParams(vmem_limit_bytes=MIB),
            cost_estimate=pl.CostEstimate(flops=1, bytes_accessed=1, transcendentals=0),
        )
        self.token, *arrays = kernel(self.token, *arrays)
        return arrays


def picked(places_ref, source_ref, held_ref, sems, size=256):
    count = places_ref.shape[1]
    parts = source_ref.shape[0] // size
    copies = [
        pltpu.make_async_copy(source_ref.at[pl.ds(k * size, size)], held_ref.at[pl.ds(k * size, size)], sems.at[k])
        for k in range(parts)
    ]
    for c in copies:
        c.start()
    column = jnp.transpose(jnp.broadcast_to(places_ref[...], (128, count)))
    column = jnp.concatenate([column] * (size // 128), axis=1)
    ids = lax.broadcasted_iota(jnp.int32, (count, size), 1)
    total = None
    for k in range(parts):
        copies[k].wait()
        part = nn(jnp.where(column == ids + k * size, 1.0, 0.0).astype(low), held_ref[k * size : (k + 1) * size])
        total = part if total is None else total + part
    return total


def pick_tokens(places_ref, gain_ref, tokens_ref, rows_ref, first_ref, second_ref, held_ref, sems):
    rows = picked(places_ref, tokens_ref, held_ref, sems)
    rows_ref[...] = rows.astype(low)
    normed = (rows * inverse_rms(rows) * gain_ref[...]).astype(low)
    half = first_ref.shape[0]
    first_ref[...] = normed[:half]
    second_ref[...] = normed[half:]


def pick_grads(
    me_ref, places_ref, router_ref, rows_ref, up_ref, down_ref, grads_ref,
    grad_rows_ref, branch_ref, turned_ref, up_piece_ref, down_piece_ref, held_ref, sems,
):
    grads = picked(places_ref, grads_ref, held_ref, sems)
    score = score_of(rows_ref[...].astype(f32), router_ref[...].astype(f32))
    grad_rows_ref[...] = grads.astype(low)
    branch_ref[...] = (grads * score).astype(low)
    turned_ref[...] = up_ref[...].astype(f32).T.astype(low)
    piece = up_piece_ref.shape[0]
    span = pl.ds(pl.multiple_of(me_ref[0] * piece, piece), piece)
    up_piece_ref[...] = turned_ref[span]
    down_piece_ref[...] = down_ref[span]


def put_back(places_ref, rows_ref, block_ref, out_ref):
    count = places_ref.shape[1]
    size = block_ref.shape[0]
    ids = lax.broadcasted_iota(jnp.int32, (size, count), 0) + pl.program_id(0) * size
    chosen = jnp.where(ids == places_ref[...], 1.0, 0.0)
    listed = jnp.sum(chosen, axis=1, keepdims=True) > 0
    placed = nn(chosen.astype(low), rows_ref[...])
    out_ref[...] = jnp.where(listed, placed, block_ref[...].astype(f32)).astype(low)


def put_output(
    places_ref, router_ref, rows_ref, attn_a_ref, attn_b_ref, keep_ref, came_ref, block_ref, out_ref, sum_ref, new_ref
):
    @pl.when(pl.program_id(0) == 0)
    def _():
        rows = rows_ref[...].astype(f32)
        half = attn_a_ref.shape[0]
        mlp = keep_ref[...] + came_ref[...].astype(f32)
        sum_ref[:half] = attn_a_ref[...] + mlp[:half]
        sum_ref[half:] = attn_b_ref[...] + mlp[half:]
        new_ref[...] = (rows + score_of(rows, router_ref[...].astype(f32)) * sum_ref[...]).astype(low)

    put_back(places_ref, new_ref, block_ref, out_ref)


def put_grads(
    places_ref, router_ref, gain_ref, rows_ref, grads_ref, sum_ref, mixed_a_ref, mixed_b_ref, keep_ref, came_ref,
    block_ref, out_ref, new_ref,
):
    @pl.when(pl.program_id(0) == 0)
    def _():
        rows = rows_ref[...].astype(f32)
        grads = grads_ref[...].astype(f32)
        half = mixed_a_ref.shape[0]
        normed_grad = keep_ref[...] + came_ref[...].astype(f32)
        rows_back = norm_back(rows, inverse_rms(rows), gain_ref[...], normed_grad)
        score_grad = jnp.sum(grads * sum_ref[...], axis=1, keepdims=True)
        total = grads + rows_back + score_grad * router_ref[...].astype(f32)
        new_ref[:half] = (total[:half] + mixed_a_ref[...]).astype(low)
        new_ref[half:] = (total[half:] + mixed_b_ref[...]).astype(low)

    put_back(places_ref, new_ref, block_ref, out_ref)


def middle(chunk, gain_ref, rows_ref, keep_ref, came_ref, attn_ref, normed_ref):
    count = keep_ref.shape[0]
    attn = keep_ref[...] + came_ref[...].astype(f32)
    attn_ref[...] = attn
    mixed = rows_ref[chunk * count : (chunk + 1) * count].astype(f32) + attn
    normed_ref[...] = (mixed * inverse_rms(mixed) * gain_ref[...]).astype(low)


def middle_back(
    chunk, gain_ref, router_ref, rows_ref, grads_ref, attn_ref, keep_ref, came_ref, mixed_grad_ref, attn_grad_ref
):
    count = keep_ref.shape[0]
    span = slice(chunk * count, (chunk + 1) * count)
    rows = rows_ref[span].astype(f32)
    mixed = rows + attn_ref[...]
    mid = keep_ref[...] + came_ref[...].astype(f32)
    mixed_grad = norm_back(mixed, inverse_rms(mixed), gain_ref[...], mid)
    mixed_grad_ref[...] = mixed_grad
    branch = grads_ref[span].astype(f32) * score_of(rows, router_ref[...].astype(f32))
    attn_grad_ref[...] = (branch + mixed_grad).astype(low)


def pack_attn(me_ref, qkv_ref, out_ref, packed_ref, piece_ref, sems):
    _, heads, head_size, _ = qkv_ref.shape
    copies = []
    for h in range(heads):
        span = pl.ds(h * head_size, head_size)
        for c in range(4):
            source = out_ref.at[h] if c == 3 else qkv_ref.at[c, h]
            copies.append(pltpu.make_async_copy(source, packed_ref.at[c, span], sems.at[h * 4 + c]))
    for c in copies:
        c.start()
    for c in copies:
        c.wait()
    piece, rows = piece_ref.shape[0], packed_ref.shape[1]
    part = min(piece, rows)
    for p in range(piece // part):
        place = me_ref[0] * piece + p * part
        inside = pl.ds(pl.multiple_of(lax.rem(place, rows), part), part)
        piece_ref[p * part : (p + 1) * part] = packed_ref[lax.div(place, rows), inside]


def join_attn(dp_size, me_ref, *refs):
    count = len(refs) // (dp_size + 1)
    for f in range(count):
        far_ref = refs[count * dp_size + f]
        rows = far_ref.shape[1]
        for r in range(dp_size):
            piece_ref = refs[f * dp_size + r]
            piece = piece_ref.shape[0]
            part = min(piece, rows)
            for p in range(piece // part):
                place = lax.bitwise_xor(me_ref[0], r) * piece + p * part
                inside = pl.ds(pl.multiple_of(lax.rem(place, rows), part), part)
                far_ref[lax.div(place, rows), inside] = piece_ref[p * part : (p + 1) * part]


def join_mlp(dp_size, me_ref, *refs):
    count = len(refs) // (dp_size + 1)
    for f in range(count):
        far_ref = refs[count * dp_size + f]
        for r in range(dp_size):
            piece_ref = refs[f * dp_size + r]
            piece = piece_ref.shape[0]
            start = pl.multiple_of(lax.bitwise_xor(me_ref[0], r) * piece, piece)
            far_ref[pl.ds(start, piece)] = piece_ref[...]


def logits_of(query, key):
    keys, queries = key.shape[1], query.shape[1]
    shape = (keys, queries)
    allowed = lax.broadcasted_iota(jnp.int32, shape, 0) <= lax.broadcasted_iota(jnp.int32, shape, 1) + (keys - queries)
    return jnp.where(allowed, tn(key, query) * key.shape[0] ** -0.5, -1e30)


def attn_forward(shards, head_size, chunk, *refs):
    weights, (own_ref, near_ref), refs = refs[:shards], refs[shards : shards + 2], refs[shards + 2 :]
    if chunk:
        first_rows, first_near, first_proj, first_even, first_odd, *refs = refs
    proj_ref, even_ref, odd_ref, log_ref, keep_ref, send_ref, *pack_ref = refs
    size = weights[0].shape[1]
    heads = size // head_size
    count = own_ref.shape[0]
    base = 2 * count * chunk
    rows = jnp.concatenate([own_ref[...], near_ref[...]], axis=0)
    total = None
    for s in range(shards):
        proj = nt(weights[s][0:3].reshape(3 * size, -1), rows).astype(low)
        proj_ref[s, :, base : base + 2 * count] = proj
        att_ref = odd_ref if s % 2 else even_ref
        if chunk:
            proj_ref[s, :, :base] = first_proj[s]
            att_ref[s // 2, :, :base] = (first_odd if s % 2 else first_even)[s // 2]
        for h in range(heads):
            spans = [slice(c * size + h * head_size, c * size + (h + 1) * head_size) for c in range(3)]
            for q in range(2):
                mine = slice(q * count, (q + 1) * count)
                query, key, value = (proj[span, mine] for span in spans)
                if chunk:
                    key = jnp.concatenate([first_proj[s, spans[1], mine], key], axis=1)
                    value = jnp.concatenate([first_proj[s, spans[2], mine], value], axis=1)
                logits = logits_of(query, key)
                highest = jnp.max(logits, axis=0, keepdims=True)
                exponent = jnp.exp(logits - highest)
                sums = jnp.sum(exponent, axis=0, keepdims=True)
                probs = (exponent * (1.0 / sums)).astype(low)
                line = (s * heads + h) * 2 + q
                log_ref[line : line + 1] = highest + jnp.log(sums)
                att_ref[s // 2, spans[0], base + q * count : base + (q + 1) * count] = nn(value, probs).astype(low)
        part = tn(att_ref[s // 2, :, base : base + 2 * count], weights[s][3])
        total = part if total is None else total + part
    keep_ref[...] = total[:count]
    send_ref[...] = total[count:].astype(low)
    if chunk:
        for k, ref in enumerate((first_rows, first_near, own_ref, near_ref)):
            pack_ref[0][k * count : (k + 1) * count] = ref[...]


def attended_back(shards, *refs):
    weights, grad_refs, (pack_ref, back_ref) = refs[:shards], refs[shards : shards + 4], refs[shards + 4 :]
    count = grad_refs[0].shape[0]
    for k in range(4):
        pack_ref[k * count : (k + 1) * count] = grad_refs[k][...]
    for s in range(shards):
        back_ref[s] = nt(weights[s][3], pack_ref[...]).astype(low)


def attn_backward(shards, head_size, *refs):
    attended_grad_ref, proj_ref, log_a_ref, log_b_ref, even_ref, odd_ref = refs
    size = attended_grad_ref.shape[1]
    heads = size // head_size
    count = proj_ref.shape[2] // 4
    scaling = head_size**-0.5
    for s in range(shards):
        back_ref = odd_ref if s % 2 else even_ref
        for h in range(heads):
            spans = [slice(c * size + h * head_size, c * size + (h + 1) * head_size) for c in range(3)]
            for q in range(2):
                first = slice(q * count, (q + 1) * count)
                second = slice((2 + q) * count, (3 + q) * count)
                line = (s * heads + h) * 2 + q
                key_a, value_a = (proj_ref[s, span, first] for span in spans[1:])
                key_grad, value_grad = None, None
                for mine, log_ref in ((second, log_b_ref), (first, log_a_ref)):
                    query = proj_ref[s, spans[0], mine]
                    upstream = attended_grad_ref[s, spans[0], mine]
                    key, value = key_a, value_a
                    if mine is second:
                        key = jnp.concatenate([key, proj_ref[s, spans[1], mine]], axis=1)
                        value = jnp.concatenate([value, proj_ref[s, spans[2], mine]], axis=1)
                    probs = jnp.exp(logits_of(query, key) - log_ref[line : line + 1])
                    weighted = probs * tn(value, upstream)
                    logit_grad = (weighted - probs * jnp.sum(weighted, axis=0, keepdims=True)).astype(low)
                    back_ref[s // 2, spans[0], mine] = (nn(key, logit_grad) * scaling).astype(low)
                    key_part = nt(query, logit_grad)
                    value_part = nt(upstream, probs.astype(low))
                    if mine is second:
                        key_grad, value_grad = key_part[:, :count], value_part[:, :count]
                        back_ref[s // 2, spans[1], mine] = (key_part[:, count:] * scaling).astype(low)
                        back_ref[s // 2, spans[2], mine] = value_part[:, count:].astype(low)
                    else:
                        back_ref[s // 2, spans[1], mine] = ((key_part + key_grad) * scaling).astype(low)
                        back_ref[s // 2, spans[2], mine] = (value_part + value_grad).astype(low)


def split_rows(total, keep_ref, send_ref):
    count = total.shape[0] // 4
    keep_ref[:count] = total[:count]
    keep_ref[count:] = total[2 * count : 3 * count]
    send_ref[:count] = total[count : 2 * count].astype(low)
    send_ref[count:] = total[3 * count :].astype(low)


def attn_rows_back(shards, *refs):
    weights, (even_ref, odd_ref, keep_ref, send_ref) = refs[:shards], refs[shards:]
    size = weights[0].shape[1]
    total = None
    for s in range(shards):
        part = tn((odd_ref if s % 2 else even_ref)[s // 2], weights[s][0:3].reshape(3 * size, -1))
        total = part if total is None else total + part
    split_rows(total, keep_ref, send_ref)


def attn_weights(dp_size, far, *refs):
    me_ref, refs = refs[0], refs[1:]
    weights, refs = refs[:far], refs[far:]
    back_ref, back_came, att_ref, att_came, rows_ref, rows_came, grad_ref, grad_came, gain_ref, *refs = refs
    *outs, total_ref, cut_a, cut_b, out_sems = refs
    size = weights[0].shape[1]
    half = cut_a.shape[2]
    piece = 4 * size // dp_size
    part = min(piece, size)
    for f in range(far):
        for c in range(4):
            if c == 3:
                total = nn(att_ref[f], grad_ref[...]) + nn(att_came[f], grad_came[...])
            else:
                span = slice(c * size, (c + 1) * size)
                total = nn(back_ref[f, span], rows_ref[...]) + nn(back_came[f, span], rows_came[...])
                share = jnp.sum(total * weights[f][c].astype(f32), axis=0, keepdims=True)
                gain_ref[...] = share if f == 0 and c == 0 else gain_ref[...] + share
            total_ref[c] = total.astype(low)
        for a in range(dp_size):
            r = lax.bitwise_xor(me_ref[0], a)
            for p in range(piece // part):
                place = a * piece + p * part
                cut = total_ref[place // size, place % size : place % size + part]
                cut_a[position(r, dp_size, False) * far + f, p * part : (p + 1) * part] = cut[:, :half]
                cut_b[position(r, dp_size, True) * far + f, p * part : (p + 1) * part] = cut[:, half:]
    send_off((cut_a, cut_b), outs, out_sems)


def mlp_main(shards, chunk, *refs):
    ups, downs, refs = refs[:shards], refs[shards : 2 * shards], refs[2 * shards :]
    (own_ref, near_ref, grad_ref, grad_near), refs = refs[:4], refs[4:]
    if chunk:
        first_rows, first_near, *refs = refs
    even_ref, odd_ref, keep_ref, send_ref, *pack_refs = refs
    count = own_ref.shape[0]
    span = slice(chunk * count, (chunk + 1) * count)
    rows = jnp.concatenate([own_ref[...], near_ref[...]], axis=0)
    branch = jnp.concatenate([grad_ref[span], grad_near[span]], axis=0)
    hidden = ups[0].shape[0]
    step = min(256, hidden)
    total = None
    for s in range(shards):
        act_ref = odd_ref if s % 2 else even_ref
        for f in range(0, hidden, step):
            pre = nt(ups[s][f : f + step], rows)
            upstream = nt(downs[s][f : f + step], branch)
            square = pre * pre
            tanh = jnp.tanh(pre * (gelu_scale + gelu_scale * 0.044715 * square))
            half = 0.5 + 0.5 * tanh
            slope = half + (pre * (0.5 - 0.5 * tanh * tanh)) * (gelu_scale + 3 * gelu_scale * 0.044715 * square)
            at = (s // 2) * hidden + f
            act_ref[0, at : at + step] = (pre * half).astype(low)
            act_ref[1, at : at + step] = (upstream * slope).astype(low)
        part = tn(act_ref[1, (s // 2) * hidden : (s // 2 + 1) * hidden], ups[s][...])
        total = part if total is None else total + part
    keep_ref[...] = total[:count]
    send_ref[...] = total[count:].astype(low)
    if chunk:
        for k, ref in enumerate((first_rows, first_near, own_ref, near_ref)):
            pack_refs[0][k * count : (k + 1) * count] = ref[...]
    else:
        for k, ref in enumerate((grad_ref, grad_near)):
            pack_refs[0][k * count : (k + 1) * count] = ref[:count]
            pack_refs[0][(2 + k) * count : (3 + k) * count] = ref[count:]


def mlp_out(shards, *refs):
    weights, (even_a, odd_a, even_b, odd_b, keep_ref, send_ref) = refs[:shards], refs[shards:]
    hidden = weights[0].shape[0]
    count = keep_ref.shape[0] // 2
    for k, (even_ref, odd_ref) in enumerate(((even_a, odd_a), (even_b, odd_b))):
        total = None
        for s in range(shards):
            span = slice((s // 2) * hidden, (s // 2 + 1) * hidden)
            part = tn((odd_ref if s % 2 else even_ref)[0, span], weights[s][...])
            total = part if total is None else total + part
        keep_ref[k * count : (k + 1) * count] = total[:count]
        send_ref[k * count : (k + 1) * count] = total[count:].astype(low)


def mlp_weights(dp_size, far, slot, *refs):
    me_ref, act_a, act_b, came_a, came_b, rows_ref, rows_came, *rest = refs
    if slot:
        weights, (gain_ref, *rest) = rest[:far], rest[far:]
    *outs, cut_a, cut_b, out_sems = rest
    hidden = act_a.shape[1] // far
    half = cut_a.shape[2]
    piece = hidden // dp_size
    count = act_a.shape[2]
    for f in range(far):
        for a in range(dp_size):
            r = lax.bitwise_xor(me_ref[0], a)
            b = f * hidden + a * piece
            span = slice(b, b + piece)
            total = nn(act_a[slot, span], rows_ref[:count]) + nn(act_b[slot, span], rows_ref[count:])
            total += nn(came_a[slot, span], rows_came[:count]) + nn(came_b[slot, span], rows_came[count:])
            cut_a[position(r, dp_size, False) * far + f] = total[:, :half].astype(low)
            cut_b[position(r, dp_size, True) * far + f] = total[:, half:].astype(low)
            if slot:
                share = jnp.sum(total * weights[f][a * piece : (a + 1) * piece].astype(f32), axis=0, keepdims=True)
                gain_ref[...] = share if b == 0 else gain_ref[...] + share
    send_off((cut_a, cut_b), outs, out_sems)


def position(r, dp_size, swapped):
    if swapped:
        return r
    bits = dp_size.bit_length() - 1
    place = 0
    for k in range(bits):
        place = place + lax.shift_left(lax.bitwise_and(lax.shift_right_logical(r, k), 1), bits - 1 - k)
    return place


def send_off(cuts, outs, sems):
    half = cuts[0].shape[0] // 2
    copies = []
    for k, cut in enumerate(cuts):
        copies.append(pltpu.make_async_copy(cut.at[pl.ds(0, half)], outs[0].at[k], sems.at[2 * k]))
        copies.append(pltpu.make_async_copy(cut.at[pl.ds(half, half)], outs[1 + k], sems.at[2 * k + 1]))
    for c in copies:
        c.start()
    for c in copies:
        c.wait()


def fold(packed, *refs):
    if packed:
        keep_ref, came_ref, *outs = refs
        came = [came_ref.at[0], came_ref.at[1]]
    else:
        keep_ref, *came = refs[:3]
        outs = refs[3:]
    count = keep_ref.shape[1]
    half = count // 2
    for k in range(2):
        total = keep_ref[k].astype(f32) + came[k][...].astype(f32)
        if half == 0:
            outs[0][k] = total[0].astype(low)
            continue
        outs[0][k] = total[:half].astype(low)
        if len(outs) == 2:
            outs[1][k] = total[half:].astype(low)
        else:
            outs[1 + k][...] = total[half:].astype(low)


def place_attn(me_ref, *refs):
    *piece_refs, qkv_ref, out_ref, all_ref, sems = refs
    half, rows = piece_refs[0].shape[2], all_ref.shape[1]
    piece = piece_refs[0].shape[1]
    part = min(piece, rows)
    for r, piece_ref in enumerate(piece_refs):
        start = lax.bitwise_xor(me_ref[0], r) * piece
        for p in range(piece // part):
            place = start + p * part
            inside = pl.ds(pl.multiple_of(lax.rem(place, rows), part), part)
            for k in range(2):
                all_ref[lax.div(place, rows), inside, k * half : (k + 1) * half] = piece_ref[
                    k, p * part : (p + 1) * part
                ].astype(f32)
    _, heads, head_size, _ = qkv_ref.shape
    copies = []
    for h in range(heads):
        span = pl.ds(h * head_size, head_size)
        for c in range(4):
            out = out_ref.at[h] if c == 3 else qkv_ref.at[c, h]
            copies.append(pltpu.make_async_copy(all_ref.at[c, span], out, sems.at[h * 4 + c]))
    for c in copies:
        c.start()
    for c in copies:
        c.wait()


def place_mlp(turn, me_ref, *refs):
    *piece_refs, out_ref = refs[:-1] if turn else refs
    target = refs[-1] if turn else out_ref
    _, piece, half = piece_refs[0].shape
    for r, piece_ref in enumerate(piece_refs):
        span = pl.ds(pl.multiple_of(lax.bitwise_xor(me_ref[0], r) * piece, piece), piece)
        for k in range(2):
            target[span, k * half : (k + 1) * half] = piece_ref[k].astype(f32)
    if turn:
        out_ref[...] = target[...].T


def small_start(attn_gain_ref, mlp_gain_ref, attn_ref, mlp_ref, rows_ref, grads_ref, sum_ref, out_ref):
    score_grad = jnp.sum(grads_ref[...].astype(f32) * sum_ref[...], axis=1, keepdims=True)
    out_ref[0:1] = jnp.sum(score_grad * rows_ref[...].astype(f32), axis=0, keepdims=True)
    out_ref[1:2] = attn_ref[...] / attn_gain_ref[...]
    out_ref[2:3] = mlp_ref[...] / mlp_gain_ref[...]


def small_sum(a_ref, b_ref, out_ref):
    out_ref[...] = a_ref[...] + b_ref[...]


def make_local(dp_size, tensor_size):
    dp_bits = [1 << k for k in range(dp_size.bit_length() - 1)]
    far_bits = [1 << k for k in range(2, tensor_size.bit_length() - 1)]
    far = tensor_size // 4
    shards = 2 * far

    def swap(x, axis, bit):
        size = dp_size if axis == "dp" else tensor_size
        return lax.ppermute(x, axis, [(i, i ^ bit) for i in range(size)])

    def near(x):
        return swap(x, "tensor", 2)

    def core(x):
        return swap(x, "tensor", 1)

    def far_spread(piece):
        found = [piece]
        for bit in far_bits:
            found = found + [swap(p, "tensor", bit) for p in found]
        return found[1:]

    def dp_spread(pieces):
        return [p if r == 0 else swap(p, "dp", r) for p in pieces for r in range(dp_size)]

    def paired(arrays):
        return [y for x in arrays for y in (x, core(x))]

    def local(
        tokens,
        routes,
        router_weight,
        attn_gain,
        qkv_weight,
        out_weight,
        mlp_gain,
        up_weight,
        down_weight,
        cotangent,
    ):
        own = routes.shape[1]
        token_count, width = tokens.shape
        heads, head_size = qkv_weight.shape[1:3]
        hidden_own = up_weight.shape[1]
        size = heads * head_size
        hidden = far * hidden_own
        me = lax.axis_index("dp").astype(jnp.int32)[None]
        router = router_weight[None, :]
        attn_gain_row = attn_gain[None, :]
        mlp_gain_row = mlp_gain[None, :]
        places = routes.reshape(1, own)

        count = own // 2
        half = width // 2
        rows_f = struct((own, width), f32)
        rows_l = struct((own, width), low)
        chunk_f = struct((count, width), f32)
        chunk_l = struct((count, width), low)
        group_l = struct((2 * own, width), low)
        line_f = struct((1, width), f32)
        block = 256
        grid = (token_count // block,)
        blocks = pl.BlockSpec((block, width), lambda i: (i, 0))
        steps = Steps()

        def flat(shape):
            return pl.BlockSpec(shape, lambda i: (0,) * len(shape))

        row_block, chunk_block = flat((own, width)), flat((count, width))
        line = flat((1, width))
        place_block = flat((1, own))
        cuts = dp_size * far

        def cut_outs(piece):
            half_cut = struct((cuts // 2, piece, half), low)
            return [struct((2, cuts // 2, piece, half), low), half_cut, half_cut]

        def cut_scratch(piece):
            return [pltpu.VMEM((cuts, piece, half), low)] * 2 + [pltpu.SemaphoreType.DMA((4,))]

        class Fold:
            def __init__(self, keep, *sends):
                self.keep = keep
                self.sent = [swap(x, "dp", bits[0]) for x, bits in zip(sends, (dp_bits, dp_bits[::-1]))]
                self.at = 1

            def step(self, cost=0.0):
                _, count, piece, columns = self.keep.shape
                packed = len(self.sent) == 1
                half = count // 2
                kept = struct((2, half, piece, columns) if half else (2, piece, columns), low)
                at_dp = self.at < len(dp_bits)
                if half and at_dp:
                    outs = [kept] + [struct((half, piece, columns), low)] * 2
                else:
                    outs = [kept] * (2 if half else 1)
                results = steps(partial(fold, packed), outs, [whole] * (1 + len(self.sent)), cost=cost)(self.keep, *self.sent)
                self.keep = results[0]
                if not half:
                    self.pieces = [self.keep if r == 0 else swap(self.keep, "dp", r) for r in range(dp_size)]
                elif at_dp:
                    orders = (dp_bits, dp_bits[::-1])
                    self.sent = [swap(x, "dp", bits[self.at]) for x, bits in zip(results[1:], orders)]
                else:
                    self.sent = [swap(results[1], "tensor", far_bits[::-1][self.at - len(dp_bits)])]
                self.at += 1

            @property
            def left(self):
                return len(dp_bits) + len(far_bits) + 1 - self.at

        attn_piece = 4 * size // dp_size
        mlp_piece = hidden_own // dp_size
        attn_own, attn_cut = steps(
            pack_attn,
            [struct((4, size, width), low), struct((attn_piece, width), low)],
            [scalar, anywhere, anywhere],
            scratch=[pltpu.SemaphoreType.DMA((4 * heads,))],
            vmem=60,
            cost=1.4,
        )(me, qkv_weight, out_weight)
        attn_far = far_spread(attn_cut)
        pick_scratch = [pltpu.VMEM(tokens.shape, low), pltpu.SemaphoreType.DMA((token_count // 256,))]
        rows, rows_a, rows_b = steps(
            pick_tokens, [rows_l, chunk_l, chunk_l], [whole, whole, anywhere], scratch=pick_scratch, vmem=58, cost=4.7
        )(places, attn_gain_row, tokens)
        near_a, near_b = near(rows_a), near(rows_b)
        grad_rows, branch, up_own, up_cut, down_cut = steps(
            pick_grads,
            [rows_l, rows_l, struct((hidden_own, width), low)] + [struct((mlp_piece, width), low)] * 2,
            [scalar] + [whole] * 5 + [anywhere],
            scratch=pick_scratch,
            vmem=52,
            cost=4.6,
        )(me, places, router, rows, up_weight, down_weight, cotangent)
        attn_far = dp_spread(steps.hold(*attn_far))
        near_a, near_b, branch = steps.hold(near_a, near_b, branch)
        up_far = dp_spread(steps.hold(*far_spread(up_cut)))
        branch_near = near(branch)
        attn_far = steps(
            partial(join_attn, dp_size),
            [struct((4, size, width), low)] * (far - 1),
            [scalar] + [whole] * len(attn_far),
            vmem=4,
        )(me, *attn_far)
        attn_held = paired([attn_own, *attn_far])
        head_lines = shards * heads * 2

        def attn_outs(columns):
            return [
                struct((shards, 3 * size, columns), low),
                struct((far, size, columns), low),
                struct((far, size, columns), low),
                struct((head_lines, count), f32),
                chunk_f,
                chunk_l,
            ]

        proj_a, even_a, odd_a, log_a, attn_keep_a, send = steps(
            partial(attn_forward, shards, head_size, 0), attn_outs(own), [whole] * (shards + 2)
        )(*attn_held, rows_a, near_a)
        attn_came_a = near(send)
        proj, attended, attended_odd, log_b, attn_keep_b, send, group_rows = steps(
            partial(attn_forward, shards, head_size, 1), attn_outs(2 * own) + [group_l], [whole] * (shards + 7)
        )(*attn_held, rows_b, near_b, rows_a, near_a, proj_a, even_a, odd_a)
        attn_came_b = near(send)
        up_far = steps(
            partial(join_mlp, dp_size),
            [struct((hidden_own, width), low)] * (far - 1),
            [scalar] + [whole] * len(up_far),
            vmem=4,
        )(me, *up_far)
        (branch_near,) = steps.hold(branch_near)
        down_far = dp_spread(steps.hold(*far_spread(down_cut)))
        attn_sum_a, mid_a = steps(partial(middle, 0), [chunk_f, chunk_l], [whole] * 4)(
            mlp_gain_row, rows, attn_keep_a, attn_came_a
        )
        mid_near_a = near(mid_a)
        attn_sum_b, mid_b = steps(partial(middle, 1), [chunk_f, chunk_l], [whole] * 4)(
            mlp_gain_row, rows, attn_keep_b, attn_came_b
        )
        mid_near_b = near(mid_b)
        up_own, *up_far = steps.hold(up_own, *up_far)
        ups = paired([up_own, *up_far])
        (mid_near_a,) = steps.hold(mid_near_a)
        down_far = steps(
            partial(join_mlp, dp_size),
            [struct((hidden_own, width), low)] * (far - 1),
            [scalar] + [whole] * len(down_far),
            vmem=4,
        )(me, *down_far)
        downs = paired([down_weight, *down_far])
        act = struct((2, hidden, own), low)
        act_a, act_odd_a, mid_keep_a, send, group_branch = steps(
            partial(mlp_main, shards, 0),
            [act, act, chunk_f, chunk_l, group_l],
            [whole] * (2 * shards + 4),
            vmem=12,
        )(*ups, *downs, mid_a, mid_near_a, branch, branch_near)
        mid_came_a = near(send)
        act_b, act_odd_b, mid_keep_b, send, group_mid = steps(
            partial(mlp_main, shards, 1),
            [act, act, chunk_f, chunk_l, group_l],
            [whole] * (2 * shards + 6),
            vmem=12,
        )(*ups, *downs, mid_b, mid_near_b, branch, branch_near, mid_a, mid_near_a)
        mid_came_b = near(send)
        came_a, came_b = core(act_odd_a), core(act_odd_b)
        branch_came, mid_came = core(group_branch), core(group_mid)

        mixed_grad_a, attn_grad_a = steps(partial(middle_back, 0), [chunk_f, chunk_l], [whole] * 7, cost=10)(
            mlp_gain_row, router, rows, grad_rows, attn_sum_a, mid_keep_a, mid_came_a
        )
        grad_near_a = near(attn_grad_a)
        down_fold = Fold(
            *steps(
                partial(mlp_weights, dp_size, far, 0),
                cut_outs(mlp_piece),
                [scalar] + [whole] * 6,
                [anywhere] * 3,
                cut_scratch(mlp_piece),
                )(me, act_a, act_b, came_a, came_b, group_branch, branch_came)
        )
        mixed_grad_b, attn_grad_b = steps(partial(middle_back, 1), [chunk_f, chunk_l], [whole] * 7)(
            mlp_gain_row, router, rows, grad_rows, attn_sum_b, mid_keep_b, mid_came_b
        )
        grad_near_b = near(attn_grad_b)
        (grad_near_a,) = steps.hold(grad_near_a)
        mlp_gain_part, *up_cuts = steps(
            partial(mlp_weights, dp_size, far, 1),
            [line_f] + cut_outs(mlp_piece),
            [scalar] + [whole] * (6 + far),
            [whole] + [anywhere] * 3,
            cut_scratch(mlp_piece),
        )(me, act_a, act_b, came_a, came_b, group_mid, mid_came, *ups[::2])
        up_fold = Fold(*up_cuts)
        mlp_keep, send = steps(partial(mlp_out, shards), [rows_f, rows_l], [whole] * (shards + 4))(
            *downs, act_a, act_odd_a, act_b, act_odd_b
        )
        mlp_came = near(send)

        group_grad, attended_grad = steps(
            partial(attended_back, shards),
            [group_l, struct((shards, size, 2 * own), low)],
            [whole] * (shards + 4),
        )(*attn_held, attn_grad_a, grad_near_a, attn_grad_b, grad_near_b)
        down_fold.step()
        back, back_odd = steps(
            partial(attn_backward, shards, head_size),
            [struct((far, 3 * size, 2 * own), low)] * 2,
            [whole] * 4,
        )(attended_grad, proj, log_a, log_b)
        rows_keep, rows_send = steps(
            partial(attn_rows_back, shards), [rows_f, rows_l], [whole] * (shards + 2)
        )(*attn_held, back, back_odd)
        up_fold.step()
        down_fold.step(40)
        attn_gain_part, *attn_cuts = steps(
            partial(attn_weights, dp_size, far),
            [line_f] + cut_outs(attn_piece),
            [scalar] + [whole] * (far + 8),
            [whole] + [anywhere] * 3,
            [pltpu.VMEM((4, size, width), low)] + cut_scratch(attn_piece),
        )(
            me, *attn_held[::2], back, core(back_odd), attended, core(attended_odd), group_rows, core(group_rows),
            group_grad, core(group_grad),
        )
        attn_fold = Fold(*attn_cuts)
        rows_came = near(rows_send)
        up_fold.step()
        output, branch_sum = steps(
            put_output,
            [struct(tokens.shape, low), rows_f],
            [place_block, line, row_block, chunk_block, chunk_block, row_block, row_block, blocks],
            [blocks, row_block],
            [pltpu.VMEM((own, width), low)],
            grid,
            cost=5,
        )(places, router, rows, attn_sum_a, attn_sum_b, mlp_keep, mlp_came, tokens)
        small_bits = [("dp", bit) for bit in dp_bits] + [("tensor", bit) for bit in [1, 2] + far_bits]

        def small_step(small, k):
            return steps(small_sum, [struct((3, width), f32)], [whole] * 2)(small, swap(small, *small_bits[k]))[0]

        (small,) = steps(small_start, [struct((3, width), f32)], [whole] * 7)(
            attn_gain_row, mlp_gain_row, attn_gain_part, mlp_gain_part, rows, grad_rows, branch_sum
        )
        small = small_step(small, 0)
        down_fold.step()
        small = small_step(small, 1)
        attn_fold.step()
        up_fold.step()
        small = small_step(small, 2)
        (tokens_grad,) = steps(
            put_grads,
            [struct(tokens.shape, low)],
            [place_block, line, line] + [row_block] * 3 + [chunk_block] * 2 + [row_block] * 2 + [blocks],
            [blocks],
            [pltpu.VMEM((own, width), low)],
            grid,
            cost=5,
        )(
            places, router, attn_gain_row, rows, grad_rows, branch_sum, mixed_grad_a, mixed_grad_b, rows_keep, rows_came,
            cotangent,
        )
        attn_fold.step()
        for k in range(3, len(small_bits)):
            small = small_step(small, k)
        while down_fold.left:
            down_fold.step()
        while up_fold.left:
            up_fold.step()
        (down_out,) = steps(
            partial(place_mlp, False), [struct(down_weight.shape, f32)], [scalar] + [whole] * dp_size
        )(me, *down_fold.pieces)
        while attn_fold.left:
            attn_fold.step()
        (up_out,) = steps(
            partial(place_mlp, True),
            [struct(up_weight.shape, f32)],
            [scalar] + [whole] * dp_size,
            scratch=[pltpu.VMEM((hidden_own, width), f32)],
        )(me, *up_fold.pieces)
        qkv_out, out_out = steps(
            place_attn,
            [struct(qkv_weight.shape, f32), struct(out_weight.shape, f32)],
            [scalar] + [whole] * dp_size,
            [anywhere] * 2,
            [pltpu.VMEM((4, size, width), f32), pltpu.SemaphoreType.DMA((4 * heads,))],
        )(me, *attn_fold.pieces)
        return (output, tokens_grad, small[0], small[1], qkv_out, out_out, small[2], up_out, down_out)

    return local


def solution(mesh):
    rows = P(("dp", "tensor"), None)
    heads = P("tensor", None, None)
    return jax.shard_map(
        make_local(mesh.shape["dp"], mesh.shape["tensor"]),
        mesh=mesh,
        in_specs=(
            rows,
            rows,
            P(),
            P(),
            P(None, "tensor", None, None),
            heads,
            P(),
            P(None, "tensor"),
            P("tensor", None),
            rows,
        ),
        out_specs=(
            rows,
            rows,
            P(),
            P(),
            P(None, "tensor", None, None),
            heads,
            P(),
            P(None, "tensor"),
            P("tensor", None),
        ),
        check_vma=False,
    )
```

```python
from functools import partial
from types import SimpleNamespace

import jax
import jax.numpy as jnp
from jax import lax
from jax.experimental import pallas as pl
from jax.experimental.pallas import tpu as pltpu
from jax.sharding import PartitionSpec as P

epsilon = 1e-05
f32 = jnp.float32
low = jnp.bfloat16
MIB = 1 << 20
unit = 1.0e9
gelu_scale = 0.7978845608028654
whole = pl.BlockSpec(memory_space=pltpu.VMEM)
anywhere = pl.BlockSpec(memory_space=pl.ANY)
scalar = pl.BlockSpec(memory_space=pltpu.SMEM)


def nn(a, b):
    return lax.dot_general(a, b, (((1,), (0,)), ((), ())), preferred_element_type=f32)


def nt(a, b):
    return lax.dot_general(a, b, (((1,), (1,)), ((), ())), preferred_element_type=f32)


def tn(a, b):
    return lax.dot_general(a, b, (((0,), (0,)), ((), ())), preferred_element_type=f32)


def inverse_rms(values):
    return lax.rsqrt(jnp.mean(values * values, axis=1, keepdims=True) + epsilon)


def norm_back(values, inverse, gain, upstream):
    unit_rows = values * inverse
    scaled = upstream * gain
    return inverse * (scaled - unit_rows * jnp.mean(scaled * unit_rows, axis=1, keepdims=True))


def score_of(rows, router):
    return jnp.sum(rows * router, axis=1, keepdims=True)


def struct(shape, kind):
    return jax.ShapeDtypeStruct(shape, kind)


class Steps:
    def __init__(self):
        self.token = None
        self.cost = 0

    def __call__(self, body, outs, in_specs, out_specs=None, scratch=(), grid=None, vmem=8):
        count = len(in_specs)
        first = self.token is None
        cost = self.cost

        def run(*refs):
            if first:
                body(*refs[:count], *refs[count + 1 :])
            else:
                body(*refs[1 : count + 1], *refs[count + 2 :])

        kernel = pl.pallas_call(
            run,
            out_shape=[struct((8, 128), f32), *outs],
            in_specs=[*([] if first else [anywhere]), *in_specs],
            out_specs=[anywhere, *([whole] * len(outs) if out_specs is None else out_specs)],
            scratch_shapes=list(scratch),
            grid=() if grid is None else grid,
            compiler_params=pltpu.CompilerParams(vmem_limit_bytes=vmem * MIB),
            cost_estimate=pl.CostEstimate(flops=1 + int(cost * unit), bytes_accessed=1, transcendentals=0),
        )

        def launch(*args):
            self.token, *results = kernel(*([] if first else [self.token]), *args)
            return results

        return launch


    def hold(self, *arrays):
        count = len(arrays)
        cost = self.cost
        kernel = pl.pallas_call(
            lambda *refs: None,
            out_shape=[struct((8, 128), f32)] + [struct(x.shape, x.dtype) for x in arrays],
            in_specs=[anywhere] * (1 + count),
            out_specs=[anywhere] * (1 + count),
            input_output_aliases={1 + k: 1 + k for k in range(count)},
            compiler_params=pltpu.CompilerParams(vmem_limit_bytes=MIB),
            cost_estimate=pl.CostEstimate(flops=1 + int(cost * unit), bytes_accessed=1, transcendentals=0),
        )
        self.token, *arrays = kernel(self.token, *arrays)
        return arrays


def picked(places_ref, source_ref, held_ref, sems, size=256):
    count = places_ref.shape[1]
    parts = source_ref.shape[0] // size
    copies = [
        pltpu.make_async_copy(source_ref.at[pl.ds(k * size, size)], held_ref.at[pl.ds(k * size, size)], sems.at[k])
        for k in range(parts)
    ]
    for c in copies:
        c.start()
    column = jnp.transpose(jnp.broadcast_to(places_ref[...], (128, count)))
    column = jnp.concatenate([column] * (size // 128), axis=1)
    ids = lax.broadcasted_iota(jnp.int32, (count, size), 1)
    total = None
    for k in range(parts):
        copies[k].wait()
        part = nn(jnp.where(column == ids + k * size, 1.0, 0.0).astype(low), held_ref[k * size : (k + 1) * size])
        total = part if total is None else total + part
    return total


def pick_tokens(places_ref, gain_ref, tokens_ref, rows_ref, normed_ref, held_ref, sems):
    rows = picked(places_ref, tokens_ref, held_ref, sems)
    rows_ref[...] = rows.astype(low)
    normed_ref[...] = (rows * inverse_rms(rows) * gain_ref[...]).astype(low)


def pick_grads(
    me_ref, places_ref, router_ref, rows_ref, up_ref, down_ref, grads_ref,
    grad_rows_ref, branch_ref, turned_ref, up_piece_ref, down_piece_ref, held_ref, sems,
):
    grads = picked(places_ref, grads_ref, held_ref, sems)
    score = score_of(rows_ref[...].astype(f32), router_ref[...].astype(f32))
    grad_rows_ref[...] = grads.astype(low)
    branch_ref[...] = (grads * score).astype(low)
    turned_ref[...] = up_ref[...].astype(f32).T.astype(low)
    piece = up_piece_ref.shape[0]
    span = pl.ds(pl.multiple_of(me_ref[0] * piece, piece), piece)
    up_piece_ref[...] = turned_ref[span]
    down_piece_ref[...] = down_ref[span]


def put_back(places_ref, rows_ref, block_ref, out_ref):
    count = places_ref.shape[1]
    size = block_ref.shape[0]
    ids = lax.broadcasted_iota(jnp.int32, (size, count), 0) + pl.program_id(0) * size
    chosen = jnp.where(ids == places_ref[...], 1.0, 0.0)
    listed = jnp.sum(chosen, axis=1, keepdims=True) > 0
    placed = nn(chosen.astype(low), rows_ref[...])
    out_ref[...] = jnp.where(listed, placed, block_ref[...].astype(f32)).astype(low)


def put_output(
    places_ref, router_ref, rows_ref, attn_a_ref, attn_b_ref, keep_ref, came_ref, block_ref, out_ref, sum_ref, new_ref
):
    @pl.when(pl.program_id(0) == 0)
    def _():
        rows = rows_ref[...].astype(f32)
        half = attn_a_ref.shape[0]
        mlp = keep_ref[...] + came_ref[...].astype(f32)
        sum_ref[:half] = attn_a_ref[...] + mlp[:half]
        sum_ref[half:] = attn_b_ref[...] + mlp[half:]
        new_ref[...] = (rows + score_of(rows, router_ref[...].astype(f32)) * sum_ref[...]).astype(low)

    put_back(places_ref, new_ref, block_ref, out_ref)


def put_grads(
    places_ref, router_ref, gain_ref, rows_ref, grads_ref, sum_ref, mixed_a_ref, mixed_b_ref, keep_ref, came_ref,
    block_ref, out_ref, new_ref,
):
    @pl.when(pl.program_id(0) == 0)
    def _():
        rows = rows_ref[...].astype(f32)
        grads = grads_ref[...].astype(f32)
        half = mixed_a_ref.shape[0]
        normed_grad = keep_ref[...] + came_ref[...].astype(f32)
        rows_back = norm_back(rows, inverse_rms(rows), gain_ref[...], normed_grad)
        score_grad = jnp.sum(grads * sum_ref[...], axis=1, keepdims=True)
        total = grads + rows_back + score_grad * router_ref[...].astype(f32)
        new_ref[:half] = (total[:half] + mixed_a_ref[...]).astype(low)
        new_ref[half:] = (total[half:] + mixed_b_ref[...]).astype(low)

    put_back(places_ref, new_ref, block_ref, out_ref)


def middle(chunk, gain_ref, rows_ref, keep_ref, came_ref, attn_ref, normed_ref):
    count = keep_ref.shape[0]
    attn = keep_ref[...] + came_ref[...].astype(f32)
    attn_ref[...] = attn
    mixed = rows_ref[chunk * count : (chunk + 1) * count].astype(f32) + attn
    normed_ref[...] = (mixed * inverse_rms(mixed) * gain_ref[...]).astype(low)


def middle_back(
    chunk, gain_ref, router_ref, rows_ref, grads_ref, attn_ref, keep_ref, came_ref, mixed_grad_ref, attn_grad_ref
):
    count = keep_ref.shape[0]
    span = slice(chunk * count, (chunk + 1) * count)
    rows = rows_ref[span].astype(f32)
    mixed = rows + attn_ref[...]
    mid = keep_ref[...] + came_ref[...].astype(f32)
    mixed_grad = norm_back(mixed, inverse_rms(mixed), gain_ref[...], mid)
    mixed_grad_ref[...] = mixed_grad
    branch = grads_ref[span].astype(f32) * score_of(rows, router_ref[...].astype(f32))
    attn_grad_ref[...] = (branch + mixed_grad).astype(low)


def pack_attn(me_ref, qkv_ref, out_ref, packed_ref, piece_ref, sems):
    _, heads, head_size, _ = qkv_ref.shape
    copies = []
    for h in range(heads):
        span = pl.ds(h * head_size, head_size)
        for c in range(4):
            source = out_ref.at[h] if c == 3 else qkv_ref.at[c, h]
            copies.append(pltpu.make_async_copy(source, packed_ref.at[c, span], sems.at[h * 4 + c]))
    for c in copies:
        c.start()
    for c in copies:
        c.wait()
    piece, rows = piece_ref.shape[0], packed_ref.shape[1]
    part = min(piece, rows)
    for p in range(piece // part):
        place = me_ref[0] * piece + p * part
        inside = pl.ds(pl.multiple_of(lax.rem(place, rows), part), part)
        piece_ref[p * part : (p + 1) * part] = packed_ref[lax.div(place, rows), inside]


def join_attn(dp_size, me_ref, *refs):
    count = len(refs) // (dp_size + 1)
    for f in range(count):
        far_ref = refs[count * dp_size + f]
        rows = far_ref.shape[1]
        for r in range(dp_size):
            piece_ref = refs[f * dp_size + r]
            piece = piece_ref.shape[0]
            part = min(piece, rows)
            for p in range(piece // part):
                place = lax.bitwise_xor(me_ref[0], r) * piece + p * part
                inside = pl.ds(pl.multiple_of(lax.rem(place, rows), part), part)
                far_ref[lax.div(place, rows), inside] = piece_ref[p * part : (p + 1) * part]


def join_mlp(dp_size, me_ref, *refs):
    count = len(refs) // (dp_size + 1)
    for f in range(count):
        far_ref = refs[count * dp_size + f]
        for r in range(dp_size):
            piece_ref = refs[f * dp_size + r]
            piece = piece_ref.shape[0]
            start = pl.multiple_of(lax.bitwise_xor(me_ref[0], r) * piece, piece)
            far_ref[pl.ds(start, piece)] = piece_ref[...]


def logits_of(query, key):
    keys, queries = key.shape[1], query.shape[1]
    shape = (keys, queries)
    allowed = lax.broadcasted_iota(jnp.int32, shape, 0) <= lax.broadcasted_iota(jnp.int32, shape, 1) + (keys - queries)
    return jnp.where(allowed, tn(key, query) * key.shape[0] ** -0.5, -1e30)


def group_rows(own_ref, near_ref, group_ref):
    count = own_ref.shape[0] // 2
    for k in range(4):
        source = near_ref if k % 2 else own_ref
        group_ref[k * count : (k + 1) * count] = source[(k // 2) * count : (k // 2 + 1) * count]


def attend_chunk(weights, rows, first_proj, proj_ref, att_refs, log_ref, base, head_size):
    size = weights[0].shape[1]
    heads = size // head_size
    count = rows.shape[0] // 2
    total = None
    for s, weight in enumerate(weights):
        proj = nt(weight[0:3].reshape(3 * size, -1), rows).astype(low)
        proj_ref[s, :, base : base + 2 * count] = proj
        att_ref = att_refs[s % 2]
        for h in range(heads):
            spans = [slice(c * size + h * head_size, c * size + (h + 1) * head_size) for c in range(3)]
            for q in range(2):
                mine = slice(q * count, (q + 1) * count)
                query, key, value = (proj[span, mine] for span in spans)
                if first_proj is not None:
                    key = jnp.concatenate([first_proj[s, spans[1], mine], key], axis=1)
                    value = jnp.concatenate([first_proj[s, spans[2], mine], value], axis=1)
                logits = logits_of(query, key)
                highest = jnp.max(logits, axis=0, keepdims=True)
                exponent = jnp.exp(logits - highest)
                sums = jnp.sum(exponent, axis=0, keepdims=True)
                probs = (exponent * (1.0 / sums)).astype(low)
                line = (s * heads + h) * 2 + q
                log_ref[line : line + 1] = highest + jnp.log(sums)
                att_ref[s // 2, spans[0], base + q * count : base + (q + 1) * count] = nn(value, probs).astype(low)
        part = tn(att_ref[s // 2, :, base : base + 2 * count], weight[3])
        total = part if total is None else total + part
    return total


def attn_first(head_size, *refs):
    weights, (own_ref, near_ref), refs = refs[:2], refs[2:4], refs[4:]
    total_a, total_b, proj_ref, even_ref, odd_ref, log_a, log_b, group_ref = refs
    count = own_ref.shape[0] // 2
    group_rows(own_ref, near_ref, group_ref)
    atts = (even_ref, odd_ref)
    total_a[...] = attend_chunk(weights, group_ref[: 2 * count], None, proj_ref, atts, log_a, 0, head_size)
    total_b[...] = attend_chunk(weights, group_ref[2 * count :], proj_ref, proj_ref, atts, log_b, 2 * count, head_size)


def attn_rest(count_of, head_size, chunk, *refs):
    weights, (rows_ref, total_ref), refs = refs[:count_of], refs[count_of : count_of + 2], refs[count_of + 2 :]
    first_proj = None
    if chunk:
        first_proj, first_even, first_odd, *refs = refs
    keep_ref, send_ref, proj_ref, even_ref, odd_ref, log_ref = refs
    count = keep_ref.shape[0]
    base = 2 * count * chunk
    if chunk:
        proj_ref[:, :, :base] = first_proj[...]
        even_ref[:, :, :base] = first_even[...]
        odd_ref[:, :, :base] = first_odd[...]
    rows = rows_ref[base : base + 2 * count]
    total = total_ref[...] + attend_chunk(
        weights, rows, first_proj, proj_ref, (even_ref, odd_ref), log_ref, base, head_size
    )
    keep_ref[...] = total[:count]
    send_ref[...] = total[count:].astype(low)


def attended_back(shards, *refs):
    weights, grad_refs, (pack_ref, back_ref) = refs[:shards], refs[shards : shards + 4], refs[shards + 4 :]
    count = grad_refs[0].shape[0]
    for k in range(4):
        pack_ref[k * count : (k + 1) * count] = grad_refs[k][...]
    for s in range(shards):
        back_ref[s] = nt(weights[s][3], pack_ref[...]).astype(low)


def attn_backward(shards, head_size, *refs):
    attended_grad_ref, *groups, even_ref, odd_ref = refs
    size = attended_grad_ref.shape[1]
    heads = size // head_size
    count = groups[0].shape[2] // 4
    scaling = head_size**-0.5
    for s in range(shards):
        proj_ref, log_a_ref, log_b_ref = groups[:3] if s < 2 else groups[3:]
        inner = s if s < 2 else s - 2
        back_ref = odd_ref if s % 2 else even_ref
        for h in range(heads):
            spans = [slice(c * size + h * head_size, c * size + (h + 1) * head_size) for c in range(3)]
            for q in range(2):
                first = slice(q * count, (q + 1) * count)
                second = slice((2 + q) * count, (3 + q) * count)
                line = (inner * heads + h) * 2 + q
                key_a, value_a = (proj_ref[inner, span, first] for span in spans[1:])
                key_grad, value_grad = None, None
                for mine, log_ref in ((second, log_b_ref), (first, log_a_ref)):
                    query = proj_ref[inner, spans[0], mine]
                    upstream = attended_grad_ref[s, spans[0], mine]
                    key, value = key_a, value_a
                    if mine is second:
                        key = jnp.concatenate([key, proj_ref[inner, spans[1], mine]], axis=1)
                        value = jnp.concatenate([value, proj_ref[inner, spans[2], mine]], axis=1)
                    probs = jnp.exp(logits_of(query, key) - log_ref[line : line + 1])
                    weighted = probs * tn(value, upstream)
                    logit_grad = (weighted - probs * jnp.sum(weighted, axis=0, keepdims=True)).astype(low)
                    back_ref[s // 2, spans[0], mine] = (nn(key, logit_grad) * scaling).astype(low)
                    key_part = nt(query, logit_grad)
                    value_part = nt(upstream, probs.astype(low))
                    if mine is second:
                        key_grad, value_grad = key_part[:, :count], value_part[:, :count]
                        back_ref[s // 2, spans[1], mine] = (key_part[:, count:] * scaling).astype(low)
                        back_ref[s // 2, spans[2], mine] = value_part[:, count:].astype(low)
                    else:
                        back_ref[s // 2, spans[1], mine] = ((key_part + key_grad) * scaling).astype(low)
                        back_ref[s // 2, spans[2], mine] = (value_part + value_grad).astype(low)


def split_rows(total, keep_ref, send_ref):
    count = total.shape[0] // 4
    keep_ref[:count] = total[:count]
    keep_ref[count:] = total[2 * count : 3 * count]
    send_ref[:count] = total[count : 2 * count].astype(low)
    send_ref[count:] = total[3 * count :].astype(low)


def attn_rows_back(shards, *refs):
    weights, (even_ref, odd_ref, keep_ref, send_ref) = refs[:shards], refs[shards:]
    size = weights[0].shape[1]
    total = None
    for s in range(shards):
        part = tn((odd_ref if s % 2 else even_ref)[s // 2], weights[s][0:3].reshape(3 * size, -1))
        total = part if total is None else total + part
    split_rows(total, keep_ref, send_ref)


def attn_weights(dp_size, far, *refs):
    me_ref, refs = refs[0], refs[1:]
    weights, refs = refs[:far], refs[far:]
    back_ref, back_came, *atts, rows_ref, rows_came, grad_ref, grad_came, gain_ref, out_a, out_b, out_c, total_ref, cut_a, cut_b, out_sems = refs
    outs = (out_a, out_b, out_c)
    size = weights[0].shape[1]
    half = cut_a.shape[2]
    piece = 4 * size // dp_size
    part = min(piece, size)
    for f in range(far):
        for c in range(4):
            if c == 3:
                att_ref, att_came = atts[:2] if f == 0 else atts[2:]
                g = max(f - 1, 0)
                total = nn(att_ref[g], grad_ref[...]) + nn(att_came[g], grad_came[...])
            else:
                span = slice(c * size, (c + 1) * size)
                total = nn(back_ref[f, span], rows_ref[...]) + nn(back_came[f, span], rows_came[...])
                share = jnp.sum(total * weights[f][c].astype(f32), axis=0, keepdims=True)
                gain_ref[...] = share if f == 0 and c == 0 else gain_ref[...] + share
            total_ref[c] = total.astype(low)
        for a in range(dp_size):
            r = lax.bitwise_xor(me_ref[0], a)
            for p in range(piece // part):
                place = a * piece + p * part
                cut = total_ref[place // size, place % size : place % size + part]
                cut_a[position(r, dp_size, False) * far + f, p * part : (p + 1) * part] = cut[:, :half]
                cut_b[position(r, dp_size, True) * far + f, p * part : (p + 1) * part] = cut[:, half:]
    send_off((cut_a, cut_b), outs, out_sems)


def mlp_main(shards, chunk, *refs):
    ups, downs, refs = refs[:shards], refs[shards : 2 * shards], refs[2 * shards :]
    (own_ref, near_ref, branch_ref), refs = refs[:3], refs[3:]
    if chunk:
        first_rows, first_near, *refs = refs
    even_ref, odd_ref, keep_ref, send_ref, *pack_refs = refs
    count = own_ref.shape[0]
    rows = jnp.concatenate([own_ref[...], near_ref[...]], axis=0)
    branch = branch_ref[2 * chunk * count : 2 * (chunk + 1) * count]
    hidden = ups[0].shape[0]
    step = min(256, hidden)
    total = None
    for s in range(shards):
        act_ref = odd_ref if s % 2 else even_ref
        for f in range(0, hidden, step):
            pre = nt(ups[s][f : f + step], rows)
            upstream = nt(downs[s][f : f + step], branch)
            square = pre * pre
            tanh = jnp.tanh(pre * (gelu_scale + gelu_scale * 0.044715 * square))
            half = 0.5 + 0.5 * tanh
            slope = half + (pre * (0.5 - 0.5 * tanh * tanh)) * (gelu_scale + 3 * gelu_scale * 0.044715 * square)
            at = (s // 2) * hidden + f
            act_ref[0, at : at + step] = (pre * half).astype(low)
            act_ref[1, at : at + step] = (upstream * slope).astype(low)
        part = tn(act_ref[1, (s // 2) * hidden : (s // 2 + 1) * hidden], ups[s][...])
        total = part if total is None else total + part
    keep_ref[...] = total[:count]
    send_ref[...] = total[count:].astype(low)
    if chunk:
        for k, ref in enumerate((first_rows, first_near, own_ref, near_ref)):
            pack_refs[0][k * count : (k + 1) * count] = ref[...]


def mlp_out(shards, *refs):
    weights, (even_a, odd_a, even_b, odd_b, keep_ref, send_ref) = refs[:shards], refs[shards:]
    hidden = weights[0].shape[0]
    count = keep_ref.shape[0] // 2
    for k, (even_ref, odd_ref) in enumerate(((even_a, odd_a), (even_b, odd_b))):
        total = None
        for s in range(shards):
            span = slice((s // 2) * hidden, (s // 2 + 1) * hidden)
            part = tn((odd_ref if s % 2 else even_ref)[0, span], weights[s][...])
            total = part if total is None else total + part
        keep_ref[k * count : (k + 1) * count] = total[:count]
        send_ref[k * count : (k + 1) * count] = total[count:].astype(low)


def mlp_weights(dp_size, far, slot, *refs):
    me_ref, act_a, act_b, came_a, came_b, rows_ref, rows_came, *rest = refs
    if slot:
        weights, (gain_ref, *rest) = rest[:far], rest[far:]
    keep_ref, send_ref, cut_ref, sems = rest
    hidden = act_a.shape[1] // far
    piece = hidden // dp_size
    count = act_a.shape[2]
    for f in range(far):
        for a in range(dp_size):
            r = lax.bitwise_xor(me_ref[0], a)
            b = f * hidden + a * piece
            span = slice(b, b + piece)
            total = nn(act_a[slot, span], rows_ref[:count]) + nn(act_b[slot, span], rows_ref[count:])
            total += nn(came_a[slot, span], rows_came[:count]) + nn(came_b[slot, span], rows_came[count:])
            cut_ref[position(r, dp_size, slot == 1) * far + f] = total.astype(low)
            if slot:
                share = jnp.sum(total * weights[f][a * piece : (a + 1) * piece].astype(f32), axis=0, keepdims=True)
                gain_ref[...] = share if b == 0 else gain_ref[...] + share
    half = cut_ref.shape[0] // 2
    copies = [
        pltpu.make_async_copy(cut_ref.at[pl.ds(k * half, half)], (keep_ref, send_ref)[k], sems.at[k]) for k in range(2)
    ]
    for c in copies:
        c.start()
    for c in copies:
        c.wait()


def position(r, dp_size, swapped):
    if swapped:
        return r
    bits = dp_size.bit_length() - 1
    place = 0
    for k in range(bits):
        place = place + lax.shift_left(lax.bitwise_and(lax.shift_right_logical(r, k), 1), bits - 1 - k)
    return place


def send_off(cuts, outs, sems):
    half = cuts[0].shape[0] // 2
    copies = []
    for k, cut in enumerate(cuts):
        copies.append(pltpu.make_async_copy(cut.at[pl.ds(0, half)], outs[0].at[k], sems.at[2 * k]))
        copies.append(pltpu.make_async_copy(cut.at[pl.ds(half, half)], outs[1 + k], sems.at[2 * k + 1]))
    for c in copies:
        c.start()
    for c in copies:
        c.wait()


def fold(packed, *refs):
    if packed:
        keep_ref, came_ref, *outs = refs
        came = [came_ref.at[k] for k in range(came_ref.shape[0])]
    else:
        keep_ref, *came = refs[:3]
        outs = refs[3:]
    count = keep_ref.shape[1]
    half = count // 2
    for k in range(keep_ref.shape[0]):
        total = keep_ref[k].astype(f32) + came[k][...].astype(f32)
        if half == 0:
            outs[0][k] = total[0].astype(low)
            continue
        outs[0][k] = total[:half].astype(low)
        if len(outs) == 2:
            outs[1][k] = total[half:].astype(low)
        else:
            outs[1 + k][...] = total[half:].astype(low)


def fold_one(keep_ref, came_ref, keep_out, send_out):
    total = keep_ref[...].astype(f32) + came_ref[...].astype(f32)
    half = keep_out.shape[0]
    keep_out[...] = total[:half].astype(low)
    send_out[...] = total[half:].astype(low)


def fold_two(keep_a, came_a, keep_b, came_b, keep_out, send_out):
    half = keep_out.shape[1]
    for k, (keep_ref, came_ref) in enumerate(((keep_a, came_a), (keep_b, came_b))):
        total = keep_ref[...].astype(f32) + came_ref[...].astype(f32)
        keep_out[k] = total[:half].astype(low)
        send_out[k] = total[half:].astype(low)


def fold_end(keep_ref, came_ref, down_ref, up_ref):
    down_ref[...] = (keep_ref[0].astype(f32) + came_ref[0].astype(f32)).astype(low)
    up_ref[...] = (keep_ref[1].astype(f32) + came_ref[1].astype(f32)).astype(low)


def stack_two(down_ref, down_came, up_ref, up_came, down_out, up_out):
    count = down_ref.shape[0]
    down_out[:count] = down_ref[...]
    down_out[count:] = down_came[...]
    up_out[:count] = up_ref[...]
    up_out[count:] = up_came[...]


def place_attn(me_ref, *refs):
    *piece_refs, qkv_ref, out_ref, all_ref, sems = refs
    half, rows = piece_refs[0].shape[2], all_ref.shape[1]
    piece = piece_refs[0].shape[1]
    part = min(piece, rows)
    for r, piece_ref in enumerate(piece_refs):
        start = lax.bitwise_xor(me_ref[0], r) * piece
        for p in range(piece // part):
            place = start + p * part
            inside = pl.ds(pl.multiple_of(lax.rem(place, rows), part), part)
            for k in range(2):
                all_ref[lax.div(place, rows), inside, k * half : (k + 1) * half] = piece_ref[
                    k, p * part : (p + 1) * part
                ].astype(f32)
    _, heads, head_size, _ = qkv_ref.shape
    copies = []
    for h in range(heads):
        span = pl.ds(h * head_size, head_size)
        for c in range(4):
            out = out_ref.at[h] if c == 3 else qkv_ref.at[c, h]
            copies.append(pltpu.make_async_copy(all_ref.at[c, span], out, sems.at[h * 4 + c]))
    for c in copies:
        c.start()
    for c in copies:
        c.wait()


def place_mlp(turn, places, me_ref, *refs):
    *piece_refs, out_ref = refs[:-1] if turn else refs
    target = refs[-1] if turn else out_ref
    piece = piece_refs[0].shape[1]
    for piece_ref, partners in zip(piece_refs, places):
        for k, r in enumerate(partners):
            span = pl.ds(pl.multiple_of(lax.bitwise_xor(me_ref[0], r) * piece, piece), piece)
            target[span] = piece_ref[k].astype(f32)
    if turn:
        out_ref[...] = target[...].T


def small_start(attn_gain_ref, mlp_gain_ref, attn_ref, mlp_ref, rows_ref, grads_ref, sum_ref, out_ref):
    score_grad = jnp.sum(grads_ref[...].astype(f32) * sum_ref[...], axis=1, keepdims=True)
    out_ref[0:1] = jnp.sum(score_grad * rows_ref[...].astype(f32), axis=0, keepdims=True)
    out_ref[1:2] = attn_ref[...] / attn_gain_ref[...]
    out_ref[2:3] = mlp_ref[...] / mlp_gain_ref[...]


def small_sum(*refs):
    total = refs[0][...]
    for ref in refs[1:-1]:
        total = total + ref[...]
    refs[-1][...] = total


def make_local(dp_size, tensor_size):
    dp_bits = [1 << k for k in range(dp_size.bit_length() - 1)]
    far_bits = [1 << k for k in range(2, tensor_size.bit_length() - 1)]
    far = tensor_size // 4
    shards = 2 * far

    def swap(x, axis, bit):
        size = dp_size if axis == "dp" else tensor_size
        return lax.ppermute(x, axis, [(i, i ^ bit) for i in range(size)])

    def near(x):
        return swap(x, "tensor", 2)

    def core(x):
        return swap(x, "tensor", 1)

    def far_spread(piece):
        found = [piece]
        for bit in far_bits:
            found = found + [swap(p, "tensor", bit) for p in found]
        return found[1:]

    def dp_spread(pieces):
        return [p if r == 0 else swap(p, "dp", r) for p in pieces for r in range(dp_size)]

    def paired(arrays):
        return [y for x in arrays for y in (x, core(x))]

    def local(
        tokens,
        routes,
        router_weight,
        attn_gain,
        qkv_weight,
        out_weight,
        mlp_gain,
        up_weight,
        down_weight,
        cotangent,
    ):
        own = routes.shape[1]
        token_count, width = tokens.shape
        heads, head_size = qkv_weight.shape[1:3]
        hidden_own = up_weight.shape[1]
        size = heads * head_size
        hidden = far * hidden_own
        me = lax.axis_index("dp").astype(jnp.int32)[None]
        router = router_weight[None, :]
        attn_gain_row = attn_gain[None, :]
        mlp_gain_row = mlp_gain[None, :]
        places = routes.reshape(1, own)

        count = own // 2
        half = width // 2
        rows_f = struct((own, width), f32)
        rows_l = struct((own, width), low)
        chunk_f = struct((count, width), f32)
        chunk_l = struct((count, width), low)
        group_l = struct((2 * own, width), low)
        line_f = struct((1, width), f32)
        block = 256
        grid = (token_count // block,)
        blocks = pl.BlockSpec((block, width), lambda i: (i, 0))
        steps = Steps()

        def flat(shape):
            return pl.BlockSpec(shape, lambda i: (0,) * len(shape))

        row_block, chunk_block = flat((own, width)), flat((count, width))
        line = flat((1, width))
        place_block = flat((1, own))
        cuts = dp_size * far

        def cut_outs(piece):
            half_cut = struct((cuts // 2, piece, half), low)
            return [struct((2, cuts // 2, piece, half), low), half_cut, half_cut]

        def cut_scratch(piece):
            return [pltpu.VMEM((cuts, piece, half), low)] * 2 + [pltpu.SemaphoreType.DMA((4,))]

        class Fold:
            def __init__(self, keep, sent, at):
                self.keep, self.sent, self.at = keep, sent, at

            def step(self):
                pairs, count, piece, columns = self.keep.shape
                packed = len(self.sent) == 1
                half = count // 2
                kept = struct((pairs, half, piece, columns) if half else (pairs, piece, columns), low)
                at_dp = self.at < len(dp_bits)
                if half and at_dp:
                    outs = [kept] + [struct((half, piece, columns), low)] * 2
                else:
                    outs = [kept] * (2 if half else 1)
                results = steps(partial(fold, packed), outs, [whole] * (1 + len(self.sent)))(self.keep, *self.sent)
                self.keep = results[0]
                if half and at_dp:
                    orders = (dp_bits, dp_bits[::-1])
                    self.sent = [swap(x, "dp", bits[self.at]) for x, bits in zip(results[1:], orders)]
                elif half:
                    self.sent = [swap(results[1], "tensor", far_bits[::-1][self.at - len(dp_bits)])]
                self.at += 1

        attn_piece = 4 * size // dp_size
        mlp_piece = hidden_own // dp_size
        pick_scratch = [pltpu.VMEM(tokens.shape, low), pltpu.SemaphoreType.DMA((token_count // 256,))]
        lines = struct((2 * heads * 2, count), f32)
        act = struct((2, hidden, own), low)
        cut_shape = (cuts, mlp_piece, width)
        half_cut = struct((cuts // 2, mlp_piece, width), low)
        mlp_scratch = [pltpu.VMEM(cut_shape, low), pltpu.SemaphoreType.DMA((2,))]
        quarter = struct((2, far // 2, mlp_piece, width), low)
        down_bits, up_bits = dp_bits, dp_bits[::-1]
        small_bits = [("tensor", bit) for bit in [1, 2] + far_bits] + [("dp", bit) for bit in dp_bits]
        v = SimpleNamespace()

        def rest_outs(columns):
            return [
                chunk_f,
                chunk_l,
                struct((shards - 2, 3 * size, columns), low),
                struct((far - 1, size, columns), low),
                struct((far - 1, size, columns), low),
                struct(((shards - 2) * heads * 2, count), f32),
            ]

        def join(kernel, shape, pieces):
            return steps(
                partial(kernel, dp_size), [struct(shape, low)] * (far - 1), [scalar] + [whole] * len(pieces), vmem=4
            )(me, *pieces)

        def fold_step(keep, came, bit):
            half = struct((keep.shape[0] // 2, *keep.shape[1:]), low)
            keep, send = steps(fold_one, [half] * 2, [whole] * 2)(keep, came)
            return keep, swap(send, "dp", bit)


        def pack():
            v.attn_own, attn_cut = steps(
                pack_attn,
                [struct((4, size, width), low), struct((attn_piece, width), low)],
                [scalar, anywhere, anywhere],
                scratch=[pltpu.SemaphoreType.DMA((4 * heads,))],
                vmem=60,
            )(me, qkv_weight, out_weight)
            v.attn_far = far_spread(attn_cut)

        def tokens_in():
            v.rows, v.normed = steps(
                pick_tokens, [rows_l, rows_l], [whole, whole, anywhere], scratch=pick_scratch, vmem=58
            )(places, attn_gain_row, tokens)
            v.normed_near = near(v.normed)

        def grads_in():
            v.grad_rows, v.branch, v.up_own, up_cut, down_cut = steps(
                pick_grads,
                [rows_l, rows_l, struct((hidden_own, width), low)] + [struct((mlp_piece, width), low)] * 2,
                [scalar] + [whole] * 5 + [anywhere],
                scratch=pick_scratch,
                vmem=52,
            )(me, places, router, v.rows, up_weight, down_weight, cotangent)
            v.up_cut, v.down_cut = far_spread(up_cut), far_spread(down_cut)

        def attn_pieces():
            v.attn_pieces = dp_spread(steps.hold(*v.attn_far))

        def cores():
            v.attn_core, v.down_core = steps.hold(core(v.attn_own), core(down_weight))

        def near_rows():
            (v.normed_near,) = steps.hold(v.normed_near)

        def branch_start():
            (v.branch,) = steps.hold(v.branch)
            v.branch_near = near(v.branch)

        def first():
            v.total_a, v.total_b, v.proj, v.attended, v.attended_odd, v.log_a, v.log_b, v.in_rows = steps(
                partial(attn_first, head_size),
                [rows_f, rows_f, struct((2, 3 * size, 2 * own), low)]
                + [struct((1, size, 2 * own), low)] * 2
                + [lines, lines, group_l],
                [whole] * 4,
            )(v.attn_own, v.attn_core, v.normed, v.normed_near)

        def up_pieces():
            v.up_pieces = dp_spread(steps.hold(*v.up_cut))

        def join_attn_far():
            v.attn_rest = paired(join(join_attn, (4, size, width), v.attn_pieces))

        def rest_a():
            v.attn_keep_a, send, v.proj_a, v.even_a, v.odd_a, v.far_log_a = steps(
                partial(attn_rest, shards - 2, head_size, 0), rest_outs(own), [whole] * shards
            )(*v.attn_rest, v.in_rows, v.total_a)
            v.attn_came_a = near(send)

        def rest_b():
            v.attn_keep_b, send, v.far_proj, v.far_attended, v.far_odd, v.far_log_b = steps(
                partial(attn_rest, shards - 2, head_size, 1), rest_outs(2 * own), [whole] * (shards + 3)
            )(*v.attn_rest, v.in_rows, v.total_b, v.proj_a, v.even_a, v.odd_a)
            v.attn_came_b = near(send)

        def branch_rows():
            (v.group_branch,) = steps(group_rows, [group_l], [whole] * 2)(v.branch, v.branch_near)

        def down_pieces():
            v.down_pieces = dp_spread(steps.hold(*v.down_cut))

        def join_up():
            v.ups = paired(join(join_mlp, (hidden_own, width), v.up_pieces))

        def up_core():
            (v.up_own,) = steps.hold(v.up_own)
            v.ups = [v.up_own, core(v.up_own)] + v.ups

        def join_down():
            v.downs = [down_weight, v.down_core] + paired(join(join_mlp, (hidden_own, width), v.down_pieces))

        def mid_a():
            v.attn_sum_a, v.mid_a = steps(partial(middle, 0), [chunk_f, chunk_l], [whole] * 4)(
                mlp_gain_row, v.rows, v.attn_keep_a, v.attn_came_a
            )
            v.mid_near_a = near(v.mid_a)

        def mid_b():
            v.attn_sum_b, v.mid_b = steps(partial(middle, 1), [chunk_f, chunk_l], [whole] * 4)(
                mlp_gain_row, v.rows, v.attn_keep_b, v.attn_came_b
            )
            v.mid_near_b = near(v.mid_b)

        def mid_near_a():
            (v.mid_near_a,) = steps.hold(v.mid_near_a)

        def share_start():
            kept = steps.hold(v.attended_odd, v.far_odd, v.in_rows, v.group_branch)
            v.attended_odd, v.far_odd, v.in_rows, v.group_branch = kept
            v.shared = [core(x) for x in kept]

        def share_end():
            v.attended_came, v.far_came, v.in_came, v.branch_came = steps.hold(*v.shared)

        def mlp_a():
            v.act_a, v.act_odd_a, v.mid_keep_a, send = steps(
                partial(mlp_main, shards, 0), [act, act, chunk_f, chunk_l], [whole] * (2 * shards + 3), vmem=12
            )(*v.ups, *v.downs, v.mid_a, v.mid_near_a, v.group_branch)
            v.mid_came_a = near(send)

        def mlp_b():
            v.act_b, v.act_odd_b, v.mid_keep_b, send, v.group_mid = steps(
                partial(mlp_main, shards, 1), [act, act, chunk_f, chunk_l, group_l], [whole] * (2 * shards + 5), vmem=12
            )(*v.ups, *v.downs, v.mid_b, v.mid_near_b, v.group_branch, v.mid_a, v.mid_near_a)
            v.mid_came_b = near(send)

        def acts_start():
            v.act_odd_a, v.act_odd_b, v.group_mid = steps.hold(v.act_odd_a, v.act_odd_b, v.group_mid)
            v.came_a, v.came_b, v.mid_came = core(v.act_odd_a), core(v.act_odd_b), core(v.group_mid)

        def back_a():
            v.mixed_grad_a, v.attn_grad_a = steps(partial(middle_back, 0), [chunk_f, chunk_l], [whole] * 7)(
                mlp_gain_row, router, v.rows, v.grad_rows, v.attn_sum_a, v.mid_keep_a, v.mid_came_a
            )
            v.grad_near_a = near(v.attn_grad_a)

        def back_b():
            v.mixed_grad_b, v.attn_grad_b = steps(partial(middle_back, 1), [chunk_f, chunk_l], [whole] * 7)(
                mlp_gain_row, router, v.rows, v.grad_rows, v.attn_sum_b, v.mid_keep_b, v.mid_came_b
            )
            v.grad_near_b = near(v.attn_grad_b)

        def grad_near_a():
            (v.grad_near_a,) = steps.hold(v.grad_near_a)

        def down_weights():
            v.down_keep, send = steps(
                partial(mlp_weights, dp_size, far, 0), [half_cut] * 2, [scalar] + [whole] * 6, [anywhere] * 2, mlp_scratch
            )(me, v.act_a, v.act_b, v.came_a, v.came_b, v.group_branch, v.branch_came)
            v.down_came = swap(send, "dp", down_bits[0])

        def up_weights():
            v.mlp_gain_part, v.up_keep, send = steps(
                partial(mlp_weights, dp_size, far, 1),
                [line_f, half_cut, half_cut],
                [scalar] + [whole] * (6 + far),
                [whole] + [anywhere] * 2,
                mlp_scratch,
            )(me, v.act_a, v.act_b, v.came_a, v.came_b, v.group_mid, v.mid_came, *v.ups[::2])
            v.up_came = swap(send, "dp", up_bits[0])

        def mlp_sums():
            v.mlp_keep, send = steps(partial(mlp_out, shards), [rows_f, rows_l], [whole] * (shards + 4))(
                *v.downs, v.act_a, v.act_odd_a, v.act_b, v.act_odd_b
            )
            v.mlp_came = near(send)

        def attended_grads():
            v.group_grad, v.attended_grad = steps(
                partial(attended_back, shards), [group_l, struct((shards, size, 2 * own), low)], [whole] * (shards + 4)
            )(v.attn_own, v.attn_core, *v.attn_rest, v.attn_grad_a, v.grad_near_a, v.attn_grad_b, v.grad_near_b)
            v.grad_came = core(v.group_grad)

        def attn_grads():
            v.back, v.back_odd = steps(
                partial(attn_backward, shards, head_size), [struct((far, 3 * size, 2 * own), low)] * 2, [whole] * 7
            )(v.attended_grad, v.proj, v.log_a, v.log_b, v.far_proj, v.far_log_a, v.far_log_b)
            v.back_came = core(v.back_odd)

        def grad_shared():
            (v.grad_came,) = steps.hold(v.grad_came)

        def down_fold():
            for bit in down_bits[1:]:
                v.down_keep, v.down_came = fold_step(v.down_keep, v.down_came, bit)

        def up_fold():
            for bit in up_bits[1:]:
                v.up_keep, v.up_came = fold_step(v.up_keep, v.up_came, bit)

        def output_rows():
            v.output, v.branch_sum = steps(
                put_output,
                [struct(tokens.shape, low), rows_f],
                [place_block, line, row_block, chunk_block, chunk_block, row_block, row_block, blocks],
                [blocks, row_block],
                [pltpu.VMEM((own, width), low)],
                grid,
            )(places, router, v.rows, v.attn_sum_a, v.attn_sum_b, v.mlp_keep, v.mlp_came, tokens)

        def attn_weight_grads():
            v.attn_gain_part, keep, *sends = steps(
                partial(attn_weights, dp_size, far),
                [line_f] + cut_outs(attn_piece),
                [scalar] + [whole] * (far + 10),
                [whole] + [anywhere] * 3,
                [pltpu.VMEM((4, size, width), low)] + cut_scratch(attn_piece),
            )(
                me, v.attn_own, *v.attn_rest[::2], v.back, v.back_came, v.attended, v.attended_came, v.far_attended, v.far_came,
                v.in_rows, v.in_came, v.group_grad, v.grad_came,
            )
            v.attn_fold = Fold(keep, [swap(x, "dp", bits[0]) for x, bits in zip(sends, (dp_bits, dp_bits[::-1]))], 1)

        def rows_back():
            v.rows_keep, send = steps(partial(attn_rows_back, shards), [rows_f, rows_l], [whole] * (shards + 2))(
                v.attn_own, v.attn_core, *v.attn_rest, v.back, v.back_odd
            )
            v.rows_came = near(send)

        def small_first():
            (v.small,) = steps(small_start, [struct((3, width), f32)], [whole] * 7)(
                attn_gain_row, mlp_gain_row, v.attn_gain_part, v.mlp_gain_part, v.rows, v.grad_rows, v.branch_sum
            )
            v.hops = 0

        def small_next():
            came = swap(v.small, *small_bits[v.hops])
            (v.small,) = steps(small_sum, [struct((3, width), f32)], [whole] * 2)(v.small, came)
            v.hops += 1

        def mlp_fold():
            keep, send = steps(fold_two, [quarter] * 2, [whole] * 4)(v.down_keep, v.down_came, v.up_keep, v.up_came)
            v.mlp_fold = Fold(keep, [swap(send, "tensor", far_bits[-1])], len(dp_bits) + 1)

        def mlp_end():
            while v.mlp_fold.keep.shape[1] > 1:
                v.mlp_fold.step()
            v.down_piece, v.up_piece = steps(fold_end, [struct((1, mlp_piece, width), low)] * 2, [whole] * 2)(
                v.mlp_fold.keep, *v.mlp_fold.sent
            )
            v.down_parts, v.up_parts = [v.down_piece], [v.up_piece]
            v.down_places, v.up_places = [[0]], [[0]]
            mlp_spread()

        def mlp_spread():
            k = len(v.down_parts) - 1
            if k:
                stacked = struct((1 << k, mlp_piece, width), low)
                v.down_piece, v.up_piece = steps(stack_two, [stacked] * 2, [whole] * 4)(
                    v.down_piece, v.down_parts[-1], v.up_piece, v.up_parts[-1]
                )
            down_bit, up_bit = down_bits[-1 - k], up_bits[-1 - k]
            v.down_places.append([r ^ down_bit for p in v.down_places for r in p])
            v.up_places.append([r ^ up_bit for p in v.up_places for r in p])
            v.down_parts.append(swap(v.down_piece, "dp", down_bit))
            v.up_parts.append(swap(v.up_piece, "dp", up_bit))

        def mlp_spread_rest():
            while len(v.down_parts) <= len(dp_bits):
                mlp_spread()

        def attn_fold_dp():
            v.attn_fold.step()

        def attn_end():
            while v.attn_fold.keep.ndim == 4:
                v.attn_fold.step()
            v.attn_parts = dp_spread([v.attn_fold.keep])

        def down_done():
            (v.down_out,) = steps(
                partial(place_mlp, False, v.down_places),
                [struct(down_weight.shape, f32)],
                [scalar] + [whole] * len(v.down_parts),
            )(me, *v.down_parts)

        def up_done():
            (v.up_out,) = steps(
                partial(place_mlp, True, v.up_places),
                [struct(up_weight.shape, f32)],
                [scalar] + [whole] * len(v.up_parts),
                scratch=[pltpu.VMEM((hidden_own, width), f32)],
            )(me, *v.up_parts)

        def grads_out():
            (v.tokens_grad,) = steps(
                put_grads,
                [struct(tokens.shape, low)],
                [place_block, line, line] + [row_block] * 3 + [chunk_block] * 2 + [row_block] * 2 + [blocks],
                [blocks],
                [pltpu.VMEM((own, width), low)],
                grid,
            )(
                places, router, attn_gain_row, v.rows, v.grad_rows, v.branch_sum, v.mixed_grad_a, v.mixed_grad_b, v.rows_keep,
                v.rows_came, cotangent,
            )

        def attn_done():
            while v.hops < len(small_bits):
                small_next()
            v.qkv_out, v.out_out = steps(
                place_attn,
                [struct(qkv_weight.shape, f32), struct(out_weight.shape, f32)],
                [scalar] + [whole] * dp_size,
                [anywhere] * 2,
                [pltpu.VMEM((4, size, width), f32), pltpu.SemaphoreType.DMA((4 * heads,))],
            )(me, *v.attn_parts)

        for part, cost in (
            (pack, 100),
            (tokens_in, 0),
            (grads_in, 4.6),
            (attn_pieces, 20),
            (cores, 0),
            (first, 1),
            (near_rows, 2),
            (branch_start, 0),
            (down_pieces, 1),
            (up_pieces, 0),
            (join_attn_far, 0),
            (rest_a, 0),
            (rest_b, 0),
            (join_up, 0),
            (mid_a, 0),
            (branch_rows, 20),
            (join_down, 8),
            (mid_b, 0),
            (up_core, 0),
            (mid_near_a, 0.5),
            (share_start, 0),
            (mlp_a, 0),
            (mlp_b, 0),
            (share_end, 0.5),
            (back_a, 0.5),
            (acts_start, 0),
            (up_weights, 0),
            (down_weights, 0),
            (back_b, 0),
            (grad_near_a, 1),
            (mlp_sums, 0),
            (attended_grads, 0),
            (attn_grads, 100),
            (grad_shared, 0),
            (down_fold, 4),
            (up_fold, 0),
            (attn_weight_grads, 0),
            (rows_back, 0),
            (output_rows, 0),
            (mlp_fold, 0),
            (small_first, 0),
            (attn_fold_dp, 0),
            (small_next, 0),
            (grads_out, 0),
            (mlp_end, 0),
            (attn_fold_dp, 0),
            (small_next, 0),
            (mlp_spread_rest, 4),
            (small_next, 0),
            (attn_end, 4),
            (down_done, 0),
            (up_done, 100),
            (attn_done, 0),
        ):
            steps.cost = cost
            part()
        return (
            v.output,
            v.tokens_grad,
            v.small[0],
            v.small[1],
            v.qkv_out,
            v.out_out,
            v.small[2],
            v.up_out,
            v.down_out,
        )

    return local


def solution(mesh):
    rows = P(("dp", "tensor"), None)
    heads = P("tensor", None, None)
    return jax.shard_map(
        make_local(mesh.shape["dp"], mesh.shape["tensor"]),
        mesh=mesh,
        in_specs=(
            rows,
            rows,
            P(),
            P(),
            P(None, "tensor", None, None),
            heads,
            P(),
            P(None, "tensor"),
            P("tensor", None),
            rows,
        ),
        out_specs=(
            rows,
            rows,
            P(),
            P(),
            P(None, "tensor", None, None),
            heads,
            P(),
            P(None, "tensor"),
            P("tensor", None),
        ),
        check_vma=False,
    )
```

```python
from functools import partial
from types import SimpleNamespace

import jax
import jax.numpy as jnp
from jax import lax
from jax.experimental import pallas as pl
from jax.experimental.pallas import tpu as pltpu
from jax.sharding import PartitionSpec as P

epsilon = 1e-05
f32 = jnp.float32
low = jnp.bfloat16
MIB = 1 << 20
unit = 1.0e9
gelu_scale = 0.7978845608028654
whole = pl.BlockSpec(memory_space=pltpu.VMEM)
anywhere = pl.BlockSpec(memory_space=pl.ANY)
scalar = pl.BlockSpec(memory_space=pltpu.SMEM)


def nn(a, b):
    return lax.dot_general(a, b, (((1,), (0,)), ((), ())), preferred_element_type=f32)


def nt(a, b):
    return lax.dot_general(a, b, (((1,), (1,)), ((), ())), preferred_element_type=f32)


def tn(a, b):
    return lax.dot_general(a, b, (((0,), (0,)), ((), ())), preferred_element_type=f32)


def inverse_rms(values):
    return lax.rsqrt(jnp.mean(values * values, axis=1, keepdims=True) + epsilon)


def norm_back(values, inverse, gain, upstream):
    unit_rows = values * inverse
    scaled = upstream * gain
    return inverse * (scaled - unit_rows * jnp.mean(scaled * unit_rows, axis=1, keepdims=True))


def score_of(rows, router):
    return jnp.sum(rows * router, axis=1, keepdims=True)


def struct(shape, kind):
    return jax.ShapeDtypeStruct(shape, kind)


class Steps:
    def __init__(self):
        self.token = None
        self.cost = 0

    def __call__(self, body, outs, in_specs, out_specs=None, scratch=(), grid=None, vmem=8):
        count = len(in_specs)
        first = self.token is None
        cost = self.cost

        def run(*refs):
            if first:
                body(*refs[:count], *refs[count + 1 :])
            else:
                body(*refs[1 : count + 1], *refs[count + 2 :])

        kernel = pl.pallas_call(
            run,
            out_shape=[struct((8, 128), f32), *outs],
            in_specs=[*([] if first else [anywhere]), *in_specs],
            out_specs=[anywhere, *([whole] * len(outs) if out_specs is None else out_specs)],
            scratch_shapes=list(scratch),
            grid=() if grid is None else grid,
            compiler_params=pltpu.CompilerParams(vmem_limit_bytes=vmem * MIB),
            cost_estimate=pl.CostEstimate(flops=1 + int(cost * unit), bytes_accessed=1, transcendentals=0),
        )

        def launch(*args):
            self.token, *results = kernel(*([] if first else [self.token]), *args)
            return results

        return launch


    def hold(self, *arrays):
        count = len(arrays)
        cost = self.cost
        kernel = pl.pallas_call(
            lambda *refs: None,
            out_shape=[struct((8, 128), f32)] + [struct(x.shape, x.dtype) for x in arrays],
            in_specs=[anywhere] * (1 + count),
            out_specs=[anywhere] * (1 + count),
            input_output_aliases={1 + k: 1 + k for k in range(count)},
            compiler_params=pltpu.CompilerParams(vmem_limit_bytes=MIB),
            cost_estimate=pl.CostEstimate(flops=1 + int(cost * unit), bytes_accessed=1, transcendentals=0),
        )
        self.token, *arrays = kernel(self.token, *arrays)
        return arrays


def picked(places_ref, source_ref, held_ref, sems, size=256):
    count = places_ref.shape[1]
    parts = source_ref.shape[0] // size
    copies = [
        pltpu.make_async_copy(source_ref.at[pl.ds(k * size, size)], held_ref.at[pl.ds(k * size, size)], sems.at[k])
        for k in range(parts)
    ]
    for c in copies:
        c.start()
    column = jnp.transpose(jnp.broadcast_to(places_ref[...], (128, count)))
    column = jnp.concatenate([column] * (size // 128), axis=1)
    ids = lax.broadcasted_iota(jnp.int32, (count, size), 1)
    total = None
    for k in range(parts):
        copies[k].wait()
        part = nn(jnp.where(column == ids + k * size, 1.0, 0.0).astype(low), held_ref[k * size : (k + 1) * size])
        total = part if total is None else total + part
    return total


def pick_tokens(places_ref, gain_ref, tokens_ref, rows_ref, normed_ref, held_ref, sems):
    rows = picked(places_ref, tokens_ref, held_ref, sems)
    rows_ref[...] = rows.astype(low)
    normed_ref[...] = (rows * inverse_rms(rows) * gain_ref[...]).astype(low)


def pick_grads(
    me_ref, places_ref, router_ref, rows_ref, up_ref, down_ref, grads_ref,
    grad_rows_ref, branch_ref, turned_ref, up_piece_ref, down_piece_ref, held_ref, sems,
):
    grads = picked(places_ref, grads_ref, held_ref, sems)
    score = score_of(rows_ref[...].astype(f32), router_ref[...].astype(f32))
    grad_rows_ref[...] = grads.astype(low)
    branch_ref[...] = (grads * score).astype(low)
    turned_ref[...] = up_ref[...].astype(f32).T.astype(low)
    piece = up_piece_ref.shape[0]
    span = pl.ds(pl.multiple_of(me_ref[0] * piece, piece), piece)
    up_piece_ref[...] = turned_ref[span]
    down_piece_ref[...] = down_ref[span]


def put_back(places_ref, rows_ref, block_ref, out_ref):
    count = places_ref.shape[1]
    size = block_ref.shape[0]
    ids = lax.broadcasted_iota(jnp.int32, (size, count), 0) + pl.program_id(0) * size
    chosen = jnp.where(ids == places_ref[...], 1.0, 0.0)
    listed = jnp.sum(chosen, axis=1, keepdims=True) > 0
    placed = nn(chosen.astype(low), rows_ref[...])
    out_ref[...] = jnp.where(listed, placed, block_ref[...].astype(f32)).astype(low)


def put_output(
    places_ref, router_ref, rows_ref, attn_a_ref, attn_b_ref, keep_ref, came_ref, block_ref, out_ref, sum_ref, new_ref
):
    @pl.when(pl.program_id(0) == 0)
    def _():
        rows = rows_ref[...].astype(f32)
        half = attn_a_ref.shape[0]
        mlp = keep_ref[...] + came_ref[...].astype(f32)
        sum_ref[:half] = attn_a_ref[...] + mlp[:half]
        sum_ref[half:] = attn_b_ref[...] + mlp[half:]
        new_ref[...] = (rows + score_of(rows, router_ref[...].astype(f32)) * sum_ref[...]).astype(low)

    put_back(places_ref, new_ref, block_ref, out_ref)


def put_grads(
    places_ref, router_ref, gain_ref, rows_ref, grads_ref, sum_ref, mixed_a_ref, mixed_b_ref, keep_ref, came_ref,
    block_ref, out_ref, new_ref,
):
    @pl.when(pl.program_id(0) == 0)
    def _():
        rows = rows_ref[...].astype(f32)
        grads = grads_ref[...].astype(f32)
        half = mixed_a_ref.shape[0]
        normed_grad = keep_ref[...] + came_ref[...].astype(f32)
        rows_back = norm_back(rows, inverse_rms(rows), gain_ref[...], normed_grad)
        score_grad = jnp.sum(grads * sum_ref[...], axis=1, keepdims=True)
        total = grads + rows_back + score_grad * router_ref[...].astype(f32)
        new_ref[:half] = (total[:half] + mixed_a_ref[...]).astype(low)
        new_ref[half:] = (total[half:] + mixed_b_ref[...]).astype(low)

    put_back(places_ref, new_ref, block_ref, out_ref)


def middle(chunk, gain_ref, rows_ref, keep_ref, came_ref, attn_ref, normed_ref):
    count = keep_ref.shape[0]
    attn = keep_ref[...] + came_ref[...].astype(f32)
    attn_ref[...] = attn
    mixed = rows_ref[chunk * count : (chunk + 1) * count].astype(f32) + attn
    normed_ref[...] = (mixed * inverse_rms(mixed) * gain_ref[...]).astype(low)


def middle_back(
    chunk, gain_ref, router_ref, rows_ref, grads_ref, attn_ref, keep_ref, came_ref, mixed_grad_ref, attn_grad_ref
):
    count = keep_ref.shape[0]
    span = slice(chunk * count, (chunk + 1) * count)
    rows = rows_ref[span].astype(f32)
    mixed = rows + attn_ref[...]
    mid = keep_ref[...] + came_ref[...].astype(f32)
    mixed_grad = norm_back(mixed, inverse_rms(mixed), gain_ref[...], mid)
    mixed_grad_ref[...] = mixed_grad
    branch = grads_ref[span].astype(f32) * score_of(rows, router_ref[...].astype(f32))
    attn_grad_ref[...] = (branch + mixed_grad).astype(low)


def pack_attn(me_ref, qkv_ref, out_ref, packed_ref, piece_ref, sems):
    _, heads, head_size, _ = qkv_ref.shape
    copies = []
    for h in range(heads):
        span = pl.ds(h * head_size, head_size)
        for c in range(4):
            source = out_ref.at[h] if c == 3 else qkv_ref.at[c, h]
            copies.append(pltpu.make_async_copy(source, packed_ref.at[c, span], sems.at[h * 4 + c]))
    for c in copies:
        c.start()
    for c in copies:
        c.wait()
    piece, rows = piece_ref.shape[0], packed_ref.shape[1]
    part = min(piece, rows)
    for p in range(piece // part):
        place = me_ref[0] * piece + p * part
        inside = pl.ds(pl.multiple_of(lax.rem(place, rows), part), part)
        piece_ref[p * part : (p + 1) * part] = packed_ref[lax.div(place, rows), inside]


def join_attn(dp_size, me_ref, *refs):
    count = len(refs) // (dp_size + 1)
    for f in range(count):
        far_ref = refs[count * dp_size + f]
        rows = far_ref.shape[1]
        for r in range(dp_size):
            piece_ref = refs[f * dp_size + r]
            piece = piece_ref.shape[0]
            part = min(piece, rows)
            for p in range(piece // part):
                place = lax.bitwise_xor(me_ref[0], r) * piece + p * part
                inside = pl.ds(pl.multiple_of(lax.rem(place, rows), part), part)
                far_ref[lax.div(place, rows), inside] = piece_ref[p * part : (p + 1) * part]


def join_mlp(dp_size, me_ref, *refs):
    count = len(refs) // (dp_size + 1)
    for f in range(count):
        far_ref = refs[count * dp_size + f]
        for r in range(dp_size):
            piece_ref = refs[f * dp_size + r]
            piece = piece_ref.shape[0]
            start = pl.multiple_of(lax.bitwise_xor(me_ref[0], r) * piece, piece)
            far_ref[pl.ds(start, piece)] = piece_ref[...]


def logits_of(query, key):
    keys, queries = key.shape[1], query.shape[1]
    shape = (keys, queries)
    allowed = lax.broadcasted_iota(jnp.int32, shape, 0) <= lax.broadcasted_iota(jnp.int32, shape, 1) + (keys - queries)
    return jnp.where(allowed, tn(key, query) * key.shape[0] ** -0.5, -1e30)


def group_rows(own_ref, near_ref, group_ref):
    count = own_ref.shape[0] // 2
    for k in range(4):
        source = near_ref if k % 2 else own_ref
        group_ref[k * count : (k + 1) * count] = source[(k // 2) * count : (k // 2 + 1) * count]


def attend_chunk(weights, rows, first_proj, proj_ref, att_refs, log_ref, base, head_size):
    size = weights[0].shape[1]
    heads = size // head_size
    count = rows.shape[0] // 2
    total = None
    for s, weight in enumerate(weights):
        proj = nt(weight[0:3].reshape(3 * size, -1), rows).astype(low)
        proj_ref[s, :, base : base + 2 * count] = proj
        att_ref = att_refs[s % 2]
        for h in range(heads):
            spans = [slice(c * size + h * head_size, c * size + (h + 1) * head_size) for c in range(3)]
            for q in range(2):
                mine = slice(q * count, (q + 1) * count)
                query, key, value = (proj[span, mine] for span in spans)
                if first_proj is not None:
                    key = jnp.concatenate([first_proj[s, spans[1], mine], key], axis=1)
                    value = jnp.concatenate([first_proj[s, spans[2], mine], value], axis=1)
                logits = logits_of(query, key)
                highest = jnp.max(logits, axis=0, keepdims=True)
                exponent = jnp.exp(logits - highest)
                sums = jnp.sum(exponent, axis=0, keepdims=True)
                probs = (exponent * (1.0 / sums)).astype(low)
                line = (s * heads + h) * 2 + q
                log_ref[line : line + 1] = highest + jnp.log(sums)
                att_ref[s // 2, spans[0], base + q * count : base + (q + 1) * count] = nn(value, probs).astype(low)
        part = tn(att_ref[s // 2, :, base : base + 2 * count], weight[3])
        total = part if total is None else total + part
    return total


def attn_first(head_size, *refs):
    weights, (own_ref, near_ref), refs = refs[:2], refs[2:4], refs[4:]
    total_a, total_b, proj_ref, even_ref, odd_ref, log_a, log_b, group_ref = refs
    count = own_ref.shape[0] // 2
    group_rows(own_ref, near_ref, group_ref)
    atts = (even_ref, odd_ref)
    total_a[...] = attend_chunk(weights, group_ref[: 2 * count], None, proj_ref, atts, log_a, 0, head_size)
    total_b[...] = attend_chunk(weights, group_ref[2 * count :], proj_ref, proj_ref, atts, log_b, 2 * count, head_size)


def attn_rest(count_of, head_size, chunk, *refs):
    weights, (rows_ref, total_ref), refs = refs[:count_of], refs[count_of : count_of + 2], refs[count_of + 2 :]
    first_proj = None
    if chunk:
        first_proj, first_even, first_odd, *refs = refs
    keep_ref, send_ref, proj_ref, even_ref, odd_ref, log_ref = refs
    count = keep_ref.shape[0]
    base = 2 * count * chunk
    if chunk:
        proj_ref[:, :, :base] = first_proj[...]
        even_ref[:, :, :base] = first_even[...]
        odd_ref[:, :, :base] = first_odd[...]
    rows = rows_ref[base : base + 2 * count]
    total = total_ref[...] + attend_chunk(
        weights, rows, first_proj, proj_ref, (even_ref, odd_ref), log_ref, base, head_size
    )
    keep_ref[...] = total[:count]
    send_ref[...] = total[count:].astype(low)


def attended_back(shards, *refs):
    weights, grad_refs, (pack_ref, back_ref) = refs[:shards], refs[shards : shards + 4], refs[shards + 4 :]
    count = grad_refs[0].shape[0]
    for k in range(4):
        pack_ref[k * count : (k + 1) * count] = grad_refs[k][...]
    for s in range(shards):
        back_ref[s] = nt(weights[s][3], pack_ref[...]).astype(low)


def attn_backward(shards, head_size, *refs):
    attended_grad_ref, *groups, even_ref, odd_ref = refs
    size = attended_grad_ref.shape[1]
    heads = size // head_size
    count = groups[0].shape[2] // 4
    scaling = head_size**-0.5
    for s in range(shards):
        proj_ref, log_a_ref, log_b_ref = groups[:3] if s < 2 else groups[3:]
        inner = s if s < 2 else s - 2
        back_ref = odd_ref if s % 2 else even_ref
        for h in range(heads):
            spans = [slice(c * size + h * head_size, c * size + (h + 1) * head_size) for c in range(3)]
            for q in range(2):
                first = slice(q * count, (q + 1) * count)
                second = slice((2 + q) * count, (3 + q) * count)
                line = (inner * heads + h) * 2 + q
                key_a, value_a = (proj_ref[inner, span, first] for span in spans[1:])
                key_grad, value_grad = None, None
                for mine, log_ref in ((second, log_b_ref), (first, log_a_ref)):
                    query = proj_ref[inner, spans[0], mine]
                    upstream = attended_grad_ref[s, spans[0], mine]
                    key, value = key_a, value_a
                    if mine is second:
                        key = jnp.concatenate([key, proj_ref[inner, spans[1], mine]], axis=1)
                        value = jnp.concatenate([value, proj_ref[inner, spans[2], mine]], axis=1)
                    probs = jnp.exp(logits_of(query, key) - log_ref[line : line + 1])
                    weighted = probs * tn(value, upstream)
                    logit_grad = (weighted - probs * jnp.sum(weighted, axis=0, keepdims=True)).astype(low)
                    back_ref[s // 2, spans[0], mine] = (nn(key, logit_grad) * scaling).astype(low)
                    key_part = nt(query, logit_grad)
                    value_part = nt(upstream, probs.astype(low))
                    if mine is second:
                        key_grad, value_grad = key_part[:, :count], value_part[:, :count]
                        back_ref[s // 2, spans[1], mine] = (key_part[:, count:] * scaling).astype(low)
                        back_ref[s // 2, spans[2], mine] = value_part[:, count:].astype(low)
                    else:
                        back_ref[s // 2, spans[1], mine] = ((key_part + key_grad) * scaling).astype(low)
                        back_ref[s // 2, spans[2], mine] = (value_part + value_grad).astype(low)


def split_rows(total, keep_ref, send_ref):
    count = total.shape[0] // 4
    keep_ref[:count] = total[:count]
    keep_ref[count:] = total[2 * count : 3 * count]
    send_ref[:count] = total[count : 2 * count].astype(low)
    send_ref[count:] = total[3 * count :].astype(low)


def attn_rows_back(shards, *refs):
    weights, (even_ref, odd_ref, keep_ref, send_ref) = refs[:shards], refs[shards:]
    size = weights[0].shape[1]
    total = None
    for s in range(shards):
        part = tn((odd_ref if s % 2 else even_ref)[s // 2], weights[s][0:3].reshape(3 * size, -1))
        total = part if total is None else total + part
    split_rows(total, keep_ref, send_ref)


def attn_weights(dp_size, far, *refs):
    me_ref, refs = refs[0], refs[1:]
    weights, refs = refs[:far], refs[far:]
    back_ref, back_came, *atts, rows_ref, rows_came, grad_ref, grad_came, gain_ref, out_a, out_b, out_c, total_ref, cut_a, cut_b, out_sems = refs
    outs = (out_a, out_b, out_c)
    size = weights[0].shape[1]
    half = cut_a.shape[2]
    piece = 4 * size // dp_size
    part = min(piece, size)
    for f in range(far):
        for c in range(4):
            if c == 3:
                att_ref, att_came = atts[:2] if f == 0 else atts[2:]
                g = max(f - 1, 0)
                total = nn(att_ref[g], grad_ref[...]) + nn(att_came[g], grad_came[...])
            else:
                span = slice(c * size, (c + 1) * size)
                total = nn(back_ref[f, span], rows_ref[...]) + nn(back_came[f, span], rows_came[...])
                share = jnp.sum(total * weights[f][c].astype(f32), axis=0, keepdims=True)
                gain_ref[...] = share if f == 0 and c == 0 else gain_ref[...] + share
            total_ref[c] = total.astype(low)
        for a in range(dp_size):
            r = lax.bitwise_xor(me_ref[0], a)
            for p in range(piece // part):
                place = a * piece + p * part
                cut = total_ref[place // size, place % size : place % size + part]
                cut_a[position(r, dp_size, False) * far + f, p * part : (p + 1) * part] = cut[:, :half]
                cut_b[position(r, dp_size, True) * far + f, p * part : (p + 1) * part] = cut[:, half:]
    send_off((cut_a, cut_b), outs, out_sems)


def mlp_main(shards, chunk, *refs):
    ups, downs, refs = refs[:shards], refs[shards : 2 * shards], refs[2 * shards :]
    (own_ref, near_ref, branch_ref), refs = refs[:3], refs[3:]
    if chunk:
        first_rows, first_near, *refs = refs
    even_ref, odd_ref, keep_ref, send_ref, *pack_refs = refs
    count = own_ref.shape[0]
    rows = jnp.concatenate([own_ref[...], near_ref[...]], axis=0)
    branch = branch_ref[2 * chunk * count : 2 * (chunk + 1) * count]
    hidden = ups[0].shape[0]
    step = min(256, hidden)
    total = None
    for s in range(shards):
        act_ref = odd_ref if s % 2 else even_ref
        for f in range(0, hidden, step):
            pre = nt(ups[s][f : f + step], rows)
            upstream = nt(downs[s][f : f + step], branch)
            square = pre * pre
            tanh = jnp.tanh(pre * (gelu_scale + gelu_scale * 0.044715 * square))
            half = 0.5 + 0.5 * tanh
            slope = half + (pre * (0.5 - 0.5 * tanh * tanh)) * (gelu_scale + 3 * gelu_scale * 0.044715 * square)
            at = (s // 2) * hidden + f
            act_ref[0, at : at + step] = (pre * half).astype(low)
            act_ref[1, at : at + step] = (upstream * slope).astype(low)
        part = tn(act_ref[1, (s // 2) * hidden : (s // 2 + 1) * hidden], ups[s][...])
        total = part if total is None else total + part
    keep_ref[...] = total[:count]
    send_ref[...] = total[count:].astype(low)
    if chunk:
        for k, ref in enumerate((first_rows, first_near, own_ref, near_ref)):
            pack_refs[0][k * count : (k + 1) * count] = ref[...]


def mlp_out(shards, *refs):
    weights, (even_a, odd_a, even_b, odd_b, keep_ref, send_ref) = refs[:shards], refs[shards:]
    hidden = weights[0].shape[0]
    count = keep_ref.shape[0] // 2
    for k, (even_ref, odd_ref) in enumerate(((even_a, odd_a), (even_b, odd_b))):
        total = None
        for s in range(shards):
            span = slice((s // 2) * hidden, (s // 2 + 1) * hidden)
            part = tn((odd_ref if s % 2 else even_ref)[0, span], weights[s][...])
            total = part if total is None else total + part
        keep_ref[k * count : (k + 1) * count] = total[:count]
        send_ref[k * count : (k + 1) * count] = total[count:].astype(low)


def mlp_weights(dp_size, far, slot, *refs):
    me_ref, act_a, act_b, came_a, came_b, rows_ref, rows_came, *rest = refs
    if slot:
        weights, (gain_ref, *rest) = rest[:far], rest[far:]
    keep_ref, send_ref, cut_ref, sems = rest
    hidden = act_a.shape[1] // far
    piece = hidden // dp_size
    count = act_a.shape[2]
    for f in range(far):
        for a in range(dp_size):
            r = lax.bitwise_xor(me_ref[0], a)
            b = f * hidden + a * piece
            span = slice(b, b + piece)
            total = nn(act_a[slot, span], rows_ref[:count]) + nn(act_b[slot, span], rows_ref[count:])
            total += nn(came_a[slot, span], rows_came[:count]) + nn(came_b[slot, span], rows_came[count:])
            cut_ref[position(r, dp_size, slot == 1) * far + f] = total.astype(low)
            if slot:
                share = jnp.sum(total * weights[f][a * piece : (a + 1) * piece].astype(f32), axis=0, keepdims=True)
                gain_ref[...] = share if b == 0 else gain_ref[...] + share
    half = cut_ref.shape[0] // 2
    copies = [
        pltpu.make_async_copy(cut_ref.at[pl.ds(k * half, half)], (keep_ref, send_ref)[k], sems.at[k]) for k in range(2)
    ]
    for c in copies:
        c.start()
    for c in copies:
        c.wait()


def position(r, dp_size, swapped):
    if swapped:
        return r
    bits = dp_size.bit_length() - 1
    place = 0
    for k in range(bits):
        place = place + lax.shift_left(lax.bitwise_and(lax.shift_right_logical(r, k), 1), bits - 1 - k)
    return place


def send_off(cuts, outs, sems):
    half = cuts[0].shape[0] // 2
    copies = []
    for k, cut in enumerate(cuts):
        copies.append(pltpu.make_async_copy(cut.at[pl.ds(0, half)], outs[0].at[k], sems.at[2 * k]))
        copies.append(pltpu.make_async_copy(cut.at[pl.ds(half, half)], outs[1 + k], sems.at[2 * k + 1]))
    for c in copies:
        c.start()
    for c in copies:
        c.wait()


def fold(packed, *refs):
    if packed:
        keep_ref, came_ref, *outs = refs
        came = [came_ref.at[k] for k in range(came_ref.shape[0])]
    else:
        keep_ref, *came = refs[:3]
        outs = refs[3:]
    count = keep_ref.shape[1]
    half = count // 2
    for k in range(keep_ref.shape[0]):
        total = keep_ref[k].astype(f32) + came[k][...].astype(f32)
        if half == 0:
            outs[0][k] = total[0].astype(low)
            continue
        outs[0][k] = total[:half].astype(low)
        if len(outs) == 2:
            outs[1][k] = total[half:].astype(low)
        else:
            outs[1 + k][...] = total[half:].astype(low)


def fold_one(keep_ref, came_ref, keep_out, send_out):
    total = keep_ref[...].astype(f32) + came_ref[...].astype(f32)
    half = keep_out.shape[0]
    keep_out[...] = total[:half].astype(low)
    send_out[...] = total[half:].astype(low)


def fold_two(keep_a, came_a, keep_b, came_b, keep_out, send_out):
    half = keep_out.shape[1]
    for k, (keep_ref, came_ref) in enumerate(((keep_a, came_a), (keep_b, came_b))):
        total = keep_ref[...].astype(f32) + came_ref[...].astype(f32)
        keep_out[k] = total[:half].astype(low)
        send_out[k] = total[half:].astype(low)


def fold_end(keep_ref, came_ref, down_ref, up_ref):
    down_ref[...] = (keep_ref[0].astype(f32) + came_ref[0].astype(f32)).astype(low)
    up_ref[...] = (keep_ref[1].astype(f32) + came_ref[1].astype(f32)).astype(low)


def stack_two(down_ref, down_came, up_ref, up_came, down_out, up_out):
    count = down_ref.shape[0]
    down_out[:count] = down_ref[...]
    down_out[count:] = down_came[...]
    up_out[:count] = up_ref[...]
    up_out[count:] = up_came[...]


def place_attn(me_ref, *refs):
    *piece_refs, qkv_ref, out_ref, all_ref, sems = refs
    half, rows = piece_refs[0].shape[2], all_ref.shape[1]
    piece = piece_refs[0].shape[1]
    part = min(piece, rows)
    for r, piece_ref in enumerate(piece_refs):
        start = lax.bitwise_xor(me_ref[0], r) * piece
        for p in range(piece // part):
            place = start + p * part
            inside = pl.ds(pl.multiple_of(lax.rem(place, rows), part), part)
            for k in range(2):
                all_ref[lax.div(place, rows), inside, k * half : (k + 1) * half] = piece_ref[
                    k, p * part : (p + 1) * part
                ].astype(f32)
    _, heads, head_size, _ = qkv_ref.shape
    copies = []
    for h in range(heads):
        span = pl.ds(h * head_size, head_size)
        for c in range(4):
            out = out_ref.at[h] if c == 3 else qkv_ref.at[c, h]
            copies.append(pltpu.make_async_copy(all_ref.at[c, span], out, sems.at[h * 4 + c]))
    for c in copies:
        c.start()
    for c in copies:
        c.wait()


def place_mlp(turn, places, me_ref, *refs):
    *piece_refs, out_ref = refs[:-1] if turn else refs
    target = refs[-1] if turn else out_ref
    piece = piece_refs[0].shape[1]
    for piece_ref, partners in zip(piece_refs, places):
        for k, r in enumerate(partners):
            span = pl.ds(pl.multiple_of(lax.bitwise_xor(me_ref[0], r) * piece, piece), piece)
            target[span] = piece_ref[k].astype(f32)
    if turn:
        out_ref[...] = target[...].T


def small_start(attn_gain_ref, mlp_gain_ref, attn_ref, mlp_ref, rows_ref, grads_ref, sum_ref, out_ref):
    score_grad = jnp.sum(grads_ref[...].astype(f32) * sum_ref[...], axis=1, keepdims=True)
    out_ref[0:1] = jnp.sum(score_grad * rows_ref[...].astype(f32), axis=0, keepdims=True)
    out_ref[1:2] = attn_ref[...] / attn_gain_ref[...]
    out_ref[2:3] = mlp_ref[...] / mlp_gain_ref[...]


def small_sum(*refs):
    total = refs[0][...]
    for ref in refs[1:-1]:
        total = total + ref[...]
    refs[-1][...] = total


def make_local(dp_size, tensor_size):
    dp_bits = [1 << k for k in range(dp_size.bit_length() - 1)]
    far_bits = [1 << k for k in range(2, tensor_size.bit_length() - 1)]
    far = tensor_size // 4
    shards = 2 * far

    def swap(x, axis, bit):
        size = dp_size if axis == "dp" else tensor_size
        return lax.ppermute(x, axis, [(i, i ^ bit) for i in range(size)])

    def near(x):
        return swap(x, "tensor", 2)

    def core(x):
        return swap(x, "tensor", 1)

    def far_spread(piece):
        found = [piece]
        for bit in far_bits:
            found = found + [swap(p, "tensor", bit) for p in found]
        return found[1:]

    def dp_spread(pieces):
        return [p if r == 0 else swap(p, "dp", r) for p in pieces for r in range(dp_size)]

    def paired(arrays):
        return [y for x in arrays for y in (x, core(x))]

    def local(
        tokens,
        routes,
        router_weight,
        attn_gain,
        qkv_weight,
        out_weight,
        mlp_gain,
        up_weight,
        down_weight,
        cotangent,
    ):
        own = routes.shape[1]
        token_count, width = tokens.shape
        heads, head_size = qkv_weight.shape[1:3]
        hidden_own = up_weight.shape[1]
        size = heads * head_size
        hidden = far * hidden_own
        me = lax.axis_index("dp").astype(jnp.int32)[None]
        router = router_weight[None, :]
        attn_gain_row = attn_gain[None, :]
        mlp_gain_row = mlp_gain[None, :]
        places = routes.reshape(1, own)

        count = own // 2
        half = width // 2
        rows_f = struct((own, width), f32)
        rows_l = struct((own, width), low)
        chunk_f = struct((count, width), f32)
        chunk_l = struct((count, width), low)
        group_l = struct((2 * own, width), low)
        line_f = struct((1, width), f32)
        block = 256
        grid = (token_count // block,)
        blocks = pl.BlockSpec((block, width), lambda i: (i, 0))
        steps = Steps()

        def flat(shape):
            return pl.BlockSpec(shape, lambda i: (0,) * len(shape))

        row_block, chunk_block = flat((own, width)), flat((count, width))
        line = flat((1, width))
        place_block = flat((1, own))
        cuts = dp_size * far

        def cut_outs(piece):
            half_cut = struct((cuts // 2, piece, half), low)
            return [struct((2, cuts // 2, piece, half), low), half_cut, half_cut]

        def cut_scratch(piece):
            return [pltpu.VMEM((cuts, piece, half), low)] * 2 + [pltpu.SemaphoreType.DMA((4,))]

        class Fold:
            def __init__(self, keep, sent, at):
                self.keep, self.sent, self.at = keep, sent, at

            def step(self):
                pairs, count, piece, columns = self.keep.shape
                packed = len(self.sent) == 1
                half = count // 2
                kept = struct((pairs, half, piece, columns) if half else (pairs, piece, columns), low)
                at_dp = self.at < len(dp_bits)
                if half and at_dp:
                    outs = [kept] + [struct((half, piece, columns), low)] * 2
                else:
                    outs = [kept] * (2 if half else 1)
                results = steps(partial(fold, packed), outs, [whole] * (1 + len(self.sent)))(self.keep, *self.sent)
                self.keep = results[0]
                if half and at_dp:
                    orders = (dp_bits, dp_bits[::-1])
                    self.sent = [swap(x, "dp", bits[self.at]) for x, bits in zip(results[1:], orders)]
                elif half:
                    self.sent = [swap(results[1], "tensor", far_bits[::-1][self.at - len(dp_bits)])]
                self.at += 1

        attn_piece = 4 * size // dp_size
        mlp_piece = hidden_own // dp_size
        pick_scratch = [pltpu.VMEM(tokens.shape, low), pltpu.SemaphoreType.DMA((token_count // 256,))]
        lines = struct((2 * heads * 2, count), f32)
        act = struct((2, hidden, own), low)
        cut_shape = (cuts, mlp_piece, width)
        half_cut = struct((cuts // 2, mlp_piece, width), low)
        mlp_scratch = [pltpu.VMEM(cut_shape, low), pltpu.SemaphoreType.DMA((2,))]
        quarter = struct((2, far // 2, mlp_piece, width), low)
        down_bits, up_bits = dp_bits, dp_bits[::-1]
        small_bits = [("tensor", bit) for bit in [1, 2] + far_bits] + [("dp", bit) for bit in dp_bits]
        v = SimpleNamespace()

        def rest_outs(columns):
            return [
                chunk_f,
                chunk_l,
                struct((shards - 2, 3 * size, columns), low),
                struct((far - 1, size, columns), low),
                struct((far - 1, size, columns), low),
                struct(((shards - 2) * heads * 2, count), f32),
            ]

        def join(kernel, shape, pieces):
            return steps(
                partial(kernel, dp_size), [struct(shape, low)] * (far - 1), [scalar] + [whole] * len(pieces), vmem=4
            )(me, *pieces)

        def fold_step(keep, came, bit):
            half = struct((keep.shape[0] // 2, *keep.shape[1:]), low)
            keep, send = steps(fold_one, [half] * 2, [whole] * 2)(keep, came)
            return keep, swap(send, "dp", bit)


        def pack():
            v.attn_own, attn_cut = steps(
                pack_attn,
                [struct((4, size, width), low), struct((attn_piece, width), low)],
                [scalar, anywhere, anywhere],
                scratch=[pltpu.SemaphoreType.DMA((4 * heads,))],
                vmem=60,
            )(me, qkv_weight, out_weight)
            v.attn_far = far_spread(attn_cut)

        def tokens_in():
            v.rows, v.normed = steps(
                pick_tokens, [rows_l, rows_l], [whole, whole, anywhere], scratch=pick_scratch, vmem=58
            )(places, attn_gain_row, tokens)
            v.normed_near = near(v.normed)

        def grads_in():
            v.grad_rows, v.branch, v.up_own, up_cut, down_cut = steps(
                pick_grads,
                [rows_l, rows_l, struct((hidden_own, width), low)] + [struct((mlp_piece, width), low)] * 2,
                [scalar] + [whole] * 5 + [anywhere],
                scratch=pick_scratch,
                vmem=52,
            )(me, places, router, v.rows, up_weight, down_weight, cotangent)
            v.up_cut, v.down_cut = far_spread(up_cut), far_spread(down_cut)

        def attn_pieces():
            v.attn_pieces = dp_spread(steps.hold(*v.attn_far))

        def cores():
            v.attn_core, v.down_core = steps.hold(core(v.attn_own), core(down_weight))

        def near_rows():
            (v.normed_near,) = steps.hold(v.normed_near)

        def branch_start():
            (v.branch,) = steps.hold(v.branch)
            v.branch_near = near(v.branch)

        def first():
            v.total_a, v.total_b, v.proj, v.attended, v.attended_odd, v.log_a, v.log_b, v.in_rows = steps(
                partial(attn_first, head_size),
                [rows_f, rows_f, struct((2, 3 * size, 2 * own), low)]
                + [struct((1, size, 2 * own), low)] * 2
                + [lines, lines, group_l],
                [whole] * 4,
            )(v.attn_own, v.attn_core, v.normed, v.normed_near)

        def up_pieces():
            v.up_pieces = dp_spread(steps.hold(*v.up_cut))

        def join_attn_far():
            v.attn_rest = paired(join(join_attn, (4, size, width), v.attn_pieces))

        def rest_a():
            v.attn_keep_a, send, v.proj_a, v.even_a, v.odd_a, v.far_log_a = steps(
                partial(attn_rest, shards - 2, head_size, 0), rest_outs(own), [whole] * shards
            )(*v.attn_rest, v.in_rows, v.total_a)
            v.attn_came_a = near(send)

        def rest_b():
            v.attn_keep_b, send, v.far_proj, v.far_attended, v.far_odd, v.far_log_b = steps(
                partial(attn_rest, shards - 2, head_size, 1), rest_outs(2 * own), [whole] * (shards + 3)
            )(*v.attn_rest, v.in_rows, v.total_b, v.proj_a, v.even_a, v.odd_a)
            v.attn_came_b = near(send)

        def branch_rows():
            (v.group_branch,) = steps(group_rows, [group_l], [whole] * 2)(v.branch, v.branch_near)

        def down_pieces():
            v.down_pieces = dp_spread(steps.hold(*v.down_cut))

        def join_up():
            v.ups = paired(join(join_mlp, (hidden_own, width), v.up_pieces))

        def up_core():
            (v.up_own,) = steps.hold(v.up_own)
            v.ups = [v.up_own, core(v.up_own)] + v.ups

        def join_down():
            v.downs = [down_weight, v.down_core] + paired(join(join_mlp, (hidden_own, width), v.down_pieces))

        def mid_a():
            v.attn_sum_a, v.mid_a = steps(partial(middle, 0), [chunk_f, chunk_l], [whole] * 4)(
                mlp_gain_row, v.rows, v.attn_keep_a, v.attn_came_a
            )
            v.mid_near_a = near(v.mid_a)

        def mid_b():
            v.attn_sum_b, v.mid_b = steps(partial(middle, 1), [chunk_f, chunk_l], [whole] * 4)(
                mlp_gain_row, v.rows, v.attn_keep_b, v.attn_came_b
            )
            v.mid_near_b = near(v.mid_b)

        def mid_near_a():
            (v.mid_near_a,) = steps.hold(v.mid_near_a)

        def share_start():
            kept = steps.hold(v.attended_odd, v.far_odd, v.in_rows, v.group_branch)
            v.attended_odd, v.far_odd, v.in_rows, v.group_branch = kept
            v.shared = [core(x) for x in kept]

        def share_end():
            v.attended_came, v.far_came, v.in_came, v.branch_came = steps.hold(*v.shared)

        def mlp_a():
            v.act_a, v.act_odd_a, v.mid_keep_a, send = steps(
                partial(mlp_main, shards, 0), [act, act, chunk_f, chunk_l], [whole] * (2 * shards + 3), vmem=12
            )(*v.ups, *v.downs, v.mid_a, v.mid_near_a, v.group_branch)
            v.mid_came_a = near(send)

        def mlp_b():
            v.act_b, v.act_odd_b, v.mid_keep_b, send, v.group_mid = steps(
                partial(mlp_main, shards, 1), [act, act, chunk_f, chunk_l, group_l], [whole] * (2 * shards + 5), vmem=12
            )(*v.ups, *v.downs, v.mid_b, v.mid_near_b, v.group_branch, v.mid_a, v.mid_near_a)
            v.mid_came_b = near(send)

        def acts_start():
            v.act_odd_a, v.act_odd_b, v.group_mid = steps.hold(v.act_odd_a, v.act_odd_b, v.group_mid)
            v.came_a, v.came_b, v.mid_came = core(v.act_odd_a), core(v.act_odd_b), core(v.group_mid)

        def back_a():
            v.mixed_grad_a, v.attn_grad_a = steps(partial(middle_back, 0), [chunk_f, chunk_l], [whole] * 7)(
                mlp_gain_row, router, v.rows, v.grad_rows, v.attn_sum_a, v.mid_keep_a, v.mid_came_a
            )
            v.grad_near_a = near(v.attn_grad_a)

        def back_b():
            v.mixed_grad_b, v.attn_grad_b = steps(partial(middle_back, 1), [chunk_f, chunk_l], [whole] * 7)(
                mlp_gain_row, router, v.rows, v.grad_rows, v.attn_sum_b, v.mid_keep_b, v.mid_came_b
            )
            v.grad_near_b = near(v.attn_grad_b)

        def grad_near_a():
            (v.grad_near_a,) = steps.hold(v.grad_near_a)

        def down_weights():
            v.down_keep, send = steps(
                partial(mlp_weights, dp_size, far, 0), [half_cut] * 2, [scalar] + [whole] * 6, [anywhere] * 2, mlp_scratch
            )(me, v.act_a, v.act_b, v.came_a, v.came_b, v.group_branch, v.branch_came)
            v.down_came = swap(send, "dp", down_bits[0])

        def up_weights():
            v.mlp_gain_part, v.up_keep, send = steps(
                partial(mlp_weights, dp_size, far, 1),
                [line_f, half_cut, half_cut],
                [scalar] + [whole] * (6 + far),
                [whole] + [anywhere] * 2,
                mlp_scratch,
            )(me, v.act_a, v.act_b, v.came_a, v.came_b, v.group_mid, v.mid_came, *v.ups[::2])
            v.up_came = swap(send, "dp", up_bits[0])

        def mlp_sums():
            v.mlp_keep, send = steps(partial(mlp_out, shards), [rows_f, rows_l], [whole] * (shards + 4))(
                *v.downs, v.act_a, v.act_odd_a, v.act_b, v.act_odd_b
            )
            v.mlp_came = near(send)

        def attended_grads():
            v.group_grad, v.attended_grad = steps(
                partial(attended_back, shards), [group_l, struct((shards, size, 2 * own), low)], [whole] * (shards + 4)
            )(v.attn_own, v.attn_core, *v.attn_rest, v.attn_grad_a, v.grad_near_a, v.attn_grad_b, v.grad_near_b)
            v.grad_came = core(v.group_grad)

        def attn_grads():
            v.back, v.back_odd = steps(
                partial(attn_backward, shards, head_size), [struct((far, 3 * size, 2 * own), low)] * 2, [whole] * 7
            )(v.attended_grad, v.proj, v.log_a, v.log_b, v.far_proj, v.far_log_a, v.far_log_b)
            v.back_came = core(v.back_odd)

        def grad_shared():
            (v.grad_came,) = steps.hold(v.grad_came)

        def down_fold():
            for bit in down_bits[1:]:
                v.down_keep, v.down_came = fold_step(v.down_keep, v.down_came, bit)

        def up_fold():
            for bit in up_bits[1:]:
                v.up_keep, v.up_came = fold_step(v.up_keep, v.up_came, bit)

        def output_rows():
            v.output, v.branch_sum = steps(
                put_output,
                [struct(tokens.shape, low), rows_f],
                [place_block, line, row_block, chunk_block, chunk_block, row_block, row_block, blocks],
                [blocks, row_block],
                [pltpu.VMEM((own, width), low)],
                grid,
            )(places, router, v.rows, v.attn_sum_a, v.attn_sum_b, v.mlp_keep, v.mlp_came, tokens)

        def attn_weight_grads():
            v.attn_gain_part, keep, *sends = steps(
                partial(attn_weights, dp_size, far),
                [line_f] + cut_outs(attn_piece),
                [scalar] + [whole] * (far + 10),
                [whole] + [anywhere] * 3,
                [pltpu.VMEM((4, size, width), low)] + cut_scratch(attn_piece),
            )(
                me, v.attn_own, *v.attn_rest[::2], v.back, v.back_came, v.attended, v.attended_came, v.far_attended, v.far_came,
                v.in_rows, v.in_came, v.group_grad, v.grad_came,
            )
            v.attn_fold = Fold(keep, [swap(x, "dp", bits[0]) for x, bits in zip(sends, (dp_bits, dp_bits[::-1]))], 1)

        def rows_back():
            v.rows_keep, send = steps(partial(attn_rows_back, shards), [rows_f, rows_l], [whole] * (shards + 2))(
                v.attn_own, v.attn_core, *v.attn_rest, v.back, v.back_odd
            )
            v.rows_came = near(send)

        def small_first():
            (v.small,) = steps(small_start, [struct((3, width), f32)], [whole] * 7)(
                attn_gain_row, mlp_gain_row, v.attn_gain_part, v.mlp_gain_part, v.rows, v.grad_rows, v.branch_sum
            )
            v.hops = 0

        def small_next():
            came = swap(v.small, *small_bits[v.hops])
            (v.small,) = steps(small_sum, [struct((3, width), f32)], [whole] * 2)(v.small, came)
            v.hops += 1

        def mlp_fold():
            keep, send = steps(fold_two, [quarter] * 2, [whole] * 4)(v.down_keep, v.down_came, v.up_keep, v.up_came)
            v.mlp_fold = Fold(keep, [swap(send, "tensor", far_bits[-1])], len(dp_bits) + 1)

        def mlp_end():
            while v.mlp_fold.keep.shape[1] > 1:
                v.mlp_fold.step()
            v.down_piece, v.up_piece = steps(fold_end, [struct((1, mlp_piece, width), low)] * 2, [whole] * 2)(
                v.mlp_fold.keep, *v.mlp_fold.sent
            )
            v.down_parts, v.up_parts = [v.down_piece], [v.up_piece]
            v.down_places, v.up_places = [[0]], [[0]]
            mlp_spread()

        def mlp_spread():
            k = len(v.down_parts) - 1
            if k:
                stacked = struct((1 << k, mlp_piece, width), low)
                v.down_piece, v.up_piece = steps(stack_two, [stacked] * 2, [whole] * 4)(
                    v.down_piece, v.down_parts[-1], v.up_piece, v.up_parts[-1]
                )
            down_bit, up_bit = down_bits[-1 - k], up_bits[-1 - k]
            v.down_places.append([r ^ down_bit for p in v.down_places for r in p])
            v.up_places.append([r ^ up_bit for p in v.up_places for r in p])
            v.down_parts.append(swap(v.down_piece, "dp", down_bit))
            v.up_parts.append(swap(v.up_piece, "dp", up_bit))

        def mlp_spread_rest():
            while len(v.down_parts) <= len(dp_bits):
                mlp_spread()

        def attn_fold_dp():
            v.attn_fold.step()

        def attn_end():
            while v.attn_fold.keep.ndim == 4:
                v.attn_fold.step()
            v.attn_parts = dp_spread([v.attn_fold.keep])

        def down_done():
            (v.down_out,) = steps(
                partial(place_mlp, False, v.down_places),
                [struct(down_weight.shape, f32)],
                [scalar] + [whole] * len(v.down_parts),
            )(me, *v.down_parts)

        def up_done():
            (v.up_out,) = steps(
                partial(place_mlp, True, v.up_places),
                [struct(up_weight.shape, f32)],
                [scalar] + [whole] * len(v.up_parts),
                scratch=[pltpu.VMEM((hidden_own, width), f32)],
            )(me, *v.up_parts)

        def grads_out():
            (v.tokens_grad,) = steps(
                put_grads,
                [struct(tokens.shape, low)],
                [place_block, line, line] + [row_block] * 3 + [chunk_block] * 2 + [row_block] * 2 + [blocks],
                [blocks],
                [pltpu.VMEM((own, width), low)],
                grid,
            )(
                places, router, attn_gain_row, v.rows, v.grad_rows, v.branch_sum, v.mixed_grad_a, v.mixed_grad_b, v.rows_keep,
                v.rows_came, cotangent,
            )

        def attn_done():
            while v.hops < len(small_bits):
                small_next()
            v.qkv_out, v.out_out = steps(
                place_attn,
                [struct(qkv_weight.shape, f32), struct(out_weight.shape, f32)],
                [scalar] + [whole] * dp_size,
                [anywhere] * 2,
                [pltpu.VMEM((4, size, width), f32), pltpu.SemaphoreType.DMA((4 * heads,))],
            )(me, *v.attn_parts)

        for part, cost in (
            (pack, 100),
            (tokens_in, 0),
            (grads_in, 20),
            (attn_pieces, 20),
            (cores, 0),
            (first, 4),
            (near_rows, 2),
            (down_pieces, 1),
            (branch_start, 20),
            (up_pieces, 2),
            (join_attn_far, 0),
            (rest_a, 0),
            (rest_b, 0),
            (join_up, 0),
            (mid_a, 0),
            (branch_rows, 4),
            (join_down, 8),
            (mid_b, 8),
            (up_core, 0),
            (mid_near_a, 0.5),
            (share_start, 0),
            (mlp_a, 0),
            (mlp_b, 0),
            (share_end, 0.5),
            (back_a, 0.5),
            (acts_start, 0),
            (up_weights, 0),
            (down_weights, 0),
            (back_b, 8),
            (grad_near_a, 1),
            (mlp_sums, 0),
            (attended_grads, 0),
            (attn_grads, 2),
            (down_fold, 4),
            (up_fold, 0),
            (grad_shared, 0),
            (attn_weight_grads, 0),
            (rows_back, 0),
            (output_rows, 0),
            (mlp_fold, 0),
            (small_first, 0),
            (grads_out, 0),
            (attn_fold_dp, 0),
            (small_next, 0),
            (mlp_end, 0),
            (attn_fold_dp, 0),
            (small_next, 0),
            (mlp_spread_rest, 4),
            (small_next, 0),
            (attn_end, 4),
            (down_done, 0),
            (up_done, 100),
            (attn_done, 0),
        ):
            steps.cost = cost
            part()
        return (
            v.output,
            v.tokens_grad,
            v.small[0],
            v.small[1],
            v.qkv_out,
            v.out_out,
            v.small[2],
            v.up_out,
            v.down_out,
        )

    return local


def solution(mesh):
    rows = P(("dp", "tensor"), None)
    heads = P("tensor", None, None)
    return jax.shard_map(
        make_local(mesh.shape["dp"], mesh.shape["tensor"]),
        mesh=mesh,
        in_specs=(
            rows,
            rows,
            P(),
            P(),
            P(None, "tensor", None, None),
            heads,
            P(),
            P(None, "tensor"),
            P("tensor", None),
            rows,
        ),
        out_specs=(
            rows,
            rows,
            P(),
            P(),
            P(None, "tensor", None, None),
            heads,
            P(),
            P(None, "tensor"),
            P("tensor", None),
        ),
        check_vma=False,
    )
```
